32 devices in a mesh: page: 4 (over z), blk: 8 (over y, x, core).
Axes of the slice: x: 2, y: 2, z: 4, core: 2. Of those that a mesh axis runs over, the one named last changes fastest.
Arguments:
- queries: bfloat16 [64, 2, 32, 128], P(None, None, 'blk'), may hold values from -192 to 192
- prompt_kv: bfloat16 [64, 64, 32, 256], P('page', None, 'blk'), may hold values from -36 to 36
- tail_kv: bfloat16 [64, 256, 32, 256], P('page', None, 'blk'), may hold values from -36 to 36
- page_table: int32 [4, 16], replicated, may hold values from 0 to 63, as said below
- prompt_len: int32 [4], replicated, may hold values from 1 to 1024, 2560 in all
- tail_len: int32 [64], replicated, may hold values from 0 to 254, as said below
- sample_prompt: int32 [64], replicated, may hold values from 0 to 3, as said below
- stream_in: bfloat16 [64, 2, 7168], P(None, None, 'blk'), may hold values from -6 to 6
- w_out: bfloat16 [4096, 7168], P('blk'), may hold values from -0.09375 to 0.09375
- b_out: bfloat16 [7168], replicated, may hold values from -3 to 3
- ln_gain: bfloat16 [7168], P('page'), may hold values from 0.25 to 1.75
- ln_bias: bfloat16 [7168], P('page'), may hold values from -3 to 3
- w_up: bfloat16 [7168, 28672], P('page', 'blk'), may hold values from -0.0625 to 0.0625
- b_up: bfloat16 [28672], P('blk'), may hold values from -3 to 3
- w_down: bfloat16 [28672, 7168], P('blk', 'page'), may hold values from -0.046875 to 0.046875
- b_down: bfloat16 [7168], P(('page', 'blk')), may hold values from -3 to 3
- w_score: bfloat16 [7168], P(('page', 'blk')), may hold values from -0.0625 to 0.0625
Outputs:
- layer_output: bfloat16 [64, 2, 7168], P(None, None, ('page', 'blk'))
- sample_score: float32 [64, 2], replicated
The draws below stay inside these ranges and needn't reach their ends.
Inputs may be any that keep to these rules, and one draw needn't show every extreme that they name: `page_table`: every slot number appears exactly once in the table. `tail_len`: some sample reaches the largest value. `sample_prompt`: each prompt has exactly 16 samples.
All inputs are finite; a program needn't handle non-finite values.
Results may differ from the reference program's by a relative error of at most 0.03.
Values may be sent and summed in bfloat16 or wider, within the bound.
No kernel may reach another device: no remote copies, remote signals or barrier semaphores. Data moves between devices by JAX's collectives and lax.ppermute only.
A program may use at most 128 MiB of HBM per device.

```python
import math
import jax
import jax.numpy as jnp
import numpy as np
from jax import lax

D = 7168
FF = 28672
HEADS = 32
HD = 128
PAGE_LEN = 64
PROMPTS = 4
NEW = 2
TAIL_MAX = 256
SAMPLES = 64
ROWS = 128
SLOTS = 64
PAGES_MAX = 16
PROMPT_MAX = 1024
N_PAGE = 4


def paged_values(key, shape, offset_shape):
    count = shape[0]
    noise = jnp.clip(jax.random.normal(key, shape, jnp.float32), -4.0, 4.0)
    offset = jnp.clip(jax.random.normal(jax.random.fold_in(key, 3), offset_shape, jnp.float32), -3.0, 3.0)
    reach = 6.0
    common = jax.random.uniform(jax.random.fold_in(key, 7), (1, 1, HEADS, HD), jnp.float32, -1.0, 1.0)
    rise = jnp.exp(math.log(reach) * jnp.arange(count, dtype=jnp.float32) / (count - 1)).reshape(count, 1, 1, 1)
    mixed = noise + offset
    key_half = 0.7 * mixed[..., :HD]
    value_half = (0.35 * mixed[..., HD:] + common) * rise
    return jnp.concatenate([key_half, value_half], axis=-1).astype(jnp.bfloat16)


def draw_queries(key, part):
    shape = (SAMPLES, NEW, HEADS, HD)
    base = jnp.clip(jax.random.normal(key, shape, jnp.float32), -4.0, 4.0)
    return base.astype(jnp.bfloat16)


def draw_prompt_kv(key, part):
    return paged_values(key, (SLOTS, PAGE_LEN, HEADS, 2 * HD), (SLOTS, 1, HEADS, 2 * HD))


def draw_tail_kv(key, part):
    return paged_values(key, (SAMPLES, TAIL_MAX, HEADS, 2 * HD), (SAMPLES, 1, HEADS, 2 * HD))


def draw_page_table(key, part):
    return jax.random.permutation(key, SLOTS).astype(jnp.int32).reshape(PROMPTS, PAGES_MAX)


def draw_tail_len(key, part):
    values = jax.random.randint(key, (SAMPLES,), 0, TAIL_MAX - 1, dtype=jnp.int32)
    chosen = jax.random.randint(jax.random.fold_in(key, 1), (), 0, SAMPLES, dtype=jnp.int32)
    return jnp.where(jnp.arange(SAMPLES, dtype=jnp.int32) == chosen, TAIL_MAX - 2, values).astype(jnp.int32)


def draw_sample_prompt(key, part):
    return (jax.random.permutation(key, SAMPLES).astype(jnp.int32) % PROMPTS).astype(jnp.int32)


def block_levels(own_key, extent, shards, least, high):
    gain = 1.0
    for position, blocks in shards:
        heights = jax.random.uniform(jax.random.fold_in(jax.random.fold_in(own_key, 6), position), (blocks,), jnp.float32, least / len(shards), high / len(shards))
        gain = gain * jnp.repeat(jnp.exp(heights), extent[position] // blocks).reshape((-1,) + (1,) * (len(extent) - 1 - position))
    return gain


def profile(number_of, total, most, skew):
    loads = [(1 << 20) // math.isqrt(rank ** skew) + 1 for rank in range(2, number_of + 1)]
    surplus, holding = total - most - (number_of - 1), [1] * (number_of - 1)
    while surplus > 0:
        free = [i for i in range(number_of - 1) if holding[i] < most]
        whole, budget = sum([loads[i] for i in free]), surplus
        for i in free:
            more = min(most - holding[i], max(1, budget * loads[i] // whole), surplus)
            holding[i] = holding[i] + more
            surplus = surplus - more
    return np.array([most] + holding)


def ragged_sizes(stream_key, amount, total, most, skew):
    if amount == 2:
        one = jax.random.randint(stream_key, (), max(1, total - most), min(most, total - 1) + 1)
        return jnp.stack([one, total - one])
    tallies = jnp.asarray(profile(amount, total, most, skew), jnp.int32)
    twos = (amount - 1) // 2
    donor, taker = tallies[1:1 + 2 * twos:2], tallies[2:2 + 2 * twos:2]
    slack = jnp.minimum(donor - 1, most - taker)
    moved = jax.random.randint(jax.random.fold_in(stream_key, 1), (twos,), 0, 1 << 20) % (slack + 1)
    tallies = tallies.at[1:1 + 2 * twos:2].set(donor - moved).at[2:2 + 2 * twos:2].set(taker + moved)
    return tallies[jax.random.permutation(jax.random.fold_in(stream_key, 2), amount)]


def bell_draw(rng, extent, spread, most, cuts=(), held_as=jnp.bfloat16):
    values = jax.random.normal(rng, extent, jnp.float32) * spread
    if len(cuts) > 0:
        values = block_levels(rng, extent, cuts, -0.22, 0.18) * values
    return jnp.clip(values, min=-most, max=most).astype(held_as)


def setup_inputs(seed: int = 0) -> dict:
    key_of = jax.random.split(jax.random.key(seed), 18)
    queries = draw_queries(jax.random.fold_in(key_of[17], 71), 0)
    prompt_kv = draw_prompt_kv(jax.random.fold_in(key_of[17], 71), 0)
    tail_kv = draw_tail_kv(jax.random.fold_in(key_of[17], 71), 0)
    page_table = draw_page_table(jax.random.fold_in(key_of[17], 71), 0)
    prompt_len = ragged_sizes(key_of[4], PROMPTS, 5 * PROMPT_MAX * PROMPTS // 8, PROMPT_MAX, 2).astype(jnp.int32)
    tail_len = draw_tail_len(jax.random.fold_in(key_of[17], 71), 0)
    sample_prompt = draw_sample_prompt(jax.random.fold_in(key_of[17], 71), 0)
    stream_in = bell_draw(key_of[7], (SAMPLES, NEW, D), 1.0, 6.0, ((2, 8),))
    w_out = bell_draw(key_of[8], (HEADS * HD, D), (HEADS * HD) ** -0.5, 0.09375, ((0, 8),))
    b_out = bell_draw(key_of[9], (D,), 0.5, 3.0)
    ln_gain = jnp.clip(1.0 + 0.15 * jax.random.normal(key_of[10], (D,), jnp.float32), 0.25, 1.75).astype(jnp.bfloat16)
    ln_bias = bell_draw(key_of[11], (D,), 0.5, 3.0, ((0, 4),))
    w_up = bell_draw(key_of[12], (D, FF), D ** -0.5, 0.0625, ((0, 4), (1, 8)))
    b_up = bell_draw(key_of[13], (FF,), 0.5, 3.0, ((0, 8),))
    w_down = bell_draw(key_of[14], (FF, D), (FF // 2) ** -0.5, 0.046875, ((0, 8), (1, 4)))
    b_down = bell_draw(key_of[15], (D,), 0.5, 3.0, ((0, 32),))
    w_score = bell_draw(key_of[16], (D,), D ** -0.5, 0.0625, ((0, 32),))
    return dict(queries=queries, prompt_kv=prompt_kv, tail_kv=tail_kv, page_table=page_table, prompt_len=prompt_len, tail_len=tail_len, sample_prompt=sample_prompt, stream_in=stream_in, w_out=w_out, b_out=b_out, ln_gain=ln_gain, ln_bias=ln_bias, w_up=w_up, b_up=b_up, w_down=w_down, b_down=b_down, w_score=w_score)


NEGATIVE = -1e+30

def reference(queries, prompt_kv, tail_kv, page_table, prompt_len, tail_len, sample_prompt, stream_in, w_out, b_out, ln_gain, ln_bias, w_up, b_up, w_down, b_down, w_score):
    inv_sqrt = 1.0 / math.sqrt(HD)
    owner_index = jnp.zeros((SLOTS,), jnp.int32).at[page_table.reshape(-1)].set(jnp.arange(SLOTS, dtype=jnp.int32))
    slot_prompt = owner_index // PAGES_MAX
    slot_page = owner_index % PAGES_MAX
    key_pos = slot_page[:, None] * PAGE_LEN + jnp.arange(PAGE_LEN, dtype=jnp.int32)[None, :]
    key_live = (key_pos < prompt_len[slot_prompt][:, None]).reshape(-1)
    key_prompt = jnp.repeat(slot_prompt, PAGE_LEN)
    prompt_visible = (sample_prompt[:, None] == key_prompt[None, :]) & key_live[None, :]
    reach_pos = tail_len[:, None] + jnp.arange(NEW, dtype=jnp.int32)[None, :]
    tail_visible = jnp.arange(TAIL_MAX, dtype=jnp.int32)[None, None, :] <= reach_pos[:, :, None]
    by_head = (jnp.moveaxis(queries, 2, 0), jnp.moveaxis(prompt_kv.reshape(SLOTS * PAGE_LEN, HEADS, 2 * HD), 1, 0), jnp.moveaxis(tail_kv, 2, 0))

    def one_head(operands):
        query_f = operands[0].astype(jnp.float32)
        prompt_f = operands[1].astype(jnp.float32)
        tail_f = operands[2].astype(jnp.float32)
        prompt_scores = jnp.einsum('snd,kd->snk', query_f, prompt_f[:, :HD]) * inv_sqrt
        tail_scores = jnp.einsum('snd,std->snt', query_f, tail_f[:, :, :HD]) * inv_sqrt
        prompt_mask = prompt_visible[:, None, :]
        highest = jnp.maximum(lax.optimization_barrier(jnp.max(jnp.where(prompt_mask, prompt_scores, NEGATIVE), axis=-1)), lax.optimization_barrier(jnp.max(jnp.where(tail_visible, tail_scores, NEGATIVE), axis=-1)))
        prompt_w = jnp.where(prompt_mask, jnp.exp(prompt_scores - highest[..., None]), 0.0)
        tail_w = jnp.where(tail_visible, jnp.exp(tail_scores - highest[..., None]), 0.0)
        weight_sum = lax.optimization_barrier(jnp.sum(prompt_w, axis=-1)) + lax.optimization_barrier(jnp.sum(tail_w, axis=-1))
        prompt_r = lax.optimization_barrier(prompt_w.astype(jnp.bfloat16)).astype(jnp.float32)
        tail_r = lax.optimization_barrier(tail_w.astype(jnp.bfloat16)).astype(jnp.float32)
        weighted = jnp.einsum('snk,kd->snd', prompt_r, prompt_f[:, HD:]) + jnp.einsum('snt,std->snd', tail_r, tail_f[:, :, HD:])
        return (weighted / weight_sum[..., None]).astype(jnp.bfloat16)
    heads_out = lax.map(one_head, by_head)
    attention = jnp.moveaxis(heads_out, 0, 2).reshape(ROWS, HEADS * HD)
    rows_in = stream_in.reshape(ROWS, D).astype(jnp.float32)
    residual = (jnp.dot(attention, w_out, preferred_element_type=jnp.float32) + rows_in + b_out.astype(jnp.float32)).astype(jnp.bfloat16)
    residual_f = residual.astype(jnp.float32)
    row_mean = lax.optimization_barrier(jnp.mean(residual_f, axis=-1, keepdims=True))
    centred = residual_f - row_mean
    inverse_std = lax.rsqrt(lax.optimization_barrier(jnp.mean(centred * centred, axis=-1, keepdims=True)) + 1e-05)
    normed = (centred * inverse_std * ln_gain.astype(jnp.float32) + ln_bias.astype(jnp.float32)).astype(jnp.bfloat16)
    group_width = D // N_PAGE
    normed_groups = jnp.moveaxis(normed.reshape(ROWS, N_PAGE, group_width), 1, 0)
    up_groups = w_up.reshape(N_PAGE, group_width, FF)

    def group_product(operands):
        return lax.optimization_barrier(jnp.dot(operands[0], operands[1], preferred_element_type=jnp.float32).astype(jnp.bfloat16))
    hidden_sum = lax.optimization_barrier(jnp.sum(lax.map(group_product, (normed_groups, up_groups)).astype(jnp.float32), axis=0))
    hidden = jnp.maximum(hidden_sum + b_up.astype(jnp.float32), 0.0).astype(jnp.bfloat16)
    output = (jnp.dot(hidden, w_down, preferred_element_type=jnp.float32) + residual_f + b_down.astype(jnp.float32)).astype(jnp.bfloat16)
    row_score = lax.optimization_barrier(jnp.sum(output.astype(jnp.float32) * w_score.astype(jnp.float32), axis=-1))
    return (output.reshape(SAMPLES, NEW, D), row_score.reshape(SAMPLES, NEW))
```

```python
import math

import jax
import jax.numpy as jnp
from jax import lax
from jax.sharding import PartitionSpec as P

NEGATIVE = -1e30
EPS = 1e-05


def combined_all(value, axis, join):
    pieces = jax.tree.map(lambda part: lax.all_gather(part, axis), value)
    head = jax.tree.map(lambda part: part[0], pieces)
    tail = jax.tree.map(lambda part: part[1:], pieces)
    subtotal, _ = lax.scan(lambda subtotal, share: (join(subtotal, share), None), head, tail)
    return subtotal


def join_partials(earlier, later):
    highest = jnp.maximum(earlier[0], later[0])
    left_scale = jnp.exp(earlier[0] - highest)
    right_scale = jnp.exp(later[0] - highest)
    return (
        highest,
        earlier[1] * left_scale + later[1] * right_scale,
        earlier[2] * left_scale[..., None] + later[2] * right_scale[..., None],
    )


def softmax_part(scores, visible):
    masked = jnp.where(visible, scores, NEGATIVE)
    highest = jnp.max(masked, axis=-1)
    weights = jnp.where(visible, jnp.exp(scores - highest[..., None]), 0.0)
    return (highest, jnp.sum(weights, axis=-1), weights.astype(jnp.bfloat16))


def send_xor(value, axis, distance):
    size = lax.axis_size(axis)
    return lax.ppermute(value, axis, [(i, i ^ distance) for i in range(size)])


def pick(pieces, index):
    return lax.dynamic_index_in_dim(pieces, index, 0, keepdims=False)


def in_order(pieces, position):
    stacked = jnp.stack(pieces)
    out = jnp.zeros_like(stacked)
    for k, piece in enumerate(pieces):
        out = lax.dynamic_update_index_in_dim(out, piece, position ^ k, 0)
    return out


def gather_xor(value, axis, distances):
    return [value] + [send_xor(value, axis, k) for k in distances]


def pair_sum(pieces):
    return (pieces[0] + pieces[1]) + (pieces[2] + pieces[3])


def scatter_blk(pieces, blk_pos):
    pair = pieces.reshape((4, 2) + pieces.shape[1:])
    core, chip = blk_pos % 2, blk_pos // 2
    keep = lax.dynamic_index_in_dim(pair, core, 1, keepdims=False)
    give = lax.dynamic_index_in_dim(pair, 1 - core, 1, keepdims=False)
    got = send_xor(give.astype(jnp.bfloat16), "blk", 1)
    both = keep + got.astype(jnp.float32)
    rounded = both.astype(jnp.bfloat16)
    arrived = [send_xor(pick(rounded, chip ^ k), "blk", 2 * k) for k in (1, 2, 3)]
    total = pick(both, chip)
    for piece in arrived:
        total = total + piece.astype(jnp.float32)
    return total


def gather_blk(value, blk_pos):
    core, chip = blk_pos % 2, blk_pos // 2
    mine = in_order(gather_xor(value, "blk", (2, 4, 6)), chip)
    other = send_xor(mine, "blk", 1)
    both = in_order([mine, other], core)
    return jnp.moveaxis(both, 0, 1).reshape((8,) + value.shape)


def prompt_partial(queries, prompt_kv, page_table, prompt_len, sample_prompt):
    heads_dev, head_dim = queries.shape[2:]
    slots_dev, page_len = prompt_kv.shape[:2]
    prompts, pages_max = page_table.shape
    page_pos = lax.axis_index("page")
    inv_sqrt = 1.0 / math.sqrt(head_dim)
    entries = page_table.reshape(-1)
    slot_ids = page_pos * slots_dev + jnp.arange(slots_dev, dtype=jnp.int32)
    matched = (entries[:, None] == slot_ids[None, :]).astype(jnp.int32)
    owner_index = jnp.sum(matched * jnp.arange(entries.shape[0], dtype=jnp.int32)[:, None], axis=0)
    slot_prompt = owner_index // pages_max
    slot_page = owner_index % pages_max
    prompt_pick = (slot_prompt[:, None] == jnp.arange(prompts, dtype=jnp.int32)[None, :]).astype(
        jnp.int32
    )
    slot_limit = jnp.sum(prompt_pick * prompt_len[None, :], axis=1)
    key_pos = slot_page[:, None] * page_len + jnp.arange(page_len, dtype=jnp.int32)[None, :]
    key_live = (key_pos < slot_limit[:, None]).reshape(-1)
    key_prompt = jnp.repeat(slot_prompt, page_len)
    prompt_visible = ((sample_prompt[:, None] == key_prompt[None, :]) & key_live[None, :])[
        :, None, None, :
    ]
    cache_rows = prompt_kv.reshape(slots_dev * page_len, heads_dev, 2 * head_dim)
    prompt_scores = (
        jnp.einsum(
            "snhd,khd->snhk",
            queries,
            cache_rows[:, :, :head_dim],
            preferred_element_type=jnp.float32,
        )
        * inv_sqrt
    )
    high_p, sum_p, weights_p = softmax_part(prompt_scores, prompt_visible)
    mixed_p = jnp.einsum(
        "snhk,khd->snhd", weights_p, cache_rows[:, :, head_dim:], preferred_element_type=jnp.float32
    )
    return high_p, sum_p, mixed_p


def tail_partial(queries, tail_kv, tail_len):
    new_count, heads_dev, head_dim = queries.shape[1:]
    own_count, tail_max = (tail_kv.shape[0], tail_kv.shape[1])
    inv_sqrt = 1.0 / math.sqrt(head_dim)
    first_row = lax.axis_index("page") * own_count
    own_queries = lax.dynamic_slice_in_dim(queries, first_row, own_count, 0)
    own_lengths = lax.dynamic_slice_in_dim(tail_len, first_row, own_count, 0)
    tail_scores = (
        jnp.einsum(
            "snhd,sthd->snht",
            own_queries,
            tail_kv[..., :head_dim],
            preferred_element_type=jnp.float32,
        )
        * inv_sqrt
    )
    reach_pos = own_lengths[:, None] + jnp.arange(new_count, dtype=jnp.int32)[None, :]
    tail_visible = (
        jnp.arange(tail_max, dtype=jnp.int32)[None, None, None, :] <= reach_pos[:, :, None, None]
    )
    high_t, sum_t, weights_t = softmax_part(tail_scores, tail_visible)
    mixed_t = jnp.einsum(
        "snht,sthd->snhd", weights_t, tail_kv[..., head_dim:], preferred_element_type=jnp.float32
    )
    return high_t, sum_t, mixed_t


def body(
    queries,
    prompt_kv,
    tail_kv,
    page_table,
    prompt_len,
    tail_len,
    sample_prompt,
    stream_in,
    w_out,
    b_out,
    ln_gain,
    ln_bias,
    w_up,
    b_up,
    w_down,
    b_down,
    w_score,
):
    bf16, f32 = jnp.bfloat16, jnp.float32
    samples, new_count, heads_dev, head_dim = queries.shape
    own_count = tail_kv.shape[0]
    rows = samples * new_count
    own_rows = own_count * new_count
    group = ln_gain.shape[0]
    page_pos = lax.axis_index("page")
    blk_pos = lax.axis_index("blk")
    score_group = gather_blk(w_score, blk_pos).reshape(group)
    image = jnp.dot(w_down, score_group[:, None], preferred_element_type=f32)[:, 0]
    image = image + send_xor(image, "page", 1)
    image = image + send_xor(image, "page", 2)
    high_p, sum_p, mixed_p = prompt_partial(
        queries, prompt_kv, page_table, prompt_len, sample_prompt
    )
    lines = own_rows * heads_dev
    packed = jnp.concatenate(
        [
            mixed_p.reshape(4, lines, head_dim),
            high_p.reshape(4, lines // head_dim, head_dim),
            sum_p.reshape(4, lines // head_dim, head_dim),
        ],
        axis=1,
    )
    shares = [pick(packed, page_pos)] + [
        send_xor(pick(packed, page_pos ^ k), "page", k) for k in (1, 2, 3)
    ]
    merged = tail_partial(queries, tail_kv, tail_len)
    small = (own_count, new_count, heads_dev)
    for share in shares:
        merged = join_partials(
            merged,
            (
                share[lines : lines + lines // head_dim].reshape(small),
                share[lines + lines // head_dim :].reshape(small),
                share[:lines].reshape(small + (head_dim,)),
            ),
        )
    own_attention = (
        (merged[2] / merged[1][..., None]).astype(bf16).reshape(own_rows, heads_dev * head_dim)
    )
    attention = in_order(gather_xor(own_attention, "page", (1, 2, 3)), page_pos).reshape(
        rows, heads_dev * head_dim
    )
    first_col = page_pos * group
    contrib = jnp.dot(
        attention,
        lax.dynamic_slice_in_dim(w_out, first_col, group, 1),
        preferred_element_type=f32,
    )
    width = stream_in.shape[2]
    per_group = group // width
    own_stream = stream_in.reshape(rows, width).astype(f32)
    spread = jnp.concatenate(
        [
            jnp.where(blk_pos == page_pos * per_group + part, own_stream, 0.0)
            for part in range(per_group)
        ],
        axis=1,
    )
    contrib = contrib + spread
    own_sum = scatter_blk(contrib.reshape(8, rows // 8, group), blk_pos)
    own_bias = lax.dynamic_slice_in_dim(b_out, first_col, group, 0).astype(f32)
    residual = gather_blk((own_sum + own_bias).astype(bf16), blk_pos).reshape(rows, group)
    residual_f = residual.astype(f32)
    group_mean = jnp.mean(residual_f, axis=1, keepdims=True)
    centred = residual_f - group_mean
    group_square = jnp.sum(centred * centred, axis=1, keepdims=True)
    piece = b_down.shape[0]
    own_residual = lax.dynamic_slice_in_dim(residual_f, blk_pos * piece, piece, 1)
    own_base = own_residual + b_down.astype(f32)
    base_score = jnp.sum(own_base * w_score.astype(f32), axis=1, keepdims=True)
    gain = ln_gain.astype(f32)
    lhs = jnp.concatenate(
        [
            (centred * gain).astype(bf16),
            ln_gain[None],
            ln_bias[None],
            jnp.zeros((14, group), bf16),
        ],
        axis=0,
    )
    up_part = jnp.dot(lhs, w_up, preferred_element_type=f32).astype(bf16)
    units = w_up.shape[1] // 4
    parts = jnp.stack([up_part[:, j * units : (j + 1) * units] for j in range(4)])
    up_shares = [pick(parts, page_pos)] + [
        send_xor(pick(parts, page_pos ^ k), "page", k) for k in (1, 2, 3)
    ]
    stats = jnp.concatenate([group_mean, group_square, base_score], axis=1).T
    all_stats = gather_xor(stats, "page", (1, 2, 3))
    means = [s[0] for s in all_stats]
    row_mean = pair_sum(means) * 0.25
    spread_sq = sum(s[1] + group * (s[0] - row_mean) ** 2 for s in all_stats)
    inverse_std = lax.rsqrt(spread_sq / (4 * group) + EPS)
    base_total = pair_sum([s[2] for s in all_stats])
    total = jnp.zeros((rows, units), f32)
    shift = jnp.zeros((1, units), f32)
    for share, mean in zip(up_shares, means):
        share_f = share.astype(f32)
        total = total + share_f[:rows] + (mean - row_mean)[:, None] * share_f[rows : rows + 1]
        shift = shift + share_f[rows + 1 : rows + 2]
    own_up = lax.dynamic_slice_in_dim(b_up, page_pos * units, units, 0).astype(f32)
    own_hidden = jnp.maximum(total * inverse_std[:, None] + shift + own_up, 0.0).astype(bf16)
    hidden_parts = in_order(gather_xor(own_hidden, "page", (1, 2, 3)), page_pos)
    hidden = jnp.concatenate([hidden_parts[j] for j in range(4)], axis=1)
    projected = jnp.dot(hidden, w_down, preferred_element_type=f32)
    out_pieces = jnp.stack([projected[:, j * piece : (j + 1) * piece] for j in range(8)])
    score = jnp.sum(hidden.astype(f32) * image[None], axis=1) + base_total
    score = score.reshape(1, rows)
    score = score + send_xor(score, "blk", 1)
    output = (scatter_blk(out_pieces, blk_pos) + own_base).astype(bf16)
    score = pair_sum(gather_xor(score, "blk", (2, 4, 6)))
    return (output.reshape(samples, new_count, piece), score.reshape(samples, new_count))


def general_body(
    queries,
    prompt_kv,
    tail_kv,
    page_table,
    prompt_len,
    tail_len,
    sample_prompt,
    stream_in,
    w_out,
    b_out,
    ln_gain,
    ln_bias,
    w_up,
    b_up,
    w_down,
    b_down,
    w_score,
):
    samples, new_count, heads_dev, head_dim = queries.shape
    slots_dev, page_len = (prompt_kv.shape[0], prompt_kv.shape[1])
    own_count, tail_max = (tail_kv.shape[0], tail_kv.shape[1])
    prompts, pages_max = page_table.shape
    page_pos = lax.axis_index("page")
    blk_pos = lax.axis_index("blk")
    inv_sqrt = 1.0 / math.sqrt(head_dim)
    entries = page_table.reshape(-1)
    slot_ids = page_pos * slots_dev + jnp.arange(slots_dev, dtype=jnp.int32)
    matched = (entries[:, None] == slot_ids[None, :]).astype(jnp.int32)
    owner_index = jnp.sum(matched * jnp.arange(entries.shape[0], dtype=jnp.int32)[:, None], axis=0)
    slot_prompt = owner_index // pages_max
    slot_page = owner_index % pages_max
    prompt_pick = (slot_prompt[:, None] == jnp.arange(prompts, dtype=jnp.int32)[None, :]).astype(
        jnp.int32
    )
    slot_limit = jnp.sum(prompt_pick * prompt_len[None, :], axis=1)
    key_pos = slot_page[:, None] * page_len + jnp.arange(page_len, dtype=jnp.int32)[None, :]
    key_live = (key_pos < slot_limit[:, None]).reshape(-1)
    key_prompt = jnp.repeat(slot_prompt, page_len)
    prompt_visible = ((sample_prompt[:, None] == key_prompt[None, :]) & key_live[None, :])[
        :, None, None, :
    ]
    cache_rows = prompt_kv.reshape(slots_dev * page_len, heads_dev, 2 * head_dim)
    prompt_scores = (
        jnp.einsum(
            "snhd,khd->snhk",
            queries,
            cache_rows[:, :, :head_dim],
            preferred_element_type=jnp.float32,
        )
        * inv_sqrt
    )
    high_p, sum_p, weights_p = softmax_part(prompt_scores, prompt_visible)
    mixed_p = jnp.einsum(
        "snhk,khd->snhd", weights_p, cache_rows[:, :, head_dim:], preferred_element_type=jnp.float32
    )
    first_row = page_pos * own_count
    own_queries = lax.dynamic_slice_in_dim(queries, first_row, own_count, 0)
    own_lengths = lax.dynamic_slice_in_dim(tail_len, first_row, own_count, 0)
    tail_scores = (
        jnp.einsum(
            "snhd,sthd->snht",
            own_queries,
            tail_kv[..., :head_dim],
            preferred_element_type=jnp.float32,
        )
        * inv_sqrt
    )
    reach_pos = own_lengths[:, None] + jnp.arange(new_count, dtype=jnp.int32)[None, :]
    tail_visible = (
        jnp.arange(tail_max, dtype=jnp.int32)[None, None, None, :] <= reach_pos[:, :, None, None]
    )
    high_t, sum_t, weights_t = softmax_part(tail_scores, tail_visible)
    mixed_t = jnp.einsum(
        "snht,sthd->snhd", weights_t, tail_kv[..., head_dim:], preferred_element_type=jnp.float32
    )
    high_t = lax.dynamic_update_slice_in_dim(
        jnp.full(high_p.shape, NEGATIVE, jnp.float32), high_t, first_row, 0
    )
    sum_t = lax.dynamic_update_slice_in_dim(
        jnp.zeros(sum_p.shape, jnp.float32), sum_t, first_row, 0
    )
    mixed_t = lax.dynamic_update_slice_in_dim(
        jnp.zeros(mixed_p.shape, jnp.float32), mixed_t, first_row, 0
    )
    partial_value = join_partials((high_p, sum_p, mixed_p), (high_t, sum_t, mixed_t))
    merged = combined_all(partial_value, "page", join_partials)
    weight_sum, weighted = (merged[1], merged[2])
    attention = (
        (weighted / weight_sum[..., None])
        .astype(jnp.bfloat16)
        .reshape(samples * new_count, heads_dev * head_dim)
    )
    contrib = jnp.dot(attention, w_out, preferred_element_type=jnp.float32)
    slice_width = stream_in.shape[2]
    column = blk_pos * slice_width
    own_stream = stream_in.reshape(samples * new_count, slice_width).astype(jnp.float32)
    contrib = lax.dynamic_update_slice_in_dim(
        contrib, lax.dynamic_slice_in_dim(contrib, column, slice_width, 1) + own_stream, column, 1
    )
    summed = lax.psum(contrib, "blk")
    residual = (summed + b_out.astype(jnp.float32)).astype(jnp.bfloat16)
    residual_f = residual.astype(jnp.float32)
    row_mean = jnp.mean(residual_f, axis=-1, keepdims=True)
    centred = residual_f - row_mean
    inverse_std = lax.rsqrt(jnp.mean(centred * centred, axis=-1, keepdims=True) + 1e-05)
    feature_count = ln_gain.shape[0]
    first_col = page_pos * feature_count
    normed = (
        lax.dynamic_slice_in_dim(centred, first_col, feature_count, 1)
        * inverse_std
        * ln_gain.astype(jnp.float32)
        + ln_bias.astype(jnp.float32)
    ).astype(jnp.bfloat16)
    up_part = jnp.dot(normed, w_up, preferred_element_type=jnp.float32).astype(jnp.bfloat16)
    hidden_sum = lax.psum(up_part, "page").astype(jnp.float32)
    hidden = jnp.maximum(hidden_sum + b_up.astype(jnp.float32), 0.0).astype(jnp.bfloat16)
    projected = jnp.dot(hidden, w_down, preferred_element_type=jnp.float32)
    out_share = lax.psum_scatter(projected, "blk", scatter_dimension=1, tiled=True)
    piece_width = b_down.shape[0]
    out_column = first_col + blk_pos * piece_width
    output = (
        out_share
        + lax.dynamic_slice_in_dim(residual_f, out_column, piece_width, 1)
        + b_down.astype(jnp.float32)
    ).astype(jnp.bfloat16)
    score_part = jnp.sum(output.astype(jnp.float32) * w_score.astype(jnp.float32), axis=-1)
    row_score = lax.psum(score_part, ("page", "blk"))
    return (output.reshape(samples, new_count, piece_width), row_score.reshape(samples, new_count))


def solution(mesh):
    compute = body if (mesh.shape["page"], mesh.shape["blk"]) == (4, 8) else general_body

    placed = (
        P(None, None, "blk", None),
        P("page", None, "blk", None),
        P("page", None, "blk", None),
        P(),
        P(),
        P(),
        P(),
        P(None, None, "blk"),
        P("blk", None),
        P(),
        P("page"),
        P("page"),
        P("page", "blk"),
        P("blk"),
        P("blk", "page"),
        P(("page", "blk")),
        P(("page", "blk")),
    )
    return jax.shard_map(
        compute,
        mesh=mesh,
        in_specs=placed,
        out_specs=(P(None, None, ("page", "blk")), P()),
        check_vma=False,
    )
```

```python
import functools
import math

import jax
import jax.numpy as jnp
from jax import lax
from jax.experimental import pallas as pl
from jax.experimental.pallas import tpu as pltpu
from jax.sharding import PartitionSpec as P

NEGATIVE = -1e30
EPS = 1e-05
VMEM_LIMIT = 24 * 2**20
FREE = pl.CostEstimate(flops=0, bytes_accessed=0, transcendentals=0)


def combined_all(value, axis, join):
    pieces = jax.tree.map(lambda part: lax.all_gather(part, axis), value)
    head = jax.tree.map(lambda part: part[0], pieces)
    tail = jax.tree.map(lambda part: part[1:], pieces)
    subtotal, _ = lax.scan(lambda subtotal, share: (join(subtotal, share), None), head, tail)
    return subtotal


def join_partials(earlier, later):
    highest = jnp.maximum(earlier[0], later[0])
    left_scale = jnp.exp(earlier[0] - highest)
    right_scale = jnp.exp(later[0] - highest)
    return (
        highest,
        earlier[1] * left_scale + later[1] * right_scale,
        earlier[2] * left_scale[..., None] + later[2] * right_scale[..., None],
    )


def softmax_part(scores, visible):
    masked = jnp.where(visible, scores, NEGATIVE)
    highest = jnp.max(masked, axis=-1)
    weights = jnp.where(visible, jnp.exp(scores - highest[..., None]), 0.0)
    return (highest, jnp.sum(weights, axis=-1), weights.astype(jnp.bfloat16))


def send_xor(value, axis, distance):
    size = lax.axis_size(axis)
    return lax.ppermute(value, axis, [(i, i ^ distance) for i in range(size)])


def in_hbm(value):
    return pltpu.with_memory_space_constraint(value, pltpu.HBM)


def in_order(pieces, position):
    stacked = jnp.stack(pieces)
    out = jnp.zeros_like(stacked)
    for k, piece in enumerate(pieces):
        out = lax.dynamic_update_index_in_dim(out, piece, position ^ k, 0)
    return out


def gather_xor(value, axis, distances):
    return [value] + [send_xor(value, axis, k) for k in distances]


def pair_sum(pieces):
    return (pieces[0] + pieces[1]) + (pieces[2] + pieces[3])


def gather_blk(value, blk_pos):
    core, chip = blk_pos % 2, blk_pos // 2
    mine = in_order(gather_xor(value, "blk", (2, 4, 6)), chip)
    other = send_xor(mine, "blk", 1)
    both = in_order([mine, other], core)
    return jnp.moveaxis(both, 0, 1).reshape((8,) + value.shape)


def flat_rows(ref_value):
    shape = ref_value.shape
    return ref_value.reshape(math.prod(shape[:-1]), shape[-1])


def prompt_kernel(scale, table_hbm, len_hbm, prompt_hbm, q_hbm, kv_hbm, *refs):
    outs, scratch = refs[:4], refs[4:]
    table_ref, len_ref, prompt_ref, q_ref, kv_ref, where_ref, code_ref, rows_ref, sems = scratch
    copies = [
        pltpu.make_async_copy(source, target, sems.at[i])
        for i, (source, target) in enumerate(
            (
                (kv_hbm, kv_ref),
                (q_hbm, q_ref),
                (table_hbm, table_ref),
                (len_hbm, len_ref),
                (prompt_hbm, prompt_ref),
            )
        )
    ]
    for copy in copies:
        copy.start()
    prompts, pages_max = table_ref.shape
    slots, page_len, heads, _ = kv_ref.shape
    samples, new = q_ref.shape[:2]
    dim = q_ref.shape[3]
    lines = outs[0].shape[0] - 8
    bf16, f32 = jnp.bfloat16, jnp.float32
    page_pos = lax.axis_index("page")
    first = page_pos * slots
    for copy in copies[2:]:
        copy.wait()
    for p in range(prompts):
        for g in range(pages_max):
            slot = table_ref[p, g] - first
            here = jnp.logical_and(slot >= 0, slot < slots)
            where_ref[jnp.where(here, slot, slots)] = p * pages_max + g
    row8 = lax.broadcasted_iota(jnp.int32, (new * heads, dim), 0)
    lane8 = lax.broadcasted_iota(jnp.int32, (new * heads, dim), 1)
    target = lane8 - row8 % heads
    for s in range(samples):
        code_ref[pl.ds(s * new * heads, new * heads), :] = jnp.where(
            target == prompt_ref[s] * heads, 1.0, 0.0
        )
    per_slot = page_len * heads
    row = lax.broadcasted_iota(jnp.int32, (per_slot, dim), 0)
    lane = lax.broadcasted_iota(jnp.int32, (per_slot, dim), 1)
    lane_code = lane - row % heads
    penalties = []
    for j in range(slots):
        entry = where_ref[j]
        prompt = entry // pages_max
        left = (len_ref[prompt] - (entry % pages_max) * page_len) * heads
        own = jnp.logical_and(lane_code == prompt * heads, row < left)
        penalties.append(jnp.where(own, 0.0, NEGATIVE).astype(bf16))
    copies[1].wait()
    rows_ref[:, :dim] = flat_rows(q_ref[...])
    rows_ref[:, dim:] = code_ref[...].astype(bf16)
    copies[0].wait()
    cache = flat_rows(kv_ref[...])
    keys = jnp.concatenate([cache[:, :dim], jnp.concatenate(penalties, axis=0)], axis=1)
    values = cache[:, dim:]
    for k in (3, 2, 1, 0):
        start = pl.multiple_of((page_pos ^ k) * lines, lines)
        scores = lax.dot_general(
            rows_ref[pl.ds(start, lines), :],
            keys,
            (((1,), (1,)), ((), ())),
            preferred_element_type=f32,
        )
        best = jnp.max(scores, axis=1, keepdims=True)
        weights = jnp.exp2((scores - best) * scale)
        norm = jnp.sum(weights, axis=1, keepdims=True)
        outs[k][0:lines, :] = jnp.dot(weights.astype(bf16), values, preferred_element_type=f32)
        outs[k][lines : lines + 1, :] = jnp.broadcast_to(best, (lines, lines)).T[0:1]
        outs[k][lines + 1 : lines + 2, :] = jnp.broadcast_to(norm, (lines, lines)).T[0:1]


def prompt_partial(queries, prompt_kv, page_table, prompt_len, sample_prompt):
    samples, new, heads, dim = queries.shape
    slots = prompt_kv.shape[0]
    total = samples * new * heads
    lines = total // 4
    anywhere = pl.BlockSpec(memory_space=pl.ANY)
    vmem = pl.BlockSpec(memory_space=pltpu.VMEM)
    return pl.pallas_call(
        functools.partial(prompt_kernel, math.log2(math.e) / math.sqrt(dim)),
        in_specs=[anywhere] * 5,
        out_specs=[vmem] * 4,
        out_shape=[jax.ShapeDtypeStruct((lines + 8, dim), jnp.float32)] * 4,
        scratch_shapes=[
            pltpu.SMEM(page_table.shape, jnp.int32),
            pltpu.SMEM(prompt_len.shape, jnp.int32),
            pltpu.SMEM(sample_prompt.shape, jnp.int32),
            pltpu.VMEM(queries.shape, queries.dtype),
            pltpu.VMEM(prompt_kv.shape, prompt_kv.dtype),
            pltpu.SMEM((slots + 1,), jnp.int32),
            pltpu.VMEM((total, dim), jnp.float32),
            pltpu.VMEM((total, 2 * dim), jnp.bfloat16),
            pltpu.SemaphoreType.DMA((5,)),
        ],
        compiler_params=pltpu.CompilerParams(vmem_limit_bytes=VMEM_LIMIT),
        name="prompt_attention",
    )(*map(in_hbm, (page_table, prompt_len, sample_prompt, queries, prompt_kv)))


def tail_kernel(scale, len_ref, q_ref, kv_ref, out_ref, best_ref, norm_ref):
    per, length, heads, _ = kv_ref.shape
    new, dim = q_ref.shape[1], q_ref.shape[3]
    lines = new * heads
    bf16, f32 = jnp.bfloat16, jnp.float32
    step = pl.program_id(0)
    first = (lax.axis_index("page") * pl.num_programs(0) + step) * per
    row = lax.broadcasted_iota(jnp.int32, (lines, length * heads), 0)
    col = lax.broadcasted_iota(jnp.int32, (lines, length * heads), 1)
    same_head = row % heads == col % heads
    ahead = jnp.where(same_head, col // heads - row // heads, length + new)
    for i in range(per):
        cache = flat_rows(kv_ref[i])
        scores = lax.dot_general(
            flat_rows(q_ref[i]),
            cache[:, :dim],
            (((1,), (1,)), ((), ())),
            preferred_element_type=f32,
        )
        scores = jnp.where(ahead <= len_ref[first + i], scores, NEGATIVE)
        best = jnp.max(scores, axis=1, keepdims=True)
        weights = jnp.exp2((scores - best) * scale)
        norm = jnp.sum(weights, axis=1, keepdims=True)
        at = pl.ds(pl.multiple_of((step * per + i) * lines, lines), lines)
        out_ref[at, :] = jnp.dot(weights.astype(bf16), cache[:, dim:], preferred_element_type=f32)
        best_ref[at, :] = jnp.broadcast_to(best, (lines, dim))
        norm_ref[at, :] = jnp.broadcast_to(norm, (lines, dim))

    @pl.when(step == pl.num_programs(0) - 1)
    def _():
        total = out_ref.shape[0] - 8
        out_ref[total : total + 1, :] = best_ref[...].T[0:1]
        out_ref[total + 1 : total + 2, :] = norm_ref[...].T[0:1]


def tail_partial(queries, tail_kv, tail_len):
    _, new, heads, dim = queries.shape
    own, length = tail_kv.shape[:2]
    per = math.gcd(own, 4)
    steps = own // per
    lines = own * new * heads
    return pl.pallas_call(
        functools.partial(tail_kernel, math.log2(math.e) / math.sqrt(dim)),
        grid=(steps,),
        in_specs=[
            pl.BlockSpec(memory_space=pltpu.SMEM),
            pl.BlockSpec(
                (per, new, heads, dim), lambda i: (lax.axis_index("page") * steps + i, 0, 0, 0)
            ),
            pl.BlockSpec((per, length, heads, 2 * dim), lambda i: (i, 0, 0, 0)),
        ],
        out_specs=pl.BlockSpec((lines + 8, dim), lambda i: (0, 0)),
        out_shape=jax.ShapeDtypeStruct((lines + 8, dim), jnp.float32),
        scratch_shapes=[pltpu.VMEM((lines, dim), jnp.float32)] * 2,
        compiler_params=pltpu.CompilerParams(vmem_limit_bytes=VMEM_LIMIT),
        cost_estimate=FREE,
        name="tail_attention",
    )(*map(in_hbm, (tail_len, queries, tail_kv)))


def merge_kernel(scale, *refs):
    parts, out_ref, held_ref = refs[:-2], refs[-2], refs[-1]
    lines, dim = held_ref.shape
    heads = out_ref.shape[1] // dim
    bests = [part[lines : lines + 1, :] for part in parts]
    best = functools.reduce(jnp.maximum, bests)
    scales = [jnp.exp2((one - best) * scale) for one in bests]
    norm = sum(factor * part[lines + 1 : lines + 2, :] for factor, part in zip(scales, parts))
    total = jnp.zeros((lines, dim), jnp.float32)
    for factor, part in zip(scales, parts):
        share = jnp.broadcast_to(factor / norm, (lines, lines)).T
        total = total + share * part[0:lines, :]
    held_ref[...] = total
    for h in range(heads):
        out_ref[:, h * dim : (h + 1) * dim] = held_ref[
            pl.ds(h, lines // heads, stride=heads), :
        ].astype(out_ref.dtype)


def merge_partials(parts, heads):
    lines, dim = parts[0].shape[0] - 8, parts[0].shape[1]
    vmem = pl.BlockSpec(memory_space=pltpu.VMEM)
    return pl.pallas_call(
        functools.partial(merge_kernel, math.log2(math.e) / math.sqrt(dim)),
        in_specs=[vmem] * len(parts),
        out_specs=vmem,
        out_shape=jax.ShapeDtypeStruct((lines // heads, heads * dim), jnp.bfloat16),
        scratch_shapes=[pltpu.VMEM((lines, dim), jnp.float32)],
        compiler_params=pltpu.CompilerParams(vmem_limit_bytes=VMEM_LIMIT),
        name="merge_partials",
    )(*parts)


def project_kernel(per_group, *refs):
    blocks, (w_ref, stream_ref, keep_ref, give_ref, lhs_ref, sum_ref) = refs[:4], refs[4:]
    page_pos, blk_pos = lax.axis_index("page"), lax.axis_index("blk")
    height = blocks[0].shape[0]
    rows, group = lhs_ref.shape[0], w_ref.shape[1]
    width = stream_ref.shape[2]
    for k, block in enumerate(blocks):
        start = pl.multiple_of((page_pos ^ k) * height, height)
        lhs_ref[pl.ds(start, height), :] = block[...]
    product = jnp.dot(lhs_ref[...], w_ref[...], preferred_element_type=jnp.float32)
    sum_ref[...] = product.reshape(sum_ref.shape)
    for part in range(per_group):

        @pl.when(blk_pos == page_pos * per_group + part)
        def _(part=part):
            stream = flat_rows(stream_ref[...]).astype(jnp.float32)
            at = (slice(None), slice(None), slice(part * width, (part + 1) * width))
            sum_ref[at] = sum_ref[at] + stream.reshape(sum_ref.shape[:2] + (width,))

    core = blk_pos % 2
    for chip in range(4):
        keep_ref[chip] = sum_ref[2 * chip + core]
        give_ref[chip] = sum_ref[2 * chip + 1 - core].astype(give_ref.dtype)


def project(blocks, w_out, stream_in, group):
    height, depth = blocks[0].shape
    rows = 4 * height
    vmem = pl.BlockSpec(memory_space=pltpu.VMEM)
    part = (4, rows // 8, group)
    return pl.pallas_call(
        functools.partial(project_kernel, group // stream_in.shape[2]),
        grid=(1,),
        in_specs=[vmem] * 4
        + [pl.BlockSpec((depth, group), lambda i: (0, lax.axis_index("page"))), vmem],
        out_specs=[vmem] * 2,
        out_shape=[
            jax.ShapeDtypeStruct(part, jnp.float32),
            jax.ShapeDtypeStruct(part, jnp.bfloat16),
        ],
        scratch_shapes=[
            pltpu.VMEM((rows, depth), jnp.bfloat16),
            pltpu.VMEM((8, rows // 8, group), jnp.float32),
        ],
        compiler_params=pltpu.CompilerParams(vmem_limit_bytes=VMEM_LIMIT),
        name="project_attention",
    )(*blocks, in_hbm(w_out), stream_in)


def pair_kernel(keep_ref, got_ref, own_ref, *out_refs):
    chip = lax.axis_index("blk") // 2
    own_ref[...] = keep_ref[chip] + got_ref[chip].astype(jnp.float32)
    for k, out_ref in enumerate(out_refs, 1):
        total = keep_ref[chip ^ k] + got_ref[chip ^ k].astype(jnp.float32)
        out_ref[...] = total.astype(out_ref.dtype)


def pair_pieces(keep, got):
    vmem = pl.BlockSpec(memory_space=pltpu.VMEM)
    shape = keep.shape[1:]
    return pl.pallas_call(
        pair_kernel,
        in_specs=[vmem] * 2,
        out_specs=[vmem] * 4,
        out_shape=[jax.ShapeDtypeStruct(shape, jnp.float32)]
        + [jax.ShapeDtypeStruct(shape, jnp.bfloat16)] * 3,
        compiler_params=pltpu.CompilerParams(vmem_limit_bytes=VMEM_LIMIT),
        name="pair_pieces",
    )(keep, got)


def residual_kernel(own_ref, a_ref, b_ref, c_ref, bias_ref, out_ref):
    total = own_ref[...] + bias_ref[...].astype(jnp.float32)
    for ref in (a_ref, b_ref, c_ref):
        total = total + ref[...].astype(jnp.float32)
    out_ref[...] = total.astype(out_ref.dtype)


def residual_rows(own, arrived, b_out):
    vmem = pl.BlockSpec(memory_space=pltpu.VMEM)
    return pl.pallas_call(
        residual_kernel,
        grid=(1,),
        in_specs=[vmem] * 4
        + [pl.BlockSpec((1, own.shape[1]), lambda i: (0, lax.axis_index("page")))],
        out_specs=vmem,
        out_shape=jax.ShapeDtypeStruct(own.shape, jnp.bfloat16),
        compiler_params=pltpu.CompilerParams(vmem_limit_bytes=VMEM_LIMIT),
        name="residual_rows",
    )(own, *arrived, b_out.reshape(1, -1))


def split2(value):
    high = value.astype(jnp.bfloat16)
    return high, (value - high.astype(jnp.float32)).astype(jnp.bfloat16)


def whole2(high, low):
    return high.astype(jnp.float32) + low.astype(jnp.float32)


def start_copies(copies):
    for copy in copies:
        copy.start()
    return copies


def shard_copies(w_hbm, w_ref, sems, shards, axis):
    page_pos = lax.axis_index("page")
    units = w_ref.shape[1 + axis]
    copies = []
    for i, k in enumerate(shards):
        at = pl.ds(pl.multiple_of((page_pos ^ k) * units, 128), units)
        source = w_hbm.at[:, at] if axis else w_hbm.at[at, :]
        copies.append(pltpu.make_async_copy(source, w_ref.at[i], sems.at[i]))
    return start_copies(copies)


def up_first_kernel(*refs):
    blocks, refs = refs[:8], refs[8:]
    gain_ref, bias_ref, score_ref, down_ref, w_hbm = refs[:5]
    out_refs, refs = refs[5:8], refs[8:]
    lhs_ref, residual_ref, stats_ref, mean_ref, square_ref, base_ref, w_ref, sems = refs
    copies = shard_copies(w_hbm, w_ref, sems, (3, 2, 1), 1)
    blk_pos = lax.axis_index("blk")
    core, chip = blk_pos % 2, blk_pos // 2
    height, group = blocks[0].shape
    rows = 8 * height
    gain = gain_ref[...].astype(jnp.float32)
    fixed = jnp.sum(down_ref[...] * score_ref[...], axis=1, keepdims=True)
    for i, block in enumerate(blocks):
        from_core = core if i < 4 else 1 - core
        start = pl.multiple_of((2 * (chip ^ (i % 4)) + from_core) * height, height)
        at = pl.ds(start, height)
        residual = block[...].astype(jnp.float32)
        mean = jnp.sum(residual, axis=1, keepdims=True) * (1.0 / group)
        centred = residual - mean
        square = jnp.sum(centred * centred, axis=1, keepdims=True)
        base = jnp.sum(residual * score_ref[...], axis=1, keepdims=True) + fixed
        residual_ref[at, :] = block[...]
        lhs_ref[at, :] = (centred * gain).astype(lhs_ref.dtype)
        mean_ref[at, :] = jnp.broadcast_to(mean, (height, rows))
        square_ref[at, :] = jnp.broadcast_to(square, (height, rows))
        base_ref[at, :] = jnp.broadcast_to(base, (height, rows))
    row = lax.broadcasted_iota(jnp.int32, (lhs_ref.shape[0] - rows, group), 0)
    bias = bias_ref[...].astype(jnp.float32)
    lhs_ref[rows:, :] = jnp.where(
        row == 0, gain, jnp.where(row == 1, bias, 0.0)
    ).astype(lhs_ref.dtype)
    pieces = []
    for ref in (mean_ref, square_ref, base_ref):
        pieces += split2(ref[...].T[0:1])
    stats_ref[...] = jnp.concatenate(pieces, axis=0)
    for i, out_ref in enumerate(out_refs):
        copies[i].wait()
        up_product(lhs_ref, w_ref.at[i], stats_ref, out_ref, rows)


def up_product(lhs_ref, w_ref, stats_ref, out_ref, rows):
    product = jnp.dot(lhs_ref[...], w_ref[...], preferred_element_type=jnp.float32)
    below = product[rows : rows + 8]
    padded = jnp.concatenate(
        [
            jnp.zeros((2, rows), jnp.float32),
            stats_ref[...].astype(jnp.float32),
        ],
        axis=0,
    )
    row = lax.broadcasted_iota(jnp.int32, (8, rows), 0)
    first = jnp.where(row < 2, below[:, :rows], padded)
    out_ref[0:rows, :] = product[:rows].astype(out_ref.dtype)
    out_ref[rows : rows + 8, :] = jnp.concatenate([first, below[:, rows:]], axis=1).astype(
        out_ref.dtype
    )


def up_first(blocks, ln_gain, ln_bias, score_row, down_row, w_up):
    height, group = blocks[0].shape
    rows = 8 * height
    units = w_up.shape[1] // 4
    bf16, f32 = jnp.bfloat16, jnp.float32
    vmem = pl.BlockSpec(memory_space=pltpu.VMEM)
    return pl.pallas_call(
        up_first_kernel,
        in_specs=[vmem] * 12 + [pl.BlockSpec(memory_space=pl.ANY)],
        out_specs=[vmem] * 6,
        out_shape=[pltpu.VMEM((rows + 8, units), bf16)] * 3
        + [
            pltpu.VMEM((rows + 16, group), bf16),
            jax.ShapeDtypeStruct((rows, group), bf16),
            pltpu.VMEM((6, rows), bf16),
        ],
        scratch_shapes=[pltpu.VMEM((rows, rows), f32)] * 3
        + [pltpu.VMEM((3, group, units), bf16), pltpu.SemaphoreType.DMA((3,))],
        compiler_params=pltpu.CompilerParams(vmem_limit_bytes=VMEM_LIMIT),
        name="norm_and_up",
    )(
        *blocks,
        ln_gain.reshape(1, group),
        ln_bias.reshape(1, group),
        score_row,
        down_row,
        in_hbm(w_up),
    )


def up_second_kernel(lhs_ref, stats_ref, w_hbm, out_ref, w_ref, sems):
    copies = shard_copies(w_hbm, w_ref, sems, (0,), 1)
    copies[0].wait()
    up_product(lhs_ref, w_ref.at[0], stats_ref, out_ref, stats_ref.shape[1])


def up_second(lhs, stats, w_up):
    group = lhs.shape[1]
    units = w_up.shape[1] // 4
    bf16 = jnp.bfloat16
    vmem = pl.BlockSpec(memory_space=pltpu.VMEM)
    return pl.pallas_call(
        up_second_kernel,
        in_specs=[vmem] * 2 + [pl.BlockSpec(memory_space=pl.ANY)],
        out_specs=vmem,
        out_shape=pltpu.VMEM((stats.shape[1] + 8, units), bf16),
        scratch_shapes=[pltpu.VMEM((1, group, units), bf16), pltpu.SemaphoreType.DMA((1,))],
        compiler_params=pltpu.CompilerParams(vmem_limit_bytes=VMEM_LIMIT),
        cost_estimate=FREE,
        name="up_own",
    )(lhs, stats, in_hbm(w_up))


def image_kernel(score_ref, w_ref, out_ref):
    image = lax.dot_general(
        score_ref[...], w_ref[...], (((1,), (1,)), ((), ())), preferred_element_type=jnp.float32
    )
    step = pl.program_id(0)
    high, low = split2(image)
    out_ref[pl.ds(step, 1), :] = high[0:1].astype(jnp.float32)
    out_ref[pl.ds(step + pl.num_programs(0), 1), :] = low[0:1].astype(jnp.float32)


def image_of(score_group, w_down):
    depth, group = w_down.shape
    tile = depth // 4
    lhs = jnp.broadcast_to(score_group.reshape(1, group), (8, group))
    return pl.pallas_call(
        image_kernel,
        grid=(4,),
        in_specs=[
            pl.BlockSpec((8, group), lambda i: (0, 0)),
            pl.BlockSpec((tile, group), lambda i: (i, 0)),
        ],
        out_specs=pl.BlockSpec((8, tile), lambda i: (0, 0)),
        out_shape=jax.ShapeDtypeStruct((8, tile), jnp.float32),
        compiler_params=pltpu.CompilerParams(vmem_limit_bytes=VMEM_LIMIT),
        cost_estimate=FREE,
        name="score_image",
    )(lhs, in_hbm(w_down))


def hidden_kernel(group, a_ref, b_ref, c_ref, d_ref, bias_ref, image_ref, out_ref, base_ref):
    parts = (a_ref, b_ref, c_ref, d_ref)
    rows = a_ref.shape[0] - 8
    f32 = jnp.float32
    tails = [part[rows : rows + 8, :].astype(f32) for part in parts]
    stats = [
        [tail[2 + i : 3 + i, :rows] + tail[3 + i : 4 + i, :rows] for tail in tails]
        for i in (0, 2, 4)
    ]
    means, squares, bases = stats
    row_mean = pair_sum(means) * 0.25
    shifts = [mean - row_mean for mean in means]
    spread = sum(square + group * shift * shift for square, shift in zip(squares, shifts))
    inverse = lax.rsqrt(spread * (0.25 / group) + EPS)
    pad = jnp.zeros((rows - 6, rows), f32)
    columns = jnp.concatenate([inverse, *shifts, pair_sum(bases), pad], axis=0).T
    total = parts[0][0:rows, :].astype(f32) + columns[:, 1:2] * tails[0][0:1]
    for k in (1, 2, 3):
        total = total + parts[k][0:rows, :].astype(f32) + columns[:, 1 + k : 2 + k] * tails[k][0:1]
    offset = sum(tail[1:2] for tail in tails) + bias_ref[...].astype(f32)
    hidden = jnp.maximum(total * columns[:, 0:1] + offset, 0.0)
    out_ref[0:rows, :] = hidden.astype(out_ref.dtype)
    out_ref[rows : rows + 8, :] = image_ref[...].astype(out_ref.dtype)
    base_ref[...] = columns[:, 5:6]


def own_hidden_units(parts, b_up, image, group):
    vmem = pl.BlockSpec(memory_space=pltpu.VMEM)
    height, units = parts[0].shape
    return pl.pallas_call(
        functools.partial(hidden_kernel, group),
        grid=(1,),
        in_specs=[vmem] * 4
        + [pl.BlockSpec((1, units), lambda i: (0, lax.axis_index("page"))), vmem],
        out_specs=[vmem] * 2,
        out_shape=[
            jax.ShapeDtypeStruct((height, units), jnp.bfloat16),
            jax.ShapeDtypeStruct((height - 8, 1), jnp.float32),
        ],
        compiler_params=pltpu.CompilerParams(vmem_limit_bytes=VMEM_LIMIT),
        name="hidden_units",
    )(*parts, b_up.reshape(1, -1), image)


def down_first_kernel(hidden_ref, w_hbm, sum_ref, held_ref, w_ref, sems, held_sems):
    rows = sum_ref.shape[0]
    copies = shard_copies(w_hbm, w_ref, sems, (0,), 0)
    held = shard_copies(w_hbm, held_ref, held_sems, (1, 2, 3), 0)
    copies[0].wait()
    sum_ref[...] = jnp.dot(
        hidden_ref[0:rows, :], w_ref[0], preferred_element_type=jnp.float32
    )
    for copy in held:
        copy.wait()


def down_first(hidden, w_down):
    rows, units = hidden.shape[0] - 8, hidden.shape[1]
    group = w_down.shape[1]
    vmem = pl.BlockSpec(memory_space=pltpu.VMEM)
    return pl.pallas_call(
        down_first_kernel,
        in_specs=[vmem, pl.BlockSpec(memory_space=pl.ANY)],
        out_specs=[vmem] * 2,
        out_shape=[
            pltpu.VMEM((rows, group), jnp.float32),
            pltpu.VMEM((3, units, group), jnp.bfloat16),
        ],
        scratch_shapes=[
            pltpu.VMEM((1, units, group), jnp.bfloat16),
            pltpu.SemaphoreType.DMA((1,)),
            pltpu.SemaphoreType.DMA((3,)),
        ],
        compiler_params=pltpu.CompilerParams(vmem_limit_bytes=VMEM_LIMIT),
        cost_estimate=FREE,
        name="down_own",
    )(hidden, in_hbm(w_down))


def down_rest_kernel(base_ref, sum_ref, held_ref, *refs):
    hiddens, (keep_ref, give_ref, score_ref, image_ref) = refs[:4], refs[4:]
    rows = sum_ref.shape[0]
    f32 = jnp.float32
    page_pos = lax.axis_index("page")
    core = lax.axis_index("blk") % 2
    piece = keep_ref.shape[2]
    product = sum_ref[...]
    for k in (1, 2, 3):
        product = product + jnp.dot(
            hiddens[k][0:rows, :], held_ref[k - 1], preferred_element_type=f32
        )
    tails = [ref[rows : rows + 8, :].astype(f32) for ref in hiddens]
    image_ref[...] = pair_sum([tail[0:4] + tail[4:8] for tail in tails])
    score = base_ref[...]
    by_owner = []
    for k, ref in enumerate(hiddens):
        image = image_ref[pl.ds(page_pos ^ k, 1), :]
        by_owner.append(jnp.sum(ref[0:rows, :].astype(f32) * image, axis=1, keepdims=True))
    score = score + pair_sum(by_owner)
    score_ref[...] = score
    pieces = split3(score)
    for chip in range(4):
        pair = [product[:, (2 * chip + c) * piece : (2 * chip + c + 1) * piece] for c in range(2)]
        keep_ref[chip] = jnp.where(core == 0, pair[0], pair[1])
        give_ref[chip, :, :piece] = jnp.where(core == 0, pair[1], pair[0]).astype(give_ref.dtype)
        give_ref[chip, :, piece:] = pieces


def down_rest(base, summed, held, hiddens):
    rows, group = summed.shape
    units = hiddens[0].shape[1]
    vmem = pl.BlockSpec(memory_space=pltpu.VMEM)
    return pl.pallas_call(
        down_rest_kernel,
        in_specs=[vmem] * 7,
        out_specs=[vmem] * 3,
        out_shape=[
            pltpu.VMEM((4, rows, group // 8), jnp.float32),
            jax.ShapeDtypeStruct((4, rows, group // 8 + 3), jnp.bfloat16),
            pltpu.VMEM((rows, 1), jnp.float32),
        ],
        scratch_shapes=[pltpu.VMEM((4, units), jnp.float32)],
        compiler_params=pltpu.CompilerParams(vmem_limit_bytes=VMEM_LIMIT),
        name="down_rest",
    )(base, summed, held, *hiddens)


def split3(value):
    high = value.astype(jnp.bfloat16)
    left = value - high.astype(jnp.float32)
    middle = left.astype(jnp.bfloat16)
    low = (left - middle.astype(jnp.float32)).astype(jnp.bfloat16)
    return jnp.concatenate([high, middle, low], axis=1)


def whole3(pieces):
    return jnp.sum(pieces.astype(jnp.float32), axis=1, keepdims=True)


def pair_score_kernel(keep_ref, score_ref, got_ref, own_ref, both_ref, *out_refs):
    chip = lax.axis_index("blk") // 2
    piece = keep_ref.shape[2]
    score = whole3(split3(score_ref[...])) + whole3(got_ref[0, :, piece:])
    both_ref[...] = score
    pieces = split3(score)
    own_ref[...] = keep_ref[chip] + got_ref[chip, :, :piece].astype(jnp.float32)
    for k, out_ref in enumerate(out_refs, 1):
        total = keep_ref[chip ^ k] + got_ref[chip ^ k, :, :piece].astype(jnp.float32)
        out_ref[:, :piece] = total.astype(out_ref.dtype)
        out_ref[:, piece:] = pieces


def pair_scores(keep, score, got):
    vmem = pl.BlockSpec(memory_space=pltpu.VMEM)
    _, rows, piece = keep.shape
    return pl.pallas_call(
        pair_score_kernel,
        in_specs=[vmem] * 3,
        out_specs=[vmem] * 5,
        out_shape=[
            jax.ShapeDtypeStruct((rows, piece), jnp.float32),
            jax.ShapeDtypeStruct((rows, 1), jnp.float32),
        ]
        + [jax.ShapeDtypeStruct((rows, piece + 3), jnp.bfloat16)] * 3,
        compiler_params=pltpu.CompilerParams(vmem_limit_bytes=VMEM_LIMIT),
        name="pair_scores",
    )(keep, score, got)


def finish_kernel(own_ref, base_ref, score_ref, a_ref, b_ref, c_ref, out_ref, total_ref, held_ref):
    piece = own_ref.shape[1]
    total = own_ref[...] + base_ref[...]
    for ref in (a_ref, b_ref, c_ref):
        total = total + ref[:, :piece].astype(jnp.float32)
    out_ref[...] = total.astype(out_ref.dtype).reshape(out_ref.shape)
    scores = [whole3(ref[:, piece:]) for ref in (a_ref, b_ref, c_ref)]
    own_score = whole3(split3(score_ref[...]))
    score = (own_score + scores[0]) + (scores[1] + scores[2])
    new, samples = total_ref.shape
    held_ref[...] = jnp.broadcast_to(score, held_ref.shape)
    for n in range(new):
        total_ref[n : n + 1, :] = held_ref[pl.ds(n, samples, stride=new), :].T[0:1]


def finish(own, base, score, arrived, samples):
    vmem = pl.BlockSpec(memory_space=pltpu.VMEM)
    rows, piece = own.shape
    return pl.pallas_call(
        finish_kernel,
        in_specs=[vmem] * 6,
        out_specs=[vmem] * 2,
        out_shape=[
            jax.ShapeDtypeStruct((samples, rows // samples, piece), jnp.bfloat16),
            jax.ShapeDtypeStruct((rows // samples, samples), jnp.float32),
        ],
        scratch_shapes=[pltpu.VMEM((rows, 128), jnp.float32)],
        compiler_params=pltpu.CompilerParams(vmem_limit_bytes=VMEM_LIMIT),
        name="finish",
    )(own, base, score, *arrived)


def body(
    queries,
    prompt_kv,
    tail_kv,
    page_table,
    prompt_len,
    tail_len,
    sample_prompt,
    stream_in,
    w_out,
    b_out,
    ln_gain,
    ln_bias,
    w_up,
    b_up,
    w_down,
    b_down,
    w_score,
):
    bf16, f32 = jnp.bfloat16, jnp.float32
    samples, new_count, heads_dev, head_dim = queries.shape
    group = ln_gain.shape[0]
    blk_pos = lax.axis_index("blk")
    piece = b_down.shape[0]
    packed = prompt_partial(queries, prompt_kv, page_table, prompt_len, sample_prompt)
    shares = [packed[0]] + [send_xor(packed[k], "page", k) for k in (1, 2, 3)]
    tail = tail_partial(queries, tail_kv, tail_len)
    own_attention = merge_partials(shares + [tail], heads_dev)
    attention = gather_xor(own_attention, "page", (1, 2, 3))
    w_score_late, own_attention = lax.optimization_barrier((w_score, own_attention))
    score_group = gather_blk(w_score_late, blk_pos).reshape(group)
    keep, give = project(attention, w_out, stream_in, group)
    own, *pieces = pair_pieces(keep, send_xor(give, "blk", 1))
    arrived = [send_xor(rounded, "blk", 2 * k) for k, rounded in enumerate(pieces, 1)]
    same_core = gather_xor(residual_rows(own, arrived, b_out), "blk", (2, 4, 6))
    blocks = same_core + [send_xor(block, "blk", 1) for block in same_core]
    score_row, down_row = [
        lax.dynamic_update_slice_in_dim(
            jnp.zeros((group,), f32), vector.astype(f32), blk_pos * piece, 0
        ).reshape(1, group)
        for vector in (w_score, b_down)
    ]
    part3, part2, part1, lhs, residual, stats = up_first(
        blocks, ln_gain, ln_bias, score_row, down_row, w_up
    )
    part0 = up_second(lhs, stats, w_up)
    image = image_of(score_group, w_down)
    parts = [part0] + [
        send_xor(part, "page", k) for k, part in ((1, part1), (2, part2), (3, part3))
    ]
    own_hidden, base_score = own_hidden_units(parts, b_up, image, group)
    hiddens = gather_xor(own_hidden, "page", (1, 2, 3))
    summed, held = down_first(own_hidden, w_down)
    keep, give, score = down_rest(base_score, summed, held, hiddens)
    own_base = lax.dynamic_slice_in_dim(residual, blk_pos * piece, piece, 1).astype(
        f32
    ) + b_down.astype(f32)
    own, score, *pieces = pair_scores(keep, score, send_xor(give, "blk", 1))
    arrived = [send_xor(piece_k, "blk", 2 * k) for k, piece_k in enumerate(pieces, 1)]
    output, score = finish(own, own_base, score, arrived, samples)
    return (output, score.T)


def general_body(
    queries,
    prompt_kv,
    tail_kv,
    page_table,
    prompt_len,
    tail_len,
    sample_prompt,
    stream_in,
    w_out,
    b_out,
    ln_gain,
    ln_bias,
    w_up,
    b_up,
    w_down,
    b_down,
    w_score,
):
    samples, new_count, heads_dev, head_dim = queries.shape
    slots_dev, page_len = (prompt_kv.shape[0], prompt_kv.shape[1])
    own_count, tail_max = (tail_kv.shape[0], tail_kv.shape[1])
    prompts, pages_max = page_table.shape
    page_pos = lax.axis_index("page")
    blk_pos = lax.axis_index("blk")
    inv_sqrt = 1.0 / math.sqrt(head_dim)
    entries = page_table.reshape(-1)
    slot_ids = page_pos * slots_dev + jnp.arange(slots_dev, dtype=jnp.int32)
    matched = (entries[:, None] == slot_ids[None, :]).astype(jnp.int32)
    owner_index = jnp.sum(matched * jnp.arange(entries.shape[0], dtype=jnp.int32)[:, None], axis=0)
    slot_prompt = owner_index // pages_max
    slot_page = owner_index % pages_max
    prompt_pick = (slot_prompt[:, None] == jnp.arange(prompts, dtype=jnp.int32)[None, :]).astype(
        jnp.int32
    )
    slot_limit = jnp.sum(prompt_pick * prompt_len[None, :], axis=1)
    key_pos = slot_page[:, None] * page_len + jnp.arange(page_len, dtype=jnp.int32)[None, :]
    key_live = (key_pos < slot_limit[:, None]).reshape(-1)
    key_prompt = jnp.repeat(slot_prompt, page_len)
    prompt_visible = ((sample_prompt[:, None] == key_prompt[None, :]) & key_live[None, :])[
        :, None, None, :
    ]
    cache_rows = prompt_kv.reshape(slots_dev * page_len, heads_dev, 2 * head_dim)
    prompt_scores = (
        jnp.einsum(
            "snhd,khd->snhk",
            queries,
            cache_rows[:, :, :head_dim],
            preferred_element_type=jnp.float32,
        )
        * inv_sqrt
    )
    high_p, sum_p, weights_p = softmax_part(prompt_scores, prompt_visible)
    mixed_p = jnp.einsum(
        "snhk,khd->snhd", weights_p, cache_rows[:, :, head_dim:], preferred_element_type=jnp.float32
    )
    first_row = page_pos * own_count
    own_queries = lax.dynamic_slice_in_dim(queries, first_row, own_count, 0)
    own_lengths = lax.dynamic_slice_in_dim(tail_len, first_row, own_count, 0)
    tail_scores = (
        jnp.einsum(
            "snhd,sthd->snht",
            own_queries,
            tail_kv[..., :head_dim],
            preferred_element_type=jnp.float32,
        )
        * inv_sqrt
    )
    reach_pos = own_lengths[:, None] + jnp.arange(new_count, dtype=jnp.int32)[None, :]
    tail_visible = (
        jnp.arange(tail_max, dtype=jnp.int32)[None, None, None, :] <= reach_pos[:, :, None, None]
    )
    high_t, sum_t, weights_t = softmax_part(tail_scores, tail_visible)
    mixed_t = jnp.einsum(
        "snht,sthd->snhd", weights_t, tail_kv[..., head_dim:], preferred_element_type=jnp.float32
    )
    high_t = lax.dynamic_update_slice_in_dim(
        jnp.full(high_p.shape, NEGATIVE, jnp.float32), high_t, first_row, 0
    )
    sum_t = lax.dynamic_update_slice_in_dim(
        jnp.zeros(sum_p.shape, jnp.float32), sum_t, first_row, 0
    )
    mixed_t = lax.dynamic_update_slice_in_dim(
        jnp.zeros(mixed_p.shape, jnp.float32), mixed_t, first_row, 0
    )
    partial_value = join_partials((high_p, sum_p, mixed_p), (high_t, sum_t, mixed_t))
    merged = combined_all(partial_value, "page", join_partials)
    weight_sum, weighted = (merged[1], merged[2])
    attention = (
        (weighted / weight_sum[..., None])
        .astype(jnp.bfloat16)
        .reshape(samples * new_count, heads_dev * head_dim)
    )
    contrib = jnp.dot(attention, w_out, preferred_element_type=jnp.float32)
    slice_width = stream_in.shape[2]
    column = blk_pos * slice_width
    own_stream = stream_in.reshape(samples * new_count, slice_width).astype(jnp.float32)
    contrib = lax.dynamic_update_slice_in_dim(
        contrib, lax.dynamic_slice_in_dim(contrib, column, slice_width, 1) + own_stream, column, 1
    )
    summed = lax.psum(contrib, "blk")
    residual = (summed + b_out.astype(jnp.float32)).astype(jnp.bfloat16)
    residual_f = residual.astype(jnp.float32)
    row_mean = jnp.mean(residual_f, axis=-1, keepdims=True)
    centred = residual_f - row_mean
    inverse_std = lax.rsqrt(jnp.mean(centred * centred, axis=-1, keepdims=True) + 1e-05)
    feature_count = ln_gain.shape[0]
    first_col = page_pos * feature_count
    normed = (
        lax.dynamic_slice_in_dim(centred, first_col, feature_count, 1)
        * inverse_std
        * ln_gain.astype(jnp.float32)
        + ln_bias.astype(jnp.float32)
    ).astype(jnp.bfloat16)
    up_part = jnp.dot(normed, w_up, preferred_element_type=jnp.float32).astype(jnp.bfloat16)
    hidden_sum = lax.psum(up_part, "page").astype(jnp.float32)
    hidden = jnp.maximum(hidden_sum + b_up.astype(jnp.float32), 0.0).astype(jnp.bfloat16)
    projected = jnp.dot(hidden, w_down, preferred_element_type=jnp.float32)
    out_share = lax.psum_scatter(projected, "blk", scatter_dimension=1, tiled=True)
    piece_width = b_down.shape[0]
    out_column = first_col + blk_pos * piece_width
    output = (
        out_share
        + lax.dynamic_slice_in_dim(residual_f, out_column, piece_width, 1)
        + b_down.astype(jnp.float32)
    ).astype(jnp.bfloat16)
    score_part = jnp.sum(output.astype(jnp.float32) * w_score.astype(jnp.float32), axis=-1)
    row_score = lax.psum(score_part, ("page", "blk"))
    return (output.reshape(samples, new_count, piece_width), row_score.reshape(samples, new_count))


def solution(mesh):
    compute = body if (mesh.shape["page"], mesh.shape["blk"]) == (4, 8) else general_body

    placed = (
        P(None, None, "blk", None),
        P("page", None, "blk", None),
        P("page", None, "blk", None),
        P(),
        P(),
        P(),
        P(),
        P(None, None, "blk"),
        P("blk", None),
        P(),
        P("page"),
        P("page"),
        P("page", "blk"),
        P("blk"),
        P("blk", "page"),
        P(("page", "blk")),
        P(("page", "blk")),
    )
    return jax.shard_map(
        compute,
        mesh=mesh,
        in_specs=placed,
        out_specs=(P(None, None, ("page", "blk")), P()),
        check_vma=False,
    )
```

```python
import functools
import math

import jax
import jax.numpy as jnp
from jax import lax
from jax.experimental import pallas as pl
from jax.experimental.pallas import tpu as pltpu
from jax.sharding import PartitionSpec as P

NEGATIVE = -1e30
EPS = 1e-05
VMEM_LIMIT = 24 * 2**20
TOP = 64
FREE = pl.CostEstimate(flops=0, bytes_accessed=0, transcendentals=0)


def combined_all(value, axis, join):
    pieces = jax.tree.map(lambda part: lax.all_gather(part, axis), value)
    head = jax.tree.map(lambda part: part[0], pieces)
    tail = jax.tree.map(lambda part: part[1:], pieces)
    subtotal, _ = lax.scan(lambda subtotal, share: (join(subtotal, share), None), head, tail)
    return subtotal


def join_partials(earlier, later):
    highest = jnp.maximum(earlier[0], later[0])
    left_scale = jnp.exp(earlier[0] - highest)
    right_scale = jnp.exp(later[0] - highest)
    return (
        highest,
        earlier[1] * left_scale + later[1] * right_scale,
        earlier[2] * left_scale[..., None] + later[2] * right_scale[..., None],
    )


def softmax_part(scores, visible):
    masked = jnp.where(visible, scores, NEGATIVE)
    highest = jnp.max(masked, axis=-1)
    weights = jnp.where(visible, jnp.exp(scores - highest[..., None]), 0.0)
    return (highest, jnp.sum(weights, axis=-1), weights.astype(jnp.bfloat16))


def send_xor(value, axis, distance):
    size = lax.axis_size(axis)
    return lax.ppermute(value, axis, [(i, i ^ distance) for i in range(size)])


def in_hbm(value):
    return pltpu.with_memory_space_constraint(value, pltpu.HBM)


def gather_xor(value, axis, distances):
    return [value] + [send_xor(value, axis, k) for k in distances]


def pair_sum(pieces):
    return (pieces[0] + pieces[1]) + (pieces[2] + pieces[3])


def start_copies(copies):
    for copy in copies:
        copy.start()
    return copies


def flat_rows(ref_value):
    shape = ref_value.shape
    return ref_value.reshape(math.prod(shape[:-1]), shape[-1])


def prompt_kernel(scale, table_hbm, len_hbm, prompt_hbm, q_hbm, kv_hbm, *refs):
    outs, refs = refs[:4], refs[4:]
    table_ref, len_ref, prompt_ref, q_ref, kv_ref, where_ref, count_ref, place_ref = refs[:8]
    query_ref, rows_ref, score_ref, best_ref, norm_ref, mixed_ref, back_ref, sems = refs[8:]
    copies = start_copies(
        [
            pltpu.make_async_copy(source, target, sems.at[i])
            for i, (source, target) in enumerate(
                (
                    (table_hbm, table_ref),
                    (len_hbm, len_ref),
                    (prompt_hbm, prompt_ref),
                    (q_hbm, q_ref),
                    (kv_hbm, kv_ref),
                )
            )
        ]
    )
    prompts, pages_max = table_ref.shape
    slots, page_len, heads, _ = kv_ref.shape
    samples, new = q_ref.shape[:2]
    dim = q_ref.shape[3]
    lines = outs[0].shape[0] - 8
    small = new * heads
    block = samples // prompts * small
    bf16, f32 = jnp.bfloat16, jnp.float32
    page_pos = lax.axis_index("page")
    first = page_pos * slots
    best_ref[...] = jnp.full(best_ref.shape, NEGATIVE, f32)
    norm_ref[...] = jnp.zeros(norm_ref.shape, f32)
    mixed_ref[...] = jnp.zeros(mixed_ref.shape, f32)
    for copy in copies[:3]:
        copy.wait()
    for p in range(prompts):
        count_ref[p] = p * (samples // prompts)
        for g in range(pages_max):
            slot = table_ref[p, g] - first
            here = jnp.logical_and(slot >= 0, slot < slots)
            where_ref[jnp.where(here, slot, slots)] = p * pages_max + g
    copies[3].wait()
    query_ref[...] = flat_rows(q_ref[...]).astype(f32)
    for s in range(samples):
        prompt = prompt_ref[s]
        place = count_ref[prompt]
        count_ref[prompt] = place + 1
        place_ref[s] = place
        to = pl.ds(pl.multiple_of(place * small, small), small)
        back_ref[to, :] = query_ref[s * small : (s + 1) * small, :]
    rows_ref[...] = back_ref[...].astype(bf16)
    width = page_len * heads
    row = lax.broadcasted_iota(jnp.int32, (block, width), 0)
    col = lax.broadcasted_iota(jnp.int32, (block, width), 1)
    position = jnp.where(row % heads == col % heads, col, page_len * heads * pages_max)
    copies[4].wait()
    cache = flat_rows(kv_ref[...])
    at = []
    for j in range(slots):
        entry = where_ref[j]
        prompt = entry // pages_max
        left = (len_ref[prompt] - (entry % pages_max) * page_len) * heads
        at.append(pl.ds(pl.multiple_of(prompt * block, block), block))
        scores = lax.dot_general(
            rows_ref[at[j], :],
            cache[j * width : (j + 1) * width, :dim],
            (((1,), (1,)), ((), ())),
            preferred_element_type=f32,
        )
        scores = jnp.where(position < jnp.minimum(left, width), scores, NEGATIVE)
        score_ref[j] = scores
        best = jnp.max(scores, axis=1, keepdims=True)
        best_ref[at[j], :] = jnp.maximum(best_ref[at[j], :], best)
    for j in range(slots):
        best = best_ref[at[j], :]
        best = jnp.concatenate([best] * (width // dim), axis=1)
        weights = jnp.exp2((score_ref[j] - best) * scale)
        norm_ref[at[j], :] += jnp.sum(weights, axis=1, keepdims=True)
        mixed_ref[at[j], :] += jnp.dot(
            weights.astype(bf16),
            cache[j * width : (j + 1) * width, dim:],
            preferred_element_type=f32,
        )
    for k, out_ref in enumerate(outs):
        for i in range(lines // small):
            place = place_ref[(page_pos ^ k) * (lines // small) + i]
            source = pl.ds(pl.multiple_of(place * small, small), small)
            to = slice(i * small, (i + 1) * small)
            out_ref[to, :] = mixed_ref[source, :]
            back_ref[k * lines + i * small : k * lines + (i + 1) * small, :] = best_ref[source, :]
            query_ref[k * lines + i * small : k * lines + (i + 1) * small, :] = norm_ref[source, :]
        out_ref[lines : lines + 1, :] = back_ref[k * lines : (k + 1) * lines, :].T[0:1]
        out_ref[lines + 1 : lines + 2, :] = query_ref[k * lines : (k + 1) * lines, :].T[0:1]


def prompt_partial(queries, prompt_kv, page_table, prompt_len, sample_prompt):
    samples, new, heads, dim = queries.shape
    slots, page_len = prompt_kv.shape[:2]
    total = samples * new * heads
    block = total // page_table.shape[0]
    lines = total // 4
    anywhere = pl.BlockSpec(memory_space=pl.ANY)
    vmem = pl.BlockSpec(memory_space=pltpu.VMEM)
    wide = pltpu.VMEM((total, dim), jnp.float32)
    return pl.pallas_call(
        functools.partial(prompt_kernel, math.log2(math.e) / math.sqrt(dim)),
        in_specs=[anywhere] * 5,
        out_specs=[vmem] * 4,
        out_shape=[pltpu.VMEM((lines + 8, dim), jnp.float32)] * 4,
        scratch_shapes=[
            pltpu.SMEM(page_table.shape, jnp.int32),
            pltpu.SMEM(prompt_len.shape, jnp.int32),
            pltpu.SMEM(sample_prompt.shape, jnp.int32),
            pltpu.VMEM(queries.shape, queries.dtype),
            pltpu.VMEM(prompt_kv.shape, prompt_kv.dtype),
            pltpu.SMEM((slots + 1,), jnp.int32),
            pltpu.SMEM(prompt_len.shape, jnp.int32),
            pltpu.SMEM(sample_prompt.shape, jnp.int32),
            wide,
            pltpu.VMEM((total, dim), jnp.bfloat16),
            pltpu.VMEM((slots, block, page_len * heads), jnp.float32),
            wide,
            wide,
            wide,
            wide,
            pltpu.SemaphoreType.DMA((5,)),
        ],
        compiler_params=pltpu.CompilerParams(vmem_limit_bytes=VMEM_LIMIT),
        name="prompt_attention",
    )(*map(in_hbm, (page_table, prompt_len, sample_prompt, queries, prompt_kv)))


def tail_kernel(scale, len_ref, q_ref, kv_hbm, out_ref, kv_ref, best_ref, norm_ref, sems):
    own, length, heads, _ = kv_ref.shape
    new, dim = q_ref.shape[1], q_ref.shape[3]
    lines, half = new * heads, length * heads // 2
    steps = sems.shape[0]
    per = own // steps
    bf16, f32 = jnp.bfloat16, jnp.float32
    copies = start_copies(
        [
            pltpu.make_async_copy(
                kv_hbm.at[pl.ds(i * per, per)], kv_ref.at[pl.ds(i * per, per)], sems.at[i]
            )
            for i in range(steps)
        ]
    )
    first = lax.axis_index("page") * own
    row = lax.broadcasted_iota(jnp.int32, (2 * lines, half), 0)
    col = lax.broadcasted_iota(jnp.int32, (2 * lines, half), 1) + (row // lines) * half
    line = row % lines
    same_head = line % heads == col % heads
    ahead = jnp.where(same_head, col // heads - line // heads, length + new)
    for step in range(steps):
        copies[step].wait()
        scores, values = [], []
        for i in range(step * per, (step + 1) * per):
            cache = flat_rows(kv_ref[i])
            keys = jnp.concatenate([cache[:half, :dim], cache[half:, :dim]], axis=1)
            values.append(jnp.concatenate([cache[:half, dim:], cache[half:, dim:]], axis=1))
            query = flat_rows(q_ref[i])
            blank = jnp.zeros_like(query)
            query = jnp.concatenate(
                [
                    jnp.concatenate([query, blank], axis=1),
                    jnp.concatenate([blank, query], axis=1),
                ],
                axis=0,
            )
            score = lax.dot_general(
                query, keys, (((1,), (1,)), ((), ())), preferred_element_type=f32
            )
            scores.append(jnp.where(ahead <= len_ref[first + i], score, NEGATIVE))
        bests = [jnp.max(score, axis=1, keepdims=True) for score in scores]
        bests = [jnp.maximum(best[:lines], best[lines:]) for best in bests]
        weights = [
            jnp.exp2((score - jnp.concatenate([best, best], axis=0)) * scale)
            for score, best in zip(scores, bests)
        ]
        norms = [jnp.sum(weight, axis=1, keepdims=True) for weight in weights]
        for i in range(per):
            mixed = jnp.dot(weights[i].astype(bf16), values[i], preferred_element_type=f32)
            at = pl.ds((step * per + i) * lines, lines)
            out_ref[at, :] = mixed[:lines, :dim] + mixed[lines:, dim:]
            best_ref[at, :] = jnp.broadcast_to(bests[i], (lines, dim))
            norm_ref[at, :] = jnp.broadcast_to(norms[i][:lines] + norms[i][lines:], (lines, dim))
    total = out_ref.shape[0] - 8
    out_ref[total : total + 1, :] = best_ref[...].T[0:1]
    out_ref[total + 1 : total + 2, :] = norm_ref[...].T[0:1]


def tail_partial(queries, tail_kv, tail_len):
    _, new, heads, dim = queries.shape
    own = tail_kv.shape[0]
    lines = own * new * heads
    return pl.pallas_call(
        functools.partial(tail_kernel, math.log2(math.e) / math.sqrt(dim)),
        grid=(1,),
        in_specs=[
            pl.BlockSpec(memory_space=pltpu.SMEM),
            pl.BlockSpec((own, new, heads, dim), lambda i: (lax.axis_index("page"), 0, 0, 0)),
            pl.BlockSpec(memory_space=pl.ANY),
        ],
        out_specs=pl.BlockSpec(memory_space=pltpu.VMEM),
        out_shape=pltpu.VMEM((lines + 8, dim), jnp.float32),
        scratch_shapes=[pltpu.VMEM(tail_kv.shape, tail_kv.dtype)]
        + [pltpu.VMEM((lines, dim), jnp.float32)] * 2
        + [pltpu.SemaphoreType.DMA((4,))],
        compiler_params=pltpu.CompilerParams(vmem_limit_bytes=VMEM_LIMIT),
        cost_estimate=FREE,
        name="tail_attention",
    )(*map(in_hbm, (tail_len, queries, tail_kv)))


def merge_kernel(scale, *refs):
    parts, out_ref, held_ref = refs[:-2], refs[-2], refs[-1]
    lines, dim = held_ref.shape
    heads = out_ref.shape[1] // dim
    bests = [part[lines : lines + 1, :] for part in parts]
    best = functools.reduce(jnp.maximum, bests)
    scales = [jnp.exp2((one - best) * scale) for one in bests]
    norm = sum(factor * part[lines + 1 : lines + 2, :] for factor, part in zip(scales, parts))
    total = jnp.zeros((lines, dim), jnp.float32)
    for factor, part in zip(scales, parts):
        share = jnp.broadcast_to(factor / norm, (lines, lines)).T
        total = total + share * part[0:lines, :]
    held_ref[...] = total
    for h in range(heads):
        out_ref[:, h * dim : (h + 1) * dim] = held_ref[
            pl.ds(h, lines // heads, stride=heads), :
        ].astype(out_ref.dtype)


def merge_partials(parts, heads):
    lines, dim = parts[0].shape[0] - 8, parts[0].shape[1]
    vmem = pl.BlockSpec(memory_space=pltpu.VMEM)
    return pl.pallas_call(
        functools.partial(merge_kernel, math.log2(math.e) / math.sqrt(dim)),
        in_specs=[vmem] * len(parts),
        out_specs=vmem,
        out_shape=jax.ShapeDtypeStruct((lines // heads, heads * dim), jnp.bfloat16),
        scratch_shapes=[pltpu.VMEM((lines, dim), jnp.float32)],
        compiler_params=pltpu.CompilerParams(vmem_limit_bytes=VMEM_LIMIT),
        name="merge_partials",
    )(*parts)


def shard_copies(w_hbm, w_ref, sems, shards, axis):
    page_pos = lax.axis_index("page")
    units = w_ref.shape[1 + axis]
    copies = []
    for i, k in enumerate(shards):
        at = pl.ds(pl.multiple_of((page_pos ^ k) * units, 128), units)
        source = w_hbm.at[:, at] if axis else w_hbm.at[at, :]
        copies.append(pltpu.make_async_copy(source, w_ref.at[i], sems.at[i]))
    return start_copies(copies)


def hold_kernel(shards, after_ref, w_hbm, out_ref, sems):
    for copy in shard_copies(w_hbm, out_ref, sems, shards, 1):
        copy.wait()


def hold_columns(after, weights, shards, units):
    depth = weights.shape[0]
    return pl.pallas_call(
        functools.partial(hold_kernel, shards),
        in_specs=[pl.BlockSpec(memory_space=pltpu.VMEM), pl.BlockSpec(memory_space=pl.ANY)],
        out_specs=pl.BlockSpec(memory_space=pltpu.VMEM),
        out_shape=pltpu.VMEM((len(shards), depth, units), weights.dtype),
        scratch_shapes=[pltpu.SemaphoreType.DMA((len(shards),))],
        compiler_params=pltpu.CompilerParams(vmem_limit_bytes=VMEM_LIMIT),
        cost_estimate=FREE,
        name="hold_columns",
    )(after, in_hbm(weights))


def project_kernel(per_group, *refs):
    blocks, (w_ref, stream_ref, keep_ref, give_ref, lhs_ref, sum_ref) = refs[:4], refs[4:]
    page_pos, blk_pos = lax.axis_index("page"), lax.axis_index("blk")
    height = blocks[0].shape[0]
    group = w_ref.shape[2]
    width = stream_ref.shape[2]
    for k, block in enumerate(blocks):
        start = pl.multiple_of((page_pos ^ k) * height, height)
        lhs_ref[pl.ds(start, height), :] = block[...]
    product = jnp.dot(lhs_ref[...], w_ref[0], preferred_element_type=jnp.float32)
    sum_ref[...] = product.reshape(sum_ref.shape)
    for part in range(per_group):

        @pl.when(blk_pos == page_pos * per_group + part)
        def _(part=part):
            stream = flat_rows(stream_ref[...]).astype(jnp.float32)
            at = (slice(None), slice(None), slice(part * width, (part + 1) * width))
            sum_ref[at] = sum_ref[at] + stream.reshape(sum_ref.shape[:2] + (width,))

    core = blk_pos % 2
    for chip in range(4):
        keep_ref[chip] = sum_ref[2 * chip + core]
        give_ref[chip] = sum_ref[2 * chip + 1 - core].astype(give_ref.dtype)


def project(blocks, w_out, stream_in, group):
    height, depth = blocks[0].shape
    rows = 4 * height
    vmem = pl.BlockSpec(memory_space=pltpu.VMEM)
    part = (4, rows // 8, group)
    return pl.pallas_call(
        functools.partial(project_kernel, group // stream_in.shape[2]),
        in_specs=[vmem] * 6,
        out_specs=[vmem] * 2,
        out_shape=[
            jax.ShapeDtypeStruct(part, jnp.float32),
            jax.ShapeDtypeStruct(part, jnp.bfloat16),
        ],
        scratch_shapes=[
            pltpu.VMEM((rows, depth), jnp.bfloat16),
            pltpu.VMEM((8, rows // 8, group), jnp.float32),
        ],
        compiler_params=pltpu.CompilerParams(vmem_limit_bytes=VMEM_LIMIT),
        name="project_attention",
    )(*blocks, w_out, stream_in)


def pair_kernel(keep_ref, got_ref, own_ref, *out_refs):
    chip = lax.axis_index("blk") // 2
    own_ref[...] = keep_ref[chip] + got_ref[chip].astype(jnp.float32)
    for k, out_ref in enumerate(out_refs, 1):
        total = keep_ref[chip ^ k] + got_ref[chip ^ k].astype(jnp.float32)
        out_ref[...] = total.astype(out_ref.dtype)


def pair_pieces(keep, got):
    vmem = pl.BlockSpec(memory_space=pltpu.VMEM)
    shape = keep.shape[1:]
    return pl.pallas_call(
        pair_kernel,
        in_specs=[vmem] * 2,
        out_specs=[vmem] * 4,
        out_shape=[jax.ShapeDtypeStruct(shape, jnp.float32)]
        + [jax.ShapeDtypeStruct(shape, jnp.bfloat16)] * 3,
        compiler_params=pltpu.CompilerParams(vmem_limit_bytes=VMEM_LIMIT),
        name="pair_pieces",
    )(keep, got)


def residual_kernel(own_ref, c_ref, b_ref, a_ref, bias_ref, score_ref, out_ref):
    group, piece = own_ref.shape[1], score_ref.shape[0]
    total = own_ref[...] + bias_ref[...].astype(jnp.float32)
    for ref in (a_ref, b_ref, c_ref):
        total = total + ref[...].astype(jnp.float32)
    out_ref[:, :group] = total.astype(out_ref.dtype)
    out_ref[:, group : group + piece] = jnp.broadcast_to(
        as_row(score_ref), (own_ref.shape[0], piece)
    ).astype(out_ref.dtype)


def residual_rows(own, arrived, b_out, w_score):
    vmem = pl.BlockSpec(memory_space=pltpu.VMEM)
    return pl.pallas_call(
        residual_kernel,
        grid=(1,),
        in_specs=[vmem] * 4
        + [pl.BlockSpec((1, own.shape[1]), lambda i: (0, lax.axis_index("page"))), vmem],
        out_specs=vmem,
        out_shape=pltpu.VMEM((own.shape[0], own.shape[1] + 256), jnp.bfloat16),
        compiler_params=pltpu.CompilerParams(vmem_limit_bytes=VMEM_LIMIT),
        name="residual_rows",
    )(own, *arrived, b_out.reshape(1, -1), w_score)


def as_row(ref):
    return ref[...].astype(jnp.float32).reshape(1, ref.shape[0])


def split2(value):
    high = value.astype(jnp.bfloat16)
    return high, (value - high.astype(jnp.float32)).astype(jnp.bfloat16)


def whole2(high, low):
    return high.astype(jnp.float32) + low.astype(jnp.float32)


def up_first_kernel(*refs):
    blocks, refs = refs[:8], refs[8:]
    gain_ref, bias_ref, down_ref, near_ref, w_hbm = refs[:5]
    out_refs, weight_ref, refs = refs[5:8], refs[8], refs[9:]
    lhs_ref, residual_ref, stats_ref, mean_ref, square_ref, base_ref, weights_ref, w_ref, sems = refs
    copies = shard_copies(w_hbm, w_ref, sems, (3, 2), 1)
    blk_pos = lax.axis_index("blk")
    core, chip = blk_pos % 2, blk_pos // 2
    height, group = blocks[0].shape[0], lhs_ref.shape[1]
    rows, piece = 8 * height, group // 8
    gain = as_row(gain_ref)
    places = []
    for i, block in enumerate(blocks):
        from_core = core if i < 4 else 1 - core
        owner = 2 * (chip ^ (i % 4)) + from_core
        places.append(pl.ds(pl.multiple_of(owner * height, height), height))
        weights_ref[pl.ds(owner, 1), :] = block[0:1, group:].astype(jnp.float32)
    weights = [weights_ref[b : b + 1, :piece] for b in range(8)]
    weight_ref[...] = jnp.concatenate(weights, axis=1)
    own_weights = [jnp.where(blk_pos == b, weight, 0.0) for b, weight in enumerate(weights)]
    score_row = jnp.concatenate(own_weights, axis=1)
    own_weight = sum(own_weights)
    fixed = jnp.sum(as_row(down_ref) * own_weight, axis=1, keepdims=True)
    for block, at in zip(blocks, places):
        residual = block[:, :group].astype(jnp.float32)
        mean = jnp.sum(residual, axis=1, keepdims=True) * (1.0 / group)
        centred = residual - mean
        square = jnp.sum(centred * centred, axis=1, keepdims=True)
        base = jnp.sum(residual * score_row, axis=1, keepdims=True) + fixed
        residual_ref[at, :] = block[:, :group]
        lhs_ref[at, :] = (centred * gain).astype(lhs_ref.dtype)
        mean_ref[at, :] = jnp.broadcast_to(mean, (height, rows))
        square_ref[at, :] = jnp.broadcast_to(square, (height, rows))
        base_ref[at, :] = jnp.broadcast_to(base, (height, rows))
    row = lax.broadcasted_iota(jnp.int32, (lhs_ref.shape[0] - rows, group), 0)
    bias = as_row(bias_ref)
    lhs_ref[rows:, :] = jnp.where(
        row == 0, gain, jnp.where(row == 1, bias, 0.0)
    ).astype(lhs_ref.dtype)
    pieces = []
    for ref in (mean_ref, square_ref, base_ref):
        pieces += split2(ref[...].T[0:1])
    stats_ref[...] = jnp.concatenate(pieces, axis=0)
    out_refs[2][...] = up_product(lhs_ref, near_ref.at[0], stats_ref, rows)
    for i in range(2):
        copies[i].wait()
        out_refs[i][...] = up_product(lhs_ref, w_ref.at[i], stats_ref, rows)


def up_product(lhs_ref, w_ref, stats_ref, rows):
    product = jnp.dot(lhs_ref[...], w_ref[...], preferred_element_type=jnp.float32)
    below = product[rows : rows + 8]
    padded = jnp.concatenate(
        [
            jnp.zeros((2, rows), jnp.float32),
            stats_ref[...].astype(jnp.float32),
        ],
        axis=0,
    )
    row = lax.broadcasted_iota(jnp.int32, (8, rows), 0)
    first = jnp.where(row < 2, below[:, :rows], padded)
    below = jnp.concatenate([first, below[:, rows:]], axis=1)
    return jnp.concatenate([product[:rows], below], axis=0).astype(jnp.bfloat16)


def up_first(blocks, ln_gain, ln_bias, b_down, near_up, w_up):
    height = blocks[0].shape[0]
    rows = 8 * height
    _, group, units = near_up.shape
    bf16, f32 = jnp.bfloat16, jnp.float32
    vmem = pl.BlockSpec(memory_space=pltpu.VMEM)
    return pl.pallas_call(
        up_first_kernel,
        in_specs=[vmem] * 12 + [pl.BlockSpec(memory_space=pl.ANY)],
        out_specs=[vmem] * 7,
        out_shape=[pltpu.VMEM((rows + 8, units), bf16)] * 3
        + [
            pltpu.VMEM((1, group), f32),
            pltpu.VMEM((rows + 16, group), bf16),
            jax.ShapeDtypeStruct((rows, group), bf16),
            pltpu.VMEM((6, rows), bf16),
        ],
        scratch_shapes=[pltpu.VMEM((rows, rows), f32)] * 3
        + [
            pltpu.VMEM((8, blocks[0].shape[1] - group), f32),
            pltpu.VMEM((2, group, units), bf16),
            pltpu.SemaphoreType.DMA((2,)),
        ],
        compiler_params=pltpu.CompilerParams(vmem_limit_bytes=VMEM_LIMIT),
        name="norm_and_up",
    )(
        *blocks,
        ln_gain,
        ln_bias,
        b_down,
        near_up,
        in_hbm(w_up),
    )


def up_own_kernel(lhs_ref, stats_ref, w_hbm, out_ref, w_ref, sems):
    copies = shard_copies(w_hbm, w_ref, sems, (0,), 1)
    copies[0].wait()
    out_ref[...] = up_product(lhs_ref, w_ref.at[0], stats_ref, stats_ref.shape[1])


def up_own(lhs, stats, w_up):
    group = lhs.shape[1]
    units = w_up.shape[1] // 4
    bf16 = jnp.bfloat16
    vmem = pl.BlockSpec(memory_space=pltpu.VMEM)
    return pl.pallas_call(
        up_own_kernel,
        in_specs=[vmem] * 2 + [pl.BlockSpec(memory_space=pl.ANY)],
        out_specs=vmem,
        out_shape=pltpu.VMEM((stats.shape[1] + 8, units), bf16),
        scratch_shapes=[pltpu.VMEM((1, group, units), bf16), pltpu.SemaphoreType.DMA((1,))],
        compiler_params=pltpu.CompilerParams(vmem_limit_bytes=VMEM_LIMIT),
        cost_estimate=FREE,
        name="up_own",
    )(lhs, stats, in_hbm(w_up))


def image_kernel(score_ref, w_ref, out_ref, column_ref):
    step = pl.program_id(0)

    @pl.when(step == 0)
    def _():
        wide = jnp.broadcast_to(score_ref[...], column_ref.shape[::-1])
        column_ref[...] = wide.T.astype(column_ref.dtype)

    image = jnp.dot(w_ref[...], column_ref[...], preferred_element_type=jnp.float32).T[0:1]
    high, low = split2(image)
    out_ref[pl.ds(step, 1), :] = high.astype(jnp.float32)
    out_ref[pl.ds(step + pl.num_programs(0), 1), :] = low.astype(jnp.float32)


def image_of(score_group, w_down):
    depth, group = w_down.shape
    tile = depth // 4
    return pl.pallas_call(
        image_kernel,
        grid=(4,),
        in_specs=[
            pl.BlockSpec((1, group), lambda i: (0, 0)),
            pl.BlockSpec((tile, group), lambda i: (i, 0)),
        ],
        out_specs=pl.BlockSpec((8, tile), lambda i: (0, 0)),
        out_shape=pltpu.VMEM((8, tile), jnp.float32),
        scratch_shapes=[pltpu.VMEM((group, 128), jnp.bfloat16)],
        compiler_params=pltpu.CompilerParams(vmem_limit_bytes=VMEM_LIMIT),
        cost_estimate=FREE,
        name="score_image",
    )(score_group, in_hbm(w_down))


def hidden_kernel(group, *refs):
    parts, (bias_ref, image_ref, whole_ref, top_ref, bottom_ref, base_ref) = refs[:4], refs[4:]
    rows, cut = parts[0].shape[0] - 8, top_ref.shape[0]
    f32 = jnp.float32
    tails = [part[rows:, :].astype(f32) for part in parts]
    stats = [
        [tail[2 + i : 3 + i, :rows] + tail[3 + i : 4 + i, :rows] for tail in tails]
        for i in (0, 2, 4)
    ]
    means, squares, bases = stats
    row_mean = pair_sum(means) * 0.25
    shifts = [mean - row_mean for mean in means]
    spread = sum(square + group * shift * shift for square, shift in zip(squares, shifts))
    inverse = lax.rsqrt(spread * (0.25 / group) + EPS)
    pad = jnp.zeros((rows - 6, rows), f32)
    columns = jnp.concatenate([inverse, *shifts, pair_sum(bases), pad], axis=0).T
    offset = sum(tail[1:2] for tail in tails) + bias_ref[...].astype(f32)
    total = sum(part[0:rows, :].astype(f32) for part in parts)
    for k, tail in enumerate(tails):
        total = total + columns[:, 1 + k : 2 + k] * tail[0:1]
    hidden = jnp.maximum(total * columns[:, 0:1] + offset, 0.0)
    below = jnp.concatenate([hidden, image_ref[...]], axis=0).astype(whole_ref.dtype)
    whole_ref[...] = below
    top_ref[...] = below[:cut]
    bottom_ref[...] = below[cut:]
    base_ref[...] = columns[:, 5:6]


def own_hidden_units(parts, b_up, image, group):
    vmem = pl.BlockSpec(memory_space=pltpu.VMEM)
    height, units = parts[0].shape
    bf16 = jnp.bfloat16
    return pl.pallas_call(
        functools.partial(hidden_kernel, group),
        grid=(1,),
        in_specs=[vmem] * 4
        + [pl.BlockSpec((1, units), lambda i: (0, lax.axis_index("page"))), vmem],
        out_specs=[vmem] * 4,
        out_shape=[
            pltpu.VMEM((height, units), bf16),
            pltpu.VMEM((TOP, units), bf16),
            pltpu.VMEM((height - TOP, units), bf16),
            pltpu.VMEM((height - 8, 1), jnp.float32),
        ],
        compiler_params=pltpu.CompilerParams(vmem_limit_bytes=VMEM_LIMIT),
        name="hidden_units",
    )(*parts, b_up.reshape(1, -1), image)


def down_first_kernel(hidden_ref, w_hbm, sum_ref, held_ref, w_ref, sems, held_sems):
    rows = sum_ref.shape[0]
    copies = shard_copies(w_hbm, w_ref, sems, (0,), 0)
    held = shard_copies(w_hbm, held_ref, held_sems, (1, 2, 3), 0)
    copies[0].wait()
    sum_ref[...] = jnp.dot(
        hidden_ref[0:rows, :], w_ref[0], preferred_element_type=jnp.float32
    )
    for copy in held:
        copy.wait()


def down_first(hidden, w_down):
    rows, units = hidden.shape[0] - 8, hidden.shape[1]
    group = w_down.shape[1]
    vmem = pl.BlockSpec(memory_space=pltpu.VMEM)
    return pl.pallas_call(
        down_first_kernel,
        in_specs=[vmem, pl.BlockSpec(memory_space=pl.ANY)],
        out_specs=[vmem] * 2,
        out_shape=[
            pltpu.VMEM((rows, group), jnp.float32),
            pltpu.VMEM((3, units, group), jnp.bfloat16),
        ],
        scratch_shapes=[
            pltpu.VMEM((1, units, group), jnp.bfloat16),
            pltpu.SemaphoreType.DMA((1,)),
            pltpu.SemaphoreType.DMA((3,)),
        ],
        compiler_params=pltpu.CompilerParams(vmem_limit_bytes=VMEM_LIMIT),
        cost_estimate=FREE,
        name="down_own",
    )(hidden, in_hbm(w_down))


def down_rest_kernel(base_ref, sum_ref, held_ref, *refs):
    parts, (keep_ref, give_ref, score_ref, image_ref) = refs[:6], refs[6:]
    rows = sum_ref.shape[0]
    f32 = jnp.float32
    page_pos = lax.axis_index("page")
    core = lax.axis_index("blk") % 2
    piece = keep_ref.shape[2]
    cut = parts[2].shape[0]
    hiddens = [part[0:rows, :] for part in parts[:2]]
    for top, bottom in (parts[2:4], parts[4:6]):
        hiddens.append(jnp.concatenate([top[...], bottom[0 : rows - cut, :]], axis=0))
    product = sum_ref[...]
    for k in (1, 2, 3):
        product = product + jnp.dot(hiddens[k], held_ref[k - 1], preferred_element_type=f32)
    tails = [
        part[part.shape[0] - 8 :, :].astype(f32) for part in (*parts[:2], parts[3], parts[5])
    ]
    image_ref[...] = pair_sum([tail[0:4] + tail[4:8] for tail in tails])
    by_owner = []
    for k, hidden in enumerate(hiddens):
        image = image_ref[pl.ds(page_pos ^ k, 1), :]
        by_owner.append(jnp.sum(hidden.astype(f32) * image, axis=1, keepdims=True))
    score = base_ref[...] + pair_sum(by_owner)
    score_ref[...] = score
    pieces = split3(score)
    for chip in range(4):
        pair = [product[:, (2 * chip + c) * piece : (2 * chip + c + 1) * piece] for c in range(2)]
        keep_ref[chip] = jnp.where(core == 0, pair[0], pair[1])
        give_ref[chip, :, :piece] = jnp.where(core == 0, pair[1], pair[0]).astype(give_ref.dtype)
        give_ref[chip, :, piece:] = pieces


def down_rest(base, summed, held, parts):
    rows, group = summed.shape
    units = parts[0].shape[1]
    vmem = pl.BlockSpec(memory_space=pltpu.VMEM)
    return pl.pallas_call(
        down_rest_kernel,
        in_specs=[vmem] * 9,
        out_specs=[vmem] * 3,
        out_shape=[
            pltpu.VMEM((4, rows, group // 8), jnp.float32),
            pltpu.VMEM((4, rows, group // 8 + 3), jnp.bfloat16),
            pltpu.VMEM((rows, 1), jnp.float32),
        ],
        scratch_shapes=[pltpu.VMEM((4, units), jnp.float32)],
        compiler_params=pltpu.CompilerParams(vmem_limit_bytes=VMEM_LIMIT),
        name="down_rest",
    )(base, summed, held, *parts)


def split3(value):
    high = value.astype(jnp.bfloat16)
    left = value - high.astype(jnp.float32)
    middle = left.astype(jnp.bfloat16)
    low = (left - middle.astype(jnp.float32)).astype(jnp.bfloat16)
    return jnp.concatenate([high, middle, low], axis=1)


def whole3(pieces):
    return jnp.sum(pieces.astype(jnp.float32), axis=1, keepdims=True)


def pair_score_kernel(keep_ref, score_ref, got_ref, own_ref, both_ref, *out_refs):
    chip = lax.axis_index("blk") // 2
    piece = keep_ref.shape[2]
    score = whole3(split3(score_ref[...])) + whole3(got_ref[0, :, piece:])
    both_ref[...] = score
    pieces = split3(score)
    own_ref[...] = keep_ref[chip] + got_ref[chip, :, :piece].astype(jnp.float32)
    for k, out_ref in enumerate(out_refs, 1):
        total = keep_ref[chip ^ k] + got_ref[chip ^ k, :, :piece].astype(jnp.float32)
        out_ref[:, :piece] = total.astype(out_ref.dtype)
        out_ref[:, piece:] = pieces


def pair_scores(keep, score, got):
    vmem = pl.BlockSpec(memory_space=pltpu.VMEM)
    _, rows, piece = keep.shape
    return pl.pallas_call(
        pair_score_kernel,
        in_specs=[vmem] * 3,
        out_specs=[vmem] * 5,
        out_shape=[
            jax.ShapeDtypeStruct((rows, piece), jnp.float32),
            jax.ShapeDtypeStruct((rows, 1), jnp.float32),
        ]
        + [jax.ShapeDtypeStruct((rows, piece + 3), jnp.bfloat16)] * 3,
        compiler_params=pltpu.CompilerParams(vmem_limit_bytes=VMEM_LIMIT),
        name="pair_scores",
    )(keep, score, got)


def finish_kernel(own_ref, base_ref, score_ref, c_ref, b_ref, a_ref, out_ref, total_ref, held_ref):
    piece = own_ref.shape[1]
    total = own_ref[...] + base_ref[...]
    for ref in (a_ref, b_ref, c_ref):
        total = total + ref[:, :piece].astype(jnp.float32)
    out_ref[...] = total.astype(out_ref.dtype).reshape(out_ref.shape)
    scores = [whole3(ref[:, piece:]) for ref in (a_ref, b_ref, c_ref)]
    own_score = whole3(split3(score_ref[...]))
    score = (own_score + scores[0]) + (scores[1] + scores[2])
    new, samples = total_ref.shape
    held_ref[...] = jnp.broadcast_to(score, held_ref.shape)
    for n in range(new):
        total_ref[n : n + 1, :] = held_ref[pl.ds(n, samples, stride=new), :].T[0:1]


def finish(own, base, score, arrived, samples):
    vmem = pl.BlockSpec(memory_space=pltpu.VMEM)
    rows, piece = own.shape
    return pl.pallas_call(
        finish_kernel,
        in_specs=[vmem] * 6,
        out_specs=[vmem] * 2,
        out_shape=[
            jax.ShapeDtypeStruct((samples, rows // samples, piece), jnp.bfloat16),
            jax.ShapeDtypeStruct((rows // samples, samples), jnp.float32),
        ],
        scratch_shapes=[pltpu.VMEM((rows, 128), jnp.float32)],
        compiler_params=pltpu.CompilerParams(vmem_limit_bytes=VMEM_LIMIT),
        name="finish",
    )(own, base, score, *arrived)


def body(
    queries,
    prompt_kv,
    tail_kv,
    page_table,
    prompt_len,
    tail_len,
    sample_prompt,
    stream_in,
    w_out,
    b_out,
    ln_gain,
    ln_bias,
    w_up,
    b_up,
    w_down,
    b_down,
    w_score,
):
    bf16, f32 = jnp.bfloat16, jnp.float32
    samples, new_count, heads_dev, head_dim = queries.shape
    group = ln_gain.shape[0]
    blk_pos = lax.axis_index("blk")
    piece = b_down.shape[0]
    packed = prompt_partial(queries, prompt_kv, page_table, prompt_len, sample_prompt)
    shares = [packed[0]] + [send_xor(packed[k], "page", k) for k in (1, 2, 3)]
    tail = tail_partial(queries, tail_kv, tail_len)
    own_attention = merge_partials(shares + [tail], heads_dev)
    attention = gather_xor(own_attention, "page", (1, 2, 3))
    held_out = hold_columns(own_attention, w_out, (0,), group)
    keep, give = project(attention, held_out, stream_in, group)
    own, *pieces = pair_pieces(keep, send_xor(give, "blk", 1))
    units = w_up.shape[1] // 4
    arrived = [send_xor(pieces[k - 1], "blk", 2 * k) for k in (3, 2, 1)]
    own_rows = residual_rows(own, arrived, b_out, w_score)
    same_core = gather_xor(own_rows, "blk", (2, 4, 6))
    near_up = hold_columns(own_rows, w_up, (1,), units)
    same_core[1], near_up = lax.optimization_barrier((same_core[1], near_up))
    blocks = same_core + [send_xor(block, "blk", 1) for block in same_core]
    part3, part2, part1, score_group, lhs, residual, stats = up_first(
        blocks, ln_gain, ln_bias, b_down, near_up, w_up
    )
    part0 = up_own(lhs, stats, w_up)
    image = image_of(score_group, w_down)
    parts = [part0] + [
        send_xor(part, "page", k) for k, part in ((1, part1), (2, part2), (3, part3))
    ]
    whole, top, bottom, base_score = own_hidden_units(parts, b_up, image, group)
    summed, held = down_first(whole, w_down)
    far_top, summed = lax.optimization_barrier((send_xor(top, "page", 2), summed))
    hiddens = [
        whole,
        send_xor(whole, "page", 1),
        far_top,
        send_xor(bottom, "page", 2),
        send_xor(far_top, "page", 1),
        send_xor(bottom, "page", 3),
    ]
    keep, give, score = down_rest(base_score, summed, held, hiddens)
    own_base = lax.dynamic_slice_in_dim(residual, blk_pos * piece, piece, 1).astype(
        f32
    ) + b_down.astype(f32)
    own, score, *pieces = pair_scores(keep, score, send_xor(give, "blk", 1))
    arrived = [send_xor(pieces[k - 1], "blk", 2 * k) for k in (3, 2, 1)]
    output, score = finish(own, own_base, score, arrived, samples)
    return (output, score.T)


def general_body(
    queries,
    prompt_kv,
    tail_kv,
    page_table,
    prompt_len,
    tail_len,
    sample_prompt,
    stream_in,
    w_out,
    b_out,
    ln_gain,
    ln_bias,
    w_up,
    b_up,
    w_down,
    b_down,
    w_score,
):
    samples, new_count, heads_dev, head_dim = queries.shape
    slots_dev, page_len = (prompt_kv.shape[0], prompt_kv.shape[1])
    own_count, tail_max = (tail_kv.shape[0], tail_kv.shape[1])
    prompts, pages_max = page_table.shape
    page_pos = lax.axis_index("page")
    blk_pos = lax.axis_index("blk")
    inv_sqrt = 1.0 / math.sqrt(head_dim)
    entries = page_table.reshape(-1)
    slot_ids = page_pos * slots_dev + jnp.arange(slots_dev, dtype=jnp.int32)
    matched = (entries[:, None] == slot_ids[None, :]).astype(jnp.int32)
    owner_index = jnp.sum(matched * jnp.arange(entries.shape[0], dtype=jnp.int32)[:, None], axis=0)
    slot_prompt = owner_index // pages_max
    slot_page = owner_index % pages_max
    prompt_pick = (slot_prompt[:, None] == jnp.arange(prompts, dtype=jnp.int32)[None, :]).astype(
        jnp.int32
    )
    slot_limit = jnp.sum(prompt_pick * prompt_len[None, :], axis=1)
    key_pos = slot_page[:, None] * page_len + jnp.arange(page_len, dtype=jnp.int32)[None, :]
    key_live = (key_pos < slot_limit[:, None]).reshape(-1)
    key_prompt = jnp.repeat(slot_prompt, page_len)
    prompt_visible = ((sample_prompt[:, None] == key_prompt[None, :]) & key_live[None, :])[
        :, None, None, :
    ]
    cache_rows = prompt_kv.reshape(slots_dev * page_len, heads_dev, 2 * head_dim)
    prompt_scores = (
        jnp.einsum(
            "snhd,khd->snhk",
            queries,
            cache_rows[:, :, :head_dim],
            preferred_element_type=jnp.float32,
        )
        * inv_sqrt
    )
    high_p, sum_p, weights_p = softmax_part(prompt_scores, prompt_visible)
    mixed_p = jnp.einsum(
        "snhk,khd->snhd", weights_p, cache_rows[:, :, head_dim:], preferred_element_type=jnp.float32
    )
    first_row = page_pos * own_count
    own_queries = lax.dynamic_slice_in_dim(queries, first_row, own_count, 0)
    own_lengths = lax.dynamic_slice_in_dim(tail_len, first_row, own_count, 0)
    tail_scores = (
        jnp.einsum(
            "snhd,sthd->snht",
            own_queries,
            tail_kv[..., :head_dim],
            preferred_element_type=jnp.float32,
        )
        * inv_sqrt
    )
    reach_pos = own_lengths[:, None] + jnp.arange(new_count, dtype=jnp.int32)[None, :]
    tail_visible = (
        jnp.arange(tail_max, dtype=jnp.int32)[None, None, None, :] <= reach_pos[:, :, None, None]
    )
    high_t, sum_t, weights_t = softmax_part(tail_scores, tail_visible)
    mixed_t = jnp.einsum(
        "snht,sthd->snhd", weights_t, tail_kv[..., head_dim:], preferred_element_type=jnp.float32
    )
    high_t = lax.dynamic_update_slice_in_dim(
        jnp.full(high_p.shape, NEGATIVE, jnp.float32), high_t, first_row, 0
    )
    sum_t = lax.dynamic_update_slice_in_dim(
        jnp.zeros(sum_p.shape, jnp.float32), sum_t, first_row, 0
    )
    mixed_t = lax.dynamic_update_slice_in_dim(
        jnp.zeros(mixed_p.shape, jnp.float32), mixed_t, first_row, 0
    )
    partial_value = join_partials((high_p, sum_p, mixed_p), (high_t, sum_t, mixed_t))
    merged = combined_all(partial_value, "page", join_partials)
    weight_sum, weighted = (merged[1], merged[2])
    attention = (
        (weighted / weight_sum[..., None])
        .astype(jnp.bfloat16)
        .reshape(samples * new_count, heads_dev * head_dim)
    )
    contrib = jnp.dot(attention, w_out, preferred_element_type=jnp.float32)
    slice_width = stream_in.shape[2]
    column = blk_pos * slice_width
    own_stream = stream_in.reshape(samples * new_count, slice_width).astype(jnp.float32)
    contrib = lax.dynamic_update_slice_in_dim(
        contrib, lax.dynamic_slice_in_dim(contrib, column, slice_width, 1) + own_stream, column, 1
    )
    summed = lax.psum(contrib, "blk")
    residual = (summed + b_out.astype(jnp.float32)).astype(jnp.bfloat16)
    residual_f = residual.astype(jnp.float32)
    row_mean = jnp.mean(residual_f, axis=-1, keepdims=True)
    centred = residual_f - row_mean
    inverse_std = lax.rsqrt(jnp.mean(centred * centred, axis=-1, keepdims=True) + 1e-05)
    feature_count = ln_gain.shape[0]
    first_col = page_pos * feature_count
    normed = (
        lax.dynamic_slice_in_dim(centred, first_col, feature_count, 1)
        * inverse_std
        * ln_gain.astype(jnp.float32)
        + ln_bias.astype(jnp.float32)
    ).astype(jnp.bfloat16)
    up_part = jnp.dot(normed, w_up, preferred_element_type=jnp.float32).astype(jnp.bfloat16)
    hidden_sum = lax.psum(up_part, "page").astype(jnp.float32)
    hidden = jnp.maximum(hidden_sum + b_up.astype(jnp.float32), 0.0).astype(jnp.bfloat16)
    projected = jnp.dot(hidden, w_down, preferred_element_type=jnp.float32)
    out_share = lax.psum_scatter(projected, "blk", scatter_dimension=1, tiled=True)
    piece_width = b_down.shape[0]
    out_column = first_col + blk_pos * piece_width
    output = (
        out_share
        + lax.dynamic_slice_in_dim(residual_f, out_column, piece_width, 1)
        + b_down.astype(jnp.float32)
    ).astype(jnp.bfloat16)
    score_part = jnp.sum(output.astype(jnp.float32) * w_score.astype(jnp.float32), axis=-1)
    row_score = lax.psum(score_part, ("page", "blk"))
    return (output.reshape(samples, new_count, piece_width), row_score.reshape(samples, new_count))


def solution(mesh):
    compute = body if (mesh.shape["page"], mesh.shape["blk"]) == (4, 8) else general_body

    placed = (
        P(None, None, "blk", None),
        P("page", None, "blk", None),
        P("page", None, "blk", None),
        P(),
        P(),
        P(),
        P(),
        P(None, None, "blk"),
        P("blk", None),
        P(),
        P("page"),
        P("page"),
        P("page", "blk"),
        P("blk"),
        P("blk", "page"),
        P(("page", "blk")),
        P(("page", "blk")),
    )
    return jax.shard_map(
        compute,
        mesh=mesh,
        in_specs=placed,
        out_specs=(P(None, None, ("page", "blk")), P()),
        check_vma=False,
    )
```

```python
import functools
import math

import jax
import jax.numpy as jnp
from jax import lax
from jax.experimental import pallas as pl
from jax.experimental.pallas import tpu as pltpu
from jax.sharding import PartitionSpec as P

NEGATIVE = -1e30
EPS = 1e-05
VMEM_LIMIT = 24 * 2**20
TOP = 48
FREE = pl.CostEstimate(flops=0, bytes_accessed=0, transcendentals=0)


def combined_all(value, axis, join):
    pieces = jax.tree.map(lambda part: lax.all_gather(part, axis), value)
    head = jax.tree.map(lambda part: part[0], pieces)
    tail = jax.tree.map(lambda part: part[1:], pieces)
    subtotal, _ = lax.scan(lambda subtotal, share: (join(subtotal, share), None), head, tail)
    return subtotal


def join_partials(earlier, later):
    highest = jnp.maximum(earlier[0], later[0])
    left_scale = jnp.exp(earlier[0] - highest)
    right_scale = jnp.exp(later[0] - highest)
    return (
        highest,
        earlier[1] * left_scale + later[1] * right_scale,
        earlier[2] * left_scale[..., None] + later[2] * right_scale[..., None],
    )


def softmax_part(scores, visible):
    masked = jnp.where(visible, scores, NEGATIVE)
    highest = jnp.max(masked, axis=-1)
    weights = jnp.where(visible, jnp.exp(scores - highest[..., None]), 0.0)
    return (highest, jnp.sum(weights, axis=-1), weights.astype(jnp.bfloat16))


def send_xor(value, axis, distance):
    size = lax.axis_size(axis)
    return lax.ppermute(value, axis, [(i, i ^ distance) for i in range(size)])


def in_hbm(value):
    return pltpu.with_memory_space_constraint(value, pltpu.HBM)


def gather_xor(value, axis, distances):
    return [value] + [send_xor(value, axis, k) for k in distances]


def pair_sum(pieces):
    return (pieces[0] + pieces[1]) + (pieces[2] + pieces[3])


def start_copies(copies):
    for copy in copies:
        copy.start()
    return copies


def flat_rows(ref_value):
    shape = ref_value.shape
    return ref_value.reshape(math.prod(shape[:-1]), shape[-1])


def pieces3(value):
    high = value.astype(jnp.bfloat16)
    left = value - high.astype(jnp.float32)
    middle = left.astype(jnp.bfloat16)
    return high, middle, (left - middle.astype(jnp.float32)).astype(jnp.bfloat16)


def prompt_kernel(scale, table_hbm, len_hbm, prompt_hbm, q_hbm, kv_hbm, tail_hbm, *refs):
    outs, held_ref, refs = refs[:4], refs[4], refs[5:]
    table_ref, len_ref, prompt_ref, q_ref, kv_ref, where_ref, count_ref, place_ref = refs[:8]
    query_ref, rows_ref, score_ref, best_ref, norm_ref, mixed_ref, back_ref, sent_ref, sems = refs[8:]
    copies = start_copies(
        [
            pltpu.make_async_copy(source, target, sems.at[i])
            for i, (source, target) in enumerate(
                (
                    (table_hbm, table_ref),
                    (len_hbm, len_ref),
                    (prompt_hbm, prompt_ref),
                    (q_hbm, q_ref),
                    (kv_hbm, kv_ref),
                    (tail_hbm.at[pl.ds(0, held_ref.shape[0])], held_ref),
                )
            )
        ]
    )
    prompts, pages_max = table_ref.shape
    slots, page_len, heads, _ = kv_ref.shape
    samples, new = q_ref.shape[:2]
    dim = q_ref.shape[3]
    lines = outs[0].shape[0] - 8
    small = new * heads
    block = samples // prompts * small
    bf16, f32 = jnp.bfloat16, jnp.float32
    page_pos = lax.axis_index("page")
    first = page_pos * slots
    best_ref[...] = jnp.full(best_ref.shape, NEGATIVE, f32)
    norm_ref[...] = jnp.zeros(norm_ref.shape, f32)
    mixed_ref[...] = jnp.zeros(mixed_ref.shape, f32)
    for copy in copies[:3]:
        copy.wait()
    for p in range(prompts):
        count_ref[p] = p * (samples // prompts)
        for g in range(pages_max):
            slot = table_ref[p, g] - first
            here = jnp.logical_and(slot >= 0, slot < slots)
            where_ref[jnp.where(here, slot, slots)] = p * pages_max + g
    copies[3].wait()
    query_ref[...] = flat_rows(q_ref[...]).astype(f32)
    for s in range(samples):
        prompt = prompt_ref[s]
        place = count_ref[prompt]
        count_ref[prompt] = place + 1
        place_ref[s] = place
        to = pl.ds(pl.multiple_of(place * small, small), small)
        back_ref[to, :] = query_ref[s * small : (s + 1) * small, :]
    rows_ref[...] = back_ref[...].astype(bf16)
    width = page_len * heads
    row = lax.broadcasted_iota(jnp.int32, (block, width), 0)
    col = lax.broadcasted_iota(jnp.int32, (block, width), 1)
    position = jnp.where(row % heads == col % heads, col, page_len * heads * pages_max)
    copies[4].wait()
    cache = flat_rows(kv_ref[...])
    at = []
    for j in range(slots):
        entry = where_ref[j]
        prompt = entry // pages_max
        left = (len_ref[prompt] - (entry % pages_max) * page_len) * heads
        at.append(pl.ds(pl.multiple_of(prompt * block, block), block))
        scores = lax.dot_general(
            rows_ref[at[j], :],
            cache[j * width : (j + 1) * width, :dim],
            (((1,), (1,)), ((), ())),
            preferred_element_type=f32,
        )
        scores = jnp.where(position < jnp.minimum(left, width), scores, NEGATIVE)
        score_ref[j] = scores
        best = jnp.max(scores, axis=1, keepdims=True)
        best_ref[at[j], :] = jnp.maximum(best_ref[at[j], :], best)
    for j in range(slots):
        best = best_ref[at[j], :]
        best = jnp.concatenate([best] * (width // dim), axis=1)
        weights = jnp.exp2((score_ref[j] - best) * scale)
        norm_ref[at[j], :] += jnp.sum(weights, axis=1, keepdims=True)
        mixed_ref[at[j], :] += jnp.dot(
            weights.astype(bf16),
            cache[j * width : (j + 1) * width, dim:],
            preferred_element_type=f32,
        )
    for k, out_ref in enumerate(outs):
        for i in range(lines // small):
            place = place_ref[(page_pos ^ k) * (lines // small) + i]
            source = pl.ds(pl.multiple_of(place * small, small), small)
            to = slice(i * small, (i + 1) * small)
            if k == 0:
                out_ref[to, :] = mixed_ref[source, :]
            else:
                sent_ref[to, :] = mixed_ref[source, :]
            back_ref[k * lines + i * small : k * lines + (i + 1) * small, :] = best_ref[source, :]
            query_ref[k * lines + i * small : k * lines + (i + 1) * small, :] = norm_ref[source, :]
        if k > 0:
            out_ref[0:lines, :] = sent_ref[...].astype(bf16)
        best = back_ref[k * lines : (k + 1) * lines, :].T[0:1]
        norm = query_ref[k * lines : (k + 1) * lines, :].T[0:1]
        if k == 0:
            out_ref[lines : lines + 1, :] = best
            out_ref[lines + 1 : lines + 2, :] = norm
        else:
            pad = jnp.zeros((2, dim), bf16)
            out_ref[lines : lines + 8, :] = jnp.concatenate(
                [*pieces3(best), *pieces3(norm), pad], axis=0
            )
    copies[5].wait()


def prompt_partial(queries, prompt_kv, tail_kv, page_table, prompt_len, sample_prompt):
    samples, new, heads, dim = queries.shape
    slots, page_len = prompt_kv.shape[:2]
    total = samples * new * heads
    block = total // page_table.shape[0]
    lines = total // 4
    anywhere = pl.BlockSpec(memory_space=pl.ANY)
    vmem = pl.BlockSpec(memory_space=pltpu.VMEM)
    wide = pltpu.VMEM((total, dim), jnp.float32)
    return pl.pallas_call(
        functools.partial(prompt_kernel, math.log2(math.e) / math.sqrt(dim)),
        in_specs=[anywhere] * 6,
        out_specs=[vmem] * 5,
        out_shape=[pltpu.VMEM((lines + 8, dim), jnp.float32)]
        + [pltpu.VMEM((lines + 8, dim), jnp.bfloat16)] * 3
        + [pltpu.VMEM((tail_kv.shape[0] // 2, *tail_kv.shape[1:]), tail_kv.dtype)],
        scratch_shapes=[
            pltpu.SMEM(page_table.shape, jnp.int32),
            pltpu.SMEM(prompt_len.shape, jnp.int32),
            pltpu.SMEM(sample_prompt.shape, jnp.int32),
            pltpu.VMEM(queries.shape, queries.dtype),
            pltpu.VMEM(prompt_kv.shape, prompt_kv.dtype),
            pltpu.SMEM((slots + 1,), jnp.int32),
            pltpu.SMEM(prompt_len.shape, jnp.int32),
            pltpu.SMEM(sample_prompt.shape, jnp.int32),
            wide,
            pltpu.VMEM((total, dim), jnp.bfloat16),
            pltpu.VMEM((slots, block, page_len * heads), jnp.float32),
            wide,
            wide,
            wide,
            wide,
            pltpu.VMEM((lines, dim), jnp.float32),
            pltpu.SemaphoreType.DMA((6,)),
        ],
        compiler_params=pltpu.CompilerParams(vmem_limit_bytes=VMEM_LIMIT),
        name="prompt_attention",
    )(*map(in_hbm, (page_table, prompt_len, sample_prompt, queries, prompt_kv, tail_kv)))


def tail_kernel(scale, len_ref, q_ref, held_ref, kv_hbm, out_ref, kv_ref, best_ref, norm_ref, sems):
    held, length, heads, _ = held_ref.shape
    own = held + kv_ref.shape[0]
    new, dim = q_ref.shape[1], q_ref.shape[3]
    lines, half = new * heads, length * heads // 2
    steps = 2 * sems.shape[0]
    per = own // steps
    bf16, f32 = jnp.bfloat16, jnp.float32
    copies = start_copies(
        [
            pltpu.make_async_copy(
                kv_hbm.at[pl.ds(held + i * per, per)], kv_ref.at[pl.ds(i * per, per)], sems.at[i]
            )
            for i in range(steps // 2)
        ]
    )
    first = lax.axis_index("page") * own
    row = lax.broadcasted_iota(jnp.int32, (2 * lines, half), 0)
    col = lax.broadcasted_iota(jnp.int32, (2 * lines, half), 1) + (row // lines) * half
    line = row % lines
    same_head = line % heads == col % heads
    ahead = jnp.where(same_head, col // heads - line // heads, length + new)
    for step in range(steps):
        if step >= steps // 2:
            copies[step - steps // 2].wait()
        scores, values = [], []
        for i in range(step * per, (step + 1) * per):
            cache = flat_rows(held_ref[i] if i < held else kv_ref[i - held])
            keys = jnp.concatenate([cache[:half, :dim], cache[half:, :dim]], axis=1)
            values.append(jnp.concatenate([cache[:half, dim:], cache[half:, dim:]], axis=1))
            query = flat_rows(q_ref[i])
            blank = jnp.zeros_like(query)
            query = jnp.concatenate(
                [
                    jnp.concatenate([query, blank], axis=1),
                    jnp.concatenate([blank, query], axis=1),
                ],
                axis=0,
            )
            score = lax.dot_general(
                query, keys, (((1,), (1,)), ((), ())), preferred_element_type=f32
            )
            scores.append(jnp.where(ahead <= len_ref[first + i], score, NEGATIVE))
        bests = [jnp.max(score, axis=1, keepdims=True) for score in scores]
        bests = [jnp.maximum(best[:lines], best[lines:]) for best in bests]
        weights = [
            jnp.exp2((score - jnp.concatenate([best, best], axis=0)) * scale)
            for score, best in zip(scores, bests)
        ]
        norms = [jnp.sum(weight, axis=1, keepdims=True) for weight in weights]
        for i in range(per):
            mixed = jnp.dot(weights[i].astype(bf16), values[i], preferred_element_type=f32)
            at = pl.ds((step * per + i) * lines, lines)
            out_ref[at, :] = mixed[:lines, :dim] + mixed[lines:, dim:]
            best_ref[at, :] = jnp.broadcast_to(bests[i], (lines, dim))
            norm_ref[at, :] = jnp.broadcast_to(norms[i][:lines] + norms[i][lines:], (lines, dim))
    total = out_ref.shape[0] - 8
    out_ref[total : total + 1, :] = best_ref[...].T[0:1]
    out_ref[total + 1 : total + 2, :] = norm_ref[...].T[0:1]


def tail_partial(queries, held_tail, tail_kv, tail_len):
    _, new, heads, dim = queries.shape
    own = tail_kv.shape[0]
    lines = own * new * heads
    return pl.pallas_call(
        functools.partial(tail_kernel, math.log2(math.e) / math.sqrt(dim)),
        grid=(1,),
        in_specs=[
            pl.BlockSpec(memory_space=pltpu.SMEM),
            pl.BlockSpec((own, new, heads, dim), lambda i: (lax.axis_index("page"), 0, 0, 0)),
            pl.BlockSpec(memory_space=pltpu.VMEM),
            pl.BlockSpec(memory_space=pl.ANY),
        ],
        out_specs=pl.BlockSpec(memory_space=pltpu.VMEM),
        out_shape=pltpu.VMEM((lines + 8, dim), jnp.float32),
        scratch_shapes=[pltpu.VMEM(held_tail.shape, tail_kv.dtype)]
        + [pltpu.VMEM((lines, dim), jnp.float32)] * 2
        + [pltpu.SemaphoreType.DMA((2,))],
        compiler_params=pltpu.CompilerParams(vmem_limit_bytes=VMEM_LIMIT),
        cost_estimate=FREE,
        name="tail_attention",
    )(in_hbm(tail_len), in_hbm(queries), held_tail, in_hbm(tail_kv))


def merge_kernel(scale, *refs):
    parts, out_ref, held_ref = refs[:-2], refs[-2], refs[-1]
    lines, dim = held_ref.shape
    heads = out_ref.shape[1] // dim
    bests, norms = [], []
    for part in parts:
        below = part[lines : lines + 8, :].astype(jnp.float32)
        if part.dtype == jnp.float32:
            bests.append(below[0:1])
            norms.append(below[1:2])
        else:
            bests.append((below[0:1] + below[1:2]) + below[2:3])
            norms.append((below[3:4] + below[4:5]) + below[5:6])
    best = functools.reduce(jnp.maximum, bests)
    scales = [jnp.exp2((one - best) * scale) for one in bests]
    norm = sum(factor * own_norm for factor, own_norm in zip(scales, norms))
    total = jnp.zeros((lines, dim), jnp.float32)
    for factor, part in zip(scales, parts):
        share = jnp.broadcast_to(factor / norm, (lines, lines)).T
        total = total + share * part[0:lines, :].astype(jnp.float32)
    held_ref[...] = total
    for h in range(heads):
        out_ref[:, h * dim : (h + 1) * dim] = held_ref[
            pl.ds(h, lines // heads, stride=heads), :
        ].astype(out_ref.dtype)


def merge_partials(parts, heads):
    lines, dim = parts[0].shape[0] - 8, parts[0].shape[1]
    vmem = pl.BlockSpec(memory_space=pltpu.VMEM)
    return pl.pallas_call(
        functools.partial(merge_kernel, math.log2(math.e) / math.sqrt(dim)),
        in_specs=[vmem] * len(parts),
        out_specs=vmem,
        out_shape=jax.ShapeDtypeStruct((lines // heads, heads * dim), jnp.bfloat16),
        scratch_shapes=[pltpu.VMEM((lines, dim), jnp.float32)],
        compiler_params=pltpu.CompilerParams(vmem_limit_bytes=VMEM_LIMIT),
        name="merge_partials",
    )(*parts)


def shard_copies(w_hbm, w_ref, sems, shards, axis):
    page_pos = lax.axis_index("page")
    units = w_ref.shape[1 + axis]
    copies = []
    for i, k in enumerate(shards):
        at = pl.ds(pl.multiple_of((page_pos ^ k) * units, 128), units)
        source = w_hbm.at[:, at] if axis else w_hbm.at[at, :]
        copies.append(pltpu.make_async_copy(source, w_ref.at[i], sems.at[i]))
    return start_copies(copies)


def hold_kernel(shards, after_ref, w_hbm, out_ref, sems):
    for copy in shard_copies(w_hbm, out_ref, sems, shards, 1):
        copy.wait()


def hold_columns(after, weights, shards, units):
    depth = weights.shape[0]
    return pl.pallas_call(
        functools.partial(hold_kernel, shards),
        in_specs=[pl.BlockSpec(memory_space=pltpu.VMEM), pl.BlockSpec(memory_space=pl.ANY)],
        out_specs=pl.BlockSpec(memory_space=pltpu.VMEM),
        out_shape=pltpu.VMEM((len(shards), depth, units), weights.dtype),
        scratch_shapes=[pltpu.SemaphoreType.DMA((len(shards),))],
        compiler_params=pltpu.CompilerParams(vmem_limit_bytes=VMEM_LIMIT),
        cost_estimate=FREE,
        name="hold_columns",
    )(after, in_hbm(weights))


def project_kernel(per_group, *refs):
    blocks, (w_ref, stream_ref, keep_ref, give_ref, lhs_ref, sum_ref) = refs[:4], refs[4:]
    page_pos, blk_pos = lax.axis_index("page"), lax.axis_index("blk")
    height = blocks[0].shape[0]
    group = w_ref.shape[2]
    width = stream_ref.shape[2]
    for k, block in enumerate(blocks):
        start = pl.multiple_of((page_pos ^ k) * height, height)
        lhs_ref[pl.ds(start, height), :] = block[...]
    product = jnp.dot(lhs_ref[...], w_ref[0], preferred_element_type=jnp.float32)
    sum_ref[...] = product.reshape(sum_ref.shape)
    for part in range(per_group):

        @pl.when(blk_pos == page_pos * per_group + part)
        def _(part=part):
            stream = flat_rows(stream_ref[...]).astype(jnp.float32)
            at = (slice(None), slice(None), slice(part * width, (part + 1) * width))
            sum_ref[at] = sum_ref[at] + stream.reshape(sum_ref.shape[:2] + (width,))

    core = blk_pos % 2
    for chip in range(4):
        keep_ref[chip] = sum_ref[2 * chip + core]
        give_ref[chip] = sum_ref[2 * chip + 1 - core].astype(give_ref.dtype)


def project(blocks, w_out, stream_in, group):
    height, depth = blocks[0].shape
    rows = 4 * height
    vmem = pl.BlockSpec(memory_space=pltpu.VMEM)
    part = (4, rows // 8, group)
    return pl.pallas_call(
        functools.partial(project_kernel, group // stream_in.shape[2]),
        in_specs=[vmem] * 6,
        out_specs=[vmem] * 2,
        out_shape=[
            jax.ShapeDtypeStruct(part, jnp.float32),
            jax.ShapeDtypeStruct(part, jnp.bfloat16),
        ],
        scratch_shapes=[
            pltpu.VMEM((rows, depth), jnp.bfloat16),
            pltpu.VMEM((8, rows // 8, group), jnp.float32),
        ],
        compiler_params=pltpu.CompilerParams(vmem_limit_bytes=VMEM_LIMIT),
        name="project_attention",
    )(*blocks, w_out, stream_in)


def pair_kernel(keep_ref, got_ref, own_ref, *out_refs):
    chip = lax.axis_index("blk") // 2
    own_ref[...] = keep_ref[chip] + got_ref[chip].astype(jnp.float32)
    for k, out_ref in enumerate(out_refs, 1):
        total = keep_ref[chip ^ k] + got_ref[chip ^ k].astype(jnp.float32)
        out_ref[...] = total.astype(out_ref.dtype)


def pair_pieces(keep, got):
    vmem = pl.BlockSpec(memory_space=pltpu.VMEM)
    shape = keep.shape[1:]
    return pl.pallas_call(
        pair_kernel,
        in_specs=[vmem] * 2,
        out_specs=[vmem] * 4,
        out_shape=[jax.ShapeDtypeStruct(shape, jnp.float32)]
        + [jax.ShapeDtypeStruct(shape, jnp.bfloat16)] * 3,
        compiler_params=pltpu.CompilerParams(vmem_limit_bytes=VMEM_LIMIT),
        name="pair_pieces",
    )(keep, got)


def as_row(ref):
    return ref[...].astype(jnp.float32).reshape(1, ref.shape[0])


def own_part(row, width):
    page_pos = lax.axis_index("page")
    parts = [row[:, p * width : (p + 1) * width] for p in range(row.shape[1] // width)]
    return sum(jnp.where(page_pos == p, part, 0.0) for p, part in enumerate(parts))


def residual_kernel(own_ref, c_ref, b_ref, a_ref, bias_ref, score_ref, out_ref):
    group, piece = own_ref.shape[1], score_ref.shape[0]
    bias = own_part(as_row(bias_ref), group)
    total = own_ref[...] + bias
    for ref in (a_ref, b_ref, c_ref):
        total = total + ref[...].astype(jnp.float32)
    out_ref[:, :group] = total.astype(out_ref.dtype)
    out_ref[:, group : group + piece] = jnp.broadcast_to(
        as_row(score_ref), (own_ref.shape[0], piece)
    ).astype(out_ref.dtype)


def residual_rows(own, arrived, b_out, w_score):
    vmem = pl.BlockSpec(memory_space=pltpu.VMEM)
    return pl.pallas_call(
        residual_kernel,
        in_specs=[vmem] * 6,
        out_specs=vmem,
        out_shape=pltpu.VMEM((own.shape[0], own.shape[1] + 256), jnp.bfloat16),
        compiler_params=pltpu.CompilerParams(vmem_limit_bytes=VMEM_LIMIT),
        name="residual_rows",
    )(own, *arrived, b_out, w_score)


def split2(value):
    high = value.astype(jnp.bfloat16)
    return high, (value - high.astype(jnp.float32)).astype(jnp.bfloat16)


def whole2(high, low):
    return high.astype(jnp.float32) + low.astype(jnp.float32)


def up_first_kernel(*refs):
    blocks, refs = refs[:8], refs[8:]
    gain_ref, bias_ref, down_ref, far_ref, near_ref = refs[:5]
    out_refs, weight_ref, refs = refs[5:10], refs[10], refs[11:]
    lhs_ref, residual_ref, stats_ref, mean_ref, square_ref, base_ref, weights_ref = refs
    blk_pos = lax.axis_index("blk")
    core, chip = blk_pos % 2, blk_pos // 2
    height, group = blocks[0].shape[0], lhs_ref.shape[1]
    rows, piece = 8 * height, group // 8
    gain = as_row(gain_ref)
    places = []
    for i, block in enumerate(blocks):
        from_core = core if i < 4 else 1 - core
        owner = 2 * (chip ^ (i % 4)) + from_core
        places.append(pl.ds(pl.multiple_of(owner * height, height), height))
        weights_ref[pl.ds(owner, 1), :] = block[0:1, group:].astype(jnp.float32)
    weights = [weights_ref[b : b + 1, :piece] for b in range(8)]
    weight_ref[...] = jnp.concatenate(weights, axis=1)
    own_weights = [jnp.where(blk_pos == b, weight, 0.0) for b, weight in enumerate(weights)]
    score_row = jnp.concatenate(own_weights, axis=1)
    own_weight = sum(own_weights)
    fixed = jnp.sum(as_row(down_ref) * own_weight, axis=1, keepdims=True)
    for block, at in zip(blocks, places):
        residual = block[:, :group].astype(jnp.float32)
        mean = jnp.sum(residual, axis=1, keepdims=True) * (1.0 / group)
        centred = residual - mean
        square = jnp.sum(centred * centred, axis=1, keepdims=True)
        base = jnp.sum(residual * score_row, axis=1, keepdims=True) + fixed
        residual_ref[at, :] = block[:, :group]
        lhs_ref[at, :] = (centred * gain).astype(lhs_ref.dtype)
        mean_ref[at, :] = jnp.broadcast_to(mean, (height, rows))
        square_ref[at, :] = jnp.broadcast_to(square, (height, rows))
        base_ref[at, :] = jnp.broadcast_to(base, (height, rows))
    row = lax.broadcasted_iota(jnp.int32, (lhs_ref.shape[0] - rows, group), 0)
    bias = as_row(bias_ref)
    lhs_ref[rows:, :] = jnp.where(
        row == 0, gain, jnp.where(row == 1, bias, 0.0)
    ).astype(lhs_ref.dtype)
    pieces = []
    for ref in (mean_ref, square_ref, base_ref):
        pieces += split2(ref[...].T[0:1])
    stats_ref[...] = jnp.concatenate(pieces, axis=0)
    for i, (top_ref, bottom_ref) in enumerate((out_refs[0:2], out_refs[2:4])):
        part = up_product(lhs_ref, far_ref.at[i], stats_ref, rows)
        top_ref[...] = part[:TOP]
        bottom_ref[...] = part[TOP:]
    out_refs[4][...] = up_product(lhs_ref, near_ref.at[0], stats_ref, rows)


def up_product(lhs_ref, w_ref, stats_ref, rows):
    product = jnp.dot(lhs_ref[...], w_ref[...], preferred_element_type=jnp.float32)
    below = product[rows : rows + 8]
    padded = jnp.concatenate(
        [
            jnp.zeros((2, rows), jnp.float32),
            stats_ref[...].astype(jnp.float32),
        ],
        axis=0,
    )
    row = lax.broadcasted_iota(jnp.int32, (8, rows), 0)
    first = jnp.where(row < 2, below[:, :rows], padded)
    below = jnp.concatenate([first, below[:, rows:]], axis=1)
    return jnp.concatenate([product[:rows], below], axis=0).astype(jnp.bfloat16)


def up_first(blocks, ln_gain, ln_bias, b_down, held_up, near_up):
    height = blocks[0].shape[0]
    rows = 8 * height
    _, group, units = held_up.shape
    bf16, f32 = jnp.bfloat16, jnp.float32
    vmem = pl.BlockSpec(memory_space=pltpu.VMEM)
    return pl.pallas_call(
        up_first_kernel,
        in_specs=[vmem] * 13,
        out_specs=[vmem] * 9,
        out_shape=[pltpu.VMEM((TOP, units), bf16), pltpu.VMEM((rows - TOP + 8, units), bf16)] * 2
        + [
            pltpu.VMEM((rows + 8, units), bf16),
            pltpu.VMEM((1, group), f32),
            pltpu.VMEM((rows + 16, group), bf16),
            jax.ShapeDtypeStruct((rows, group), bf16),
            pltpu.VMEM((6, rows), bf16),
        ],
        scratch_shapes=[pltpu.VMEM((rows, rows), f32)] * 3
        + [
            pltpu.VMEM((8, blocks[0].shape[1] - group), f32),
        ],
        compiler_params=pltpu.CompilerParams(vmem_limit_bytes=VMEM_LIMIT),
        name="norm_and_up",
    )(
        *blocks,
        ln_gain,
        ln_bias,
        b_down,
        held_up,
        near_up,
    )


def up_own_kernel(lhs_ref, stats_ref, w_hbm, out_ref, w_ref, sems):
    copies = shard_copies(w_hbm, w_ref, sems, (0,), 1)
    copies[0].wait()
    out_ref[...] = up_product(lhs_ref, w_ref.at[0], stats_ref, stats_ref.shape[1])


def up_own(lhs, stats, w_up):
    group = lhs.shape[1]
    units = w_up.shape[1] // 4
    bf16 = jnp.bfloat16
    vmem = pl.BlockSpec(memory_space=pltpu.VMEM)
    return pl.pallas_call(
        up_own_kernel,
        in_specs=[vmem] * 2 + [pl.BlockSpec(memory_space=pl.ANY)],
        out_specs=vmem,
        out_shape=pltpu.VMEM((stats.shape[1] + 8, units), bf16),
        scratch_shapes=[pltpu.VMEM((1, group, units), bf16), pltpu.SemaphoreType.DMA((1,))],
        compiler_params=pltpu.CompilerParams(vmem_limit_bytes=VMEM_LIMIT),
        cost_estimate=FREE,
        name="up_own",
    )(lhs, stats, in_hbm(w_up))


def relay_kernel(a_ref, b_ref, out_ref):
    out_ref[...] = (a_ref[...].astype(jnp.float32) + b_ref[...].astype(jnp.float32)).astype(
        out_ref.dtype
    )


def relay_sum(part, got):
    vmem = pl.BlockSpec(memory_space=pltpu.VMEM)
    return pl.pallas_call(
        relay_kernel,
        in_specs=[vmem] * 2,
        out_specs=vmem,
        out_shape=pltpu.VMEM(part.shape, part.dtype),
        compiler_params=pltpu.CompilerParams(vmem_limit_bytes=VMEM_LIMIT),
        cost_estimate=FREE,
        name="relay_sum",
    )(part, got)


def image_kernel(first, score_ref, w_hbm, out_ref, w_ref, sems):
    count, units, group = w_ref.shape
    copies = start_copies(
        [
            pltpu.make_async_copy(
                w_hbm.at[pl.ds((first + i) * units, units)], w_ref.at[i], sems.at[i]
            )
            for i in range(count)
        ]
    )
    lanes = 128
    for i in range(count):
        copies[i].wait()
        for start in range(0, units, lanes):
            total = jnp.zeros((lanes, lanes), jnp.float32)
            for col in range(0, group, lanes):
                weights = w_ref[i, start : start + lanes, col : col + lanes].astype(jnp.float32)
                total = total + weights * score_ref[:, col : col + lanes]
            high, low = split2(jnp.sum(total.T, axis=0, keepdims=True))
            out_ref[i : i + 1, start : start + lanes] = high.astype(jnp.float32)
            out_ref[count + i : count + i + 1, start : start + lanes] = low.astype(jnp.float32)


def image_of(score_group, w_down, first, count):
    depth, group = w_down.shape
    tile = depth // 4
    vmem = pl.BlockSpec(memory_space=pltpu.VMEM)
    return pl.pallas_call(
        functools.partial(image_kernel, first),
        in_specs=[vmem, pl.BlockSpec(memory_space=pl.ANY)],
        out_specs=vmem,
        out_shape=pltpu.VMEM((2 * count, tile), jnp.float32),
        scratch_shapes=[
            pltpu.VMEM((count, tile, group), jnp.bfloat16),
            pltpu.SemaphoreType.DMA((count,)),
        ],
        compiler_params=pltpu.CompilerParams(vmem_limit_bytes=VMEM_LIMIT),
        cost_estimate=FREE,
        name="score_image",
    )(score_group, in_hbm(w_down))


def hidden_kernel(group, *refs):
    parts, (bias_ref, image_a_ref, image_b_ref, out_ref, base_ref) = refs[:5], refs[5:]
    rows, cut = parts[0].shape[0] - 8, parts[2].shape[0]
    f32 = jnp.float32
    tails = [part[part.shape[0] - 8 :, :].astype(f32) for part in (*parts[:2], *parts[3:])]
    stats = [
        [tail[2 + i : 3 + i, :rows] + tail[3 + i : 4 + i, :rows] for tail in tails]
        for i in (0, 2, 4)
    ]
    means, squares, bases = stats
    row_mean = pair_sum(means) * 0.25
    shifts = [mean - row_mean for mean in means]
    spread = sum(square + group * shift * shift for square, shift in zip(squares, shifts))
    inverse = lax.rsqrt(spread * (0.25 / group) + EPS)
    pad = jnp.zeros((rows - 6, rows), f32)
    columns = jnp.concatenate([inverse, *shifts, pair_sum(bases), pad], axis=0).T
    offset = sum(tail[1:2] for tail in tails) + own_part(as_row(bias_ref), bias_ref.shape[0] // 4)
    upper = parts[2][...].astype(f32)
    lower = parts[3][0 : rows - cut, :].astype(f32) + parts[4][0 : rows - cut, :].astype(f32)
    total = jnp.concatenate([upper, lower], axis=0)
    for part in parts[:2]:
        total = total + part[0:rows, :].astype(f32)
    for k, tail in enumerate(tails):
        total = total + columns[:, 1 + k : 2 + k] * tail[0:1]
    hidden = jnp.maximum(total * columns[:, 0:1] + offset, 0.0)
    image = [ref[at, :] for at in (slice(0, 2), slice(2, 4)) for ref in (image_a_ref, image_b_ref)]
    out_ref[...] = jnp.concatenate([hidden, *image], axis=0).astype(out_ref.dtype)
    base_ref[...] = columns[:, 5:6]


def own_hidden_units(parts, b_up, images, group):
    vmem = pl.BlockSpec(memory_space=pltpu.VMEM)
    height, units = parts[0].shape
    return pl.pallas_call(
        functools.partial(hidden_kernel, group),
        in_specs=[vmem] * 8,
        out_specs=[vmem] * 2,
        out_shape=[
            pltpu.VMEM((height, units), jnp.bfloat16),
            pltpu.VMEM((height - 8, 1), jnp.float32),
        ],
        compiler_params=pltpu.CompilerParams(vmem_limit_bytes=VMEM_LIMIT),
        name="hidden_units",
    )(*parts, b_up, *images)


def down_first_kernel(hidden_ref, w_hbm, sum_ref, held_ref, w_ref, sems, held_sems):
    rows = sum_ref.shape[0]
    copies = shard_copies(w_hbm, w_ref, sems, (0,), 0)
    held = shard_copies(w_hbm, held_ref, held_sems, (1, 2, 3), 0)
    copies[0].wait()
    sum_ref[...] = jnp.dot(
        hidden_ref[0:rows, :], w_ref[0], preferred_element_type=jnp.float32
    )
    for copy in held:
        copy.wait()


def down_first(hidden, w_down):
    rows, units = hidden.shape[0] - 8, hidden.shape[1]
    group = w_down.shape[1]
    vmem = pl.BlockSpec(memory_space=pltpu.VMEM)
    return pl.pallas_call(
        down_first_kernel,
        in_specs=[vmem, pl.BlockSpec(memory_space=pl.ANY)],
        out_specs=[vmem] * 2,
        out_shape=[
            pltpu.VMEM((rows, group), jnp.float32),
            pltpu.VMEM((3, units, group), jnp.bfloat16),
        ],
        scratch_shapes=[
            pltpu.VMEM((1, units, group), jnp.bfloat16),
            pltpu.SemaphoreType.DMA((1,)),
            pltpu.SemaphoreType.DMA((3,)),
        ],
        compiler_params=pltpu.CompilerParams(vmem_limit_bytes=VMEM_LIMIT),
        cost_estimate=FREE,
        name="down_own",
    )(hidden, in_hbm(w_down))


def down_middle_kernel(sum_ref, held_ref, near_ref, far_ref, out_ref):
    rows = sum_ref.shape[0]
    out_ref[...] = (
        sum_ref[...]
        + jnp.dot(near_ref[0:rows, :], held_ref[0], preferred_element_type=jnp.float32)
        + jnp.dot(far_ref[0:rows, :], held_ref[1], preferred_element_type=jnp.float32)
    )


def down_middle(summed, held, near, far):
    vmem = pl.BlockSpec(memory_space=pltpu.VMEM)
    return pl.pallas_call(
        down_middle_kernel,
        in_specs=[vmem] * 4,
        out_specs=vmem,
        out_shape=pltpu.VMEM(summed.shape, summed.dtype),
        compiler_params=pltpu.CompilerParams(vmem_limit_bytes=VMEM_LIMIT),
        cost_estimate=FREE,
        name="down_middle",
    )(summed, held, near, far)


def down_last_kernel(base_ref, sum_ref, held_ref, *refs):
    parts, (keep_ref, give_ref, score_ref, image_ref) = refs[:4], refs[4:]
    rows = sum_ref.shape[0]
    f32 = jnp.float32
    page_pos = lax.axis_index("page")
    core = lax.axis_index("blk") % 2
    piece = keep_ref.shape[2]
    product = sum_ref[...] + jnp.dot(
        parts[3][0:rows, :], held_ref[2], preferred_element_type=f32
    )
    tails = [part[rows:, :].astype(f32) for part in parts]
    image_ref[...] = pair_sum([tail[0:4] + tail[4:8] for tail in tails])
    by_owner = []
    for k, part in enumerate(parts):
        image = image_ref[pl.ds(page_pos ^ k, 1), :]
        by_owner.append(jnp.sum(part[0:rows, :].astype(f32) * image, axis=1, keepdims=True))
    score = base_ref[...] + pair_sum(by_owner)
    score_ref[...] = score
    pieces = split3(score)
    for chip in range(4):
        pair = [product[:, (2 * chip + c) * piece : (2 * chip + c + 1) * piece] for c in range(2)]
        keep_ref[chip] = jnp.where(core == 0, pair[0], pair[1])
        give_ref[chip, :, :piece] = jnp.where(core == 0, pair[1], pair[0]).astype(give_ref.dtype)
        give_ref[chip, :, piece:] = pieces


def down_last(base, summed, held, parts):
    rows, group = summed.shape
    units = parts[0].shape[1]
    vmem = pl.BlockSpec(memory_space=pltpu.VMEM)
    return pl.pallas_call(
        down_last_kernel,
        in_specs=[vmem] * 7,
        out_specs=[vmem] * 3,
        out_shape=[
            pltpu.VMEM((4, rows, group // 8), jnp.float32),
            pltpu.VMEM((4, rows, group // 8 + 3), jnp.bfloat16),
            pltpu.VMEM((rows, 1), jnp.float32),
        ],
        scratch_shapes=[pltpu.VMEM((4, units), jnp.float32)],
        compiler_params=pltpu.CompilerParams(vmem_limit_bytes=VMEM_LIMIT),
        name="down_last",
    )(base, summed, held, *parts)


def split3(value):
    return jnp.concatenate(pieces3(value), axis=1)


def whole3(pieces):
    return jnp.sum(pieces.astype(jnp.float32), axis=1, keepdims=True)


def pair_score_kernel(keep_ref, score_ref, got_ref, own_ref, both_ref, *out_refs):
    chip = lax.axis_index("blk") // 2
    piece = keep_ref.shape[2]
    score = whole3(split3(score_ref[...])) + whole3(got_ref[0, :, piece:])
    both_ref[...] = score
    pieces = split3(score)
    own_ref[...] = keep_ref[chip] + got_ref[chip, :, :piece].astype(jnp.float32)
    for k, out_ref in enumerate(out_refs, 1):
        total = keep_ref[chip ^ k] + got_ref[chip ^ k, :, :piece].astype(jnp.float32)
        out_ref[:, :piece] = total.astype(out_ref.dtype)
        out_ref[:, piece:] = pieces


def pair_scores(keep, score, got):
    vmem = pl.BlockSpec(memory_space=pltpu.VMEM)
    _, rows, piece = keep.shape
    return pl.pallas_call(
        pair_score_kernel,
        in_specs=[vmem] * 3,
        out_specs=[vmem] * 5,
        out_shape=[
            jax.ShapeDtypeStruct((rows, piece), jnp.float32),
            jax.ShapeDtypeStruct((rows, 1), jnp.float32),
        ]
        + [jax.ShapeDtypeStruct((rows, piece + 3), jnp.bfloat16)] * 3,
        compiler_params=pltpu.CompilerParams(vmem_limit_bytes=VMEM_LIMIT),
        name="pair_scores",
    )(keep, score, got)


def finish_kernel(own_ref, base_ref, score_ref, c_ref, b_ref, a_ref, out_ref, total_ref, held_ref):
    piece = own_ref.shape[1]
    total = own_ref[...] + base_ref[...]
    for ref in (a_ref, b_ref, c_ref):
        total = total + ref[:, :piece].astype(jnp.float32)
    out_ref[...] = total.astype(out_ref.dtype).reshape(out_ref.shape)
    scores = [whole3(ref[:, piece:]) for ref in (a_ref, b_ref, c_ref)]
    own_score = whole3(split3(score_ref[...]))
    score = (own_score + scores[0]) + (scores[1] + scores[2])
    new, samples = total_ref.shape
    held_ref[...] = jnp.broadcast_to(score, held_ref.shape)
    for n in range(new):
        total_ref[n : n + 1, :] = held_ref[pl.ds(n, samples, stride=new), :].T[0:1]


def finish(own, base, score, arrived, samples):
    vmem = pl.BlockSpec(memory_space=pltpu.VMEM)
    rows, piece = own.shape
    return pl.pallas_call(
        finish_kernel,
        in_specs=[vmem] * 6,
        out_specs=[vmem] * 2,
        out_shape=[
            jax.ShapeDtypeStruct((samples, rows // samples, piece), jnp.bfloat16),
            jax.ShapeDtypeStruct((rows // samples, samples), jnp.float32),
        ],
        scratch_shapes=[pltpu.VMEM((rows, 128), jnp.float32)],
        compiler_params=pltpu.CompilerParams(vmem_limit_bytes=VMEM_LIMIT),
        name="finish",
    )(own, base, score, *arrived)


def body(
    queries,
    prompt_kv,
    tail_kv,
    page_table,
    prompt_len,
    tail_len,
    sample_prompt,
    stream_in,
    w_out,
    b_out,
    ln_gain,
    ln_bias,
    w_up,
    b_up,
    w_down,
    b_down,
    w_score,
):
    bf16, f32 = jnp.bfloat16, jnp.float32
    samples, new_count, heads_dev, head_dim = queries.shape
    group = ln_gain.shape[0]
    blk_pos = lax.axis_index("blk")
    piece = b_down.shape[0]
    *packed, held_tail = prompt_partial(
        queries, prompt_kv, tail_kv, page_table, prompt_len, sample_prompt
    )
    sent = {k: send_xor(packed[k], "page", k) for k in (2, 3, 1)}
    shares = [packed[0], sent[1], sent[2], sent[3]]
    tail = tail_partial(queries, held_tail, tail_kv, tail_len)
    own_attention = merge_partials(shares + [tail], heads_dev)
    sent = {k: send_xor(own_attention, "page", k) for k in (2, 1, 3)}
    attention = [own_attention, sent[1], sent[2], sent[3]]
    held_out = hold_columns(own_attention, w_out, (0,), group)
    near_up = hold_columns(own_attention, w_up, (1,), w_up.shape[1] // 4)
    held_out, near_up = lax.optimization_barrier((held_out, near_up))
    keep, give = project(attention, held_out, stream_in, group)
    own, *pieces = pair_pieces(keep, send_xor(give, "blk", 1))
    units = w_up.shape[1] // 4
    arrived = [send_xor(pieces[k - 1], "blk", 2 * k) for k in (3, 2, 1)]
    held_up = hold_columns(own, w_up, (3, 2), units)
    own, held_up = lax.optimization_barrier((own, held_up))
    own_rows = residual_rows(own, arrived, b_out, w_score)
    same_core = gather_xor(own_rows, "blk", (2, 4, 6))
    blocks = same_core + [send_xor(block, "blk", 1) for block in same_core]
    top3, bottom3, top2, bottom2, part1, score_group, lhs, residual, stats = up_first(
        blocks, ln_gain, ln_bias, b_down, held_up, near_up
    )
    passing = send_xor(top3, "page", 1)
    far = send_xor(bottom3, "page", 3)
    middle = send_xor(bottom2, "page", 2)
    near = send_xor(part1, "page", 1)
    part0 = up_own(lhs, stats, w_up)
    image_a = image_of(score_group, w_down, 0, 2)
    passing, part0, image_a = lax.optimization_barrier((passing, part0, image_a))
    both, score_group = lax.optimization_barrier((relay_sum(top2, passing), score_group))
    images = image_a, image_of(score_group, w_down, 2, 2)
    parts = [part0, near, send_xor(both, "page", 2), middle, far]
    hidden, base_score = own_hidden_units(parts, b_up, images, group)
    summed, held = down_first(hidden, w_down)
    far, near, summed = lax.optimization_barrier(
        (send_xor(hidden, "page", 2), send_xor(hidden, "page", 1), summed)
    )
    summed = down_middle(summed, held, near, far)
    relayed = send_xor(far, "page", 1)
    keep, give, score = down_last(base_score, summed, held, [hidden, near, far, relayed])
    own_base = lax.dynamic_slice_in_dim(residual, blk_pos * piece, piece, 1).astype(
        f32
    ) + b_down.astype(f32)
    own, score, *pieces = pair_scores(keep, score, send_xor(give, "blk", 1))
    arrived = [send_xor(pieces[k - 1], "blk", 2 * k) for k in (3, 2, 1)]
    output, score = finish(own, own_base, score, arrived, samples)
    return (output, score.T)


def general_body(
    queries,
    prompt_kv,
    tail_kv,
    page_table,
    prompt_len,
    tail_len,
    sample_prompt,
    stream_in,
    w_out,
    b_out,
    ln_gain,
    ln_bias,
    w_up,
    b_up,
    w_down,
    b_down,
    w_score,
):
    samples, new_count, heads_dev, head_dim = queries.shape
    slots_dev, page_len = (prompt_kv.shape[0], prompt_kv.shape[1])
    own_count, tail_max = (tail_kv.shape[0], tail_kv.shape[1])
    prompts, pages_max = page_table.shape
    page_pos = lax.axis_index("page")
    blk_pos = lax.axis_index("blk")
    inv_sqrt = 1.0 / math.sqrt(head_dim)
    entries = page_table.reshape(-1)
    slot_ids = page_pos * slots_dev + jnp.arange(slots_dev, dtype=jnp.int32)
    matched = (entries[:, None] == slot_ids[None, :]).astype(jnp.int32)
    owner_index = jnp.sum(matched * jnp.arange(entries.shape[0], dtype=jnp.int32)[:, None], axis=0)
    slot_prompt = owner_index // pages_max
    slot_page = owner_index % pages_max
    prompt_pick = (slot_prompt[:, None] == jnp.arange(prompts, dtype=jnp.int32)[None, :]).astype(
        jnp.int32
    )
    slot_limit = jnp.sum(prompt_pick * prompt_len[None, :], axis=1)
    key_pos = slot_page[:, None] * page_len + jnp.arange(page_len, dtype=jnp.int32)[None, :]
    key_live = (key_pos < slot_limit[:, None]).reshape(-1)
    key_prompt = jnp.repeat(slot_prompt, page_len)
    prompt_visible = ((sample_prompt[:, None] == key_prompt[None, :]) & key_live[None, :])[
        :, None, None, :
    ]
    cache_rows = prompt_kv.reshape(slots_dev * page_len, heads_dev, 2 * head_dim)
    prompt_scores = (
        jnp.einsum(
            "snhd,khd->snhk",
            queries,
            cache_rows[:, :, :head_dim],
            preferred_element_type=jnp.float32,
        )
        * inv_sqrt
    )
    high_p, sum_p, weights_p = softmax_part(prompt_scores, prompt_visible)
    mixed_p = jnp.einsum(
        "snhk,khd->snhd", weights_p, cache_rows[:, :, head_dim:], preferred_element_type=jnp.float32
    )
    first_row = page_pos * own_count
    own_queries = lax.dynamic_slice_in_dim(queries, first_row, own_count, 0)
    own_lengths = lax.dynamic_slice_in_dim(tail_len, first_row, own_count, 0)
    tail_scores = (
        jnp.einsum(
            "snhd,sthd->snht",
            own_queries,
            tail_kv[..., :head_dim],
            preferred_element_type=jnp.float32,
        )
        * inv_sqrt
    )
    reach_pos = own_lengths[:, None] + jnp.arange(new_count, dtype=jnp.int32)[None, :]
    tail_visible = (
        jnp.arange(tail_max, dtype=jnp.int32)[None, None, None, :] <= reach_pos[:, :, None, None]
    )
    high_t, sum_t, weights_t = softmax_part(tail_scores, tail_visible)
    mixed_t = jnp.einsum(
        "snht,sthd->snhd", weights_t, tail_kv[..., head_dim:], preferred_element_type=jnp.float32
    )
    high_t = lax.dynamic_update_slice_in_dim(
        jnp.full(high_p.shape, NEGATIVE, jnp.float32), high_t, first_row, 0
    )
    sum_t = lax.dynamic_update_slice_in_dim(
        jnp.zeros(sum_p.shape, jnp.float32), sum_t, first_row, 0
    )
    mixed_t = lax.dynamic_update_slice_in_dim(
        jnp.zeros(mixed_p.shape, jnp.float32), mixed_t, first_row, 0
    )
    partial_value = join_partials((high_p, sum_p, mixed_p), (high_t, sum_t, mixed_t))
    merged = combined_all(partial_value, "page", join_partials)
    weight_sum, weighted = (merged[1], merged[2])
    attention = (
        (weighted / weight_sum[..., None])
        .astype(jnp.bfloat16)
        .reshape(samples * new_count, heads_dev * head_dim)
    )
    contrib = jnp.dot(attention, w_out, preferred_element_type=jnp.float32)
    slice_width = stream_in.shape[2]
    column = blk_pos * slice_width
    own_stream = stream_in.reshape(samples * new_count, slice_width).astype(jnp.float32)
    contrib = lax.dynamic_update_slice_in_dim(
        contrib, lax.dynamic_slice_in_dim(contrib, column, slice_width, 1) + own_stream, column, 1
    )
    summed = lax.psum(contrib, "blk")
    residual = (summed + b_out.astype(jnp.float32)).astype(jnp.bfloat16)
    residual_f = residual.astype(jnp.float32)
    row_mean = jnp.mean(residual_f, axis=-1, keepdims=True)
    centred = residual_f - row_mean
    inverse_std = lax.rsqrt(jnp.mean(centred * centred, axis=-1, keepdims=True) + 1e-05)
    feature_count = ln_gain.shape[0]
    first_col = page_pos * feature_count
    normed = (
        lax.dynamic_slice_in_dim(centred, first_col, feature_count, 1)
        * inverse_std
        * ln_gain.astype(jnp.float32)
        + ln_bias.astype(jnp.float32)
    ).astype(jnp.bfloat16)
    up_part = jnp.dot(normed, w_up, preferred_element_type=jnp.float32).astype(jnp.bfloat16)
    hidden_sum = lax.psum(up_part, "page").astype(jnp.float32)
    hidden = jnp.maximum(hidden_sum + b_up.astype(jnp.float32), 0.0).astype(jnp.bfloat16)
    projected = jnp.dot(hidden, w_down, preferred_element_type=jnp.float32)
    out_share = lax.psum_scatter(projected, "blk", scatter_dimension=1, tiled=True)
    piece_width = b_down.shape[0]
    out_column = first_col + blk_pos * piece_width
    output = (
        out_share
        + lax.dynamic_slice_in_dim(residual_f, out_column, piece_width, 1)
        + b_down.astype(jnp.float32)
    ).astype(jnp.bfloat16)
    score_part = jnp.sum(output.astype(jnp.float32) * w_score.astype(jnp.float32), axis=-1)
    row_score = lax.psum(score_part, ("page", "blk"))
    return (output.reshape(samples, new_count, piece_width), row_score.reshape(samples, new_count))


def solution(mesh):
    compute = body if (mesh.shape["page"], mesh.shape["blk"]) == (4, 8) else general_body

    placed = (
        P(None, None, "blk", None),
        P("page", None, "blk", None),
        P("page", None, "blk", None),
        P(),
        P(),
        P(),
        P(),
        P(None, None, "blk"),
        P("blk", None),
        P(),
        P("page"),
        P("page"),
        P("page", "blk"),
        P("blk"),
        P("blk", "page"),
        P(("page", "blk")),
        P(("page", "blk")),
    )
    return jax.shard_map(
        compute,
        mesh=mesh,
        in_specs=placed,
        out_specs=(P(None, None, ("page", "blk")), P()),
        check_vma=False,
    )
```

```python
import functools
import math

import jax
import jax.numpy as jnp
from jax import lax
from jax.experimental import pallas as pl
from jax.experimental.pallas import tpu as pltpu
from jax.sharding import PartitionSpec as P

NEGATIVE = -1e30
EPS = 1e-05
VMEM_LIMIT = 24 * 2**20
TOP = 64
FREE = pl.CostEstimate(flops=0, bytes_accessed=0, transcendentals=0)


def combined_all(value, axis, join):
    pieces = jax.tree.map(lambda part: lax.all_gather(part, axis), value)
    head = jax.tree.map(lambda part: part[0], pieces)
    tail = jax.tree.map(lambda part: part[1:], pieces)
    subtotal, _ = lax.scan(lambda subtotal, share: (join(subtotal, share), None), head, tail)
    return subtotal


def join_partials(earlier, later):
    highest = jnp.maximum(earlier[0], later[0])
    left_scale = jnp.exp(earlier[0] - highest)
    right_scale = jnp.exp(later[0] - highest)
    return (
        highest,
        earlier[1] * left_scale + later[1] * right_scale,
        earlier[2] * left_scale[..., None] + later[2] * right_scale[..., None],
    )


def softmax_part(scores, visible):
    masked = jnp.where(visible, scores, NEGATIVE)
    highest = jnp.max(masked, axis=-1)
    weights = jnp.where(visible, jnp.exp(scores - highest[..., None]), 0.0)
    return (highest, jnp.sum(weights, axis=-1), weights.astype(jnp.bfloat16))


def send_xor(value, axis, distance):
    size = lax.axis_size(axis)
    return lax.ppermute(value, axis, [(i, i ^ distance) for i in range(size)])


def in_hbm(value):
    return pltpu.with_memory_space_constraint(value, pltpu.HBM)


def gather_xor(value, axis, distances):
    return [value] + [send_xor(value, axis, k) for k in distances]


def pair_sum(pieces):
    return (pieces[0] + pieces[1]) + (pieces[2] + pieces[3])


def start_copies(copies):
    for copy in copies:
        copy.start()
    return copies


def flat_rows(ref_value):
    shape = ref_value.shape
    return ref_value.reshape(math.prod(shape[:-1]), shape[-1])


def pieces3(value):
    high = value.astype(jnp.bfloat16)
    left = value - high.astype(jnp.float32)
    middle = left.astype(jnp.bfloat16)
    return high, middle, (left - middle.astype(jnp.float32)).astype(jnp.bfloat16)


def prompt_kernel(scale, table_hbm, len_hbm, prompt_hbm, q_hbm, kv_hbm, tail_hbm, tail_len_hbm, *refs):
    outs, (held_ref, own_q_ref, own_len_ref), refs = refs[:4], refs[4:7], refs[7:]
    table_ref, len_ref, prompt_ref, q_ref, kv_ref, where_ref, count_ref, place_ref = refs[:8]
    query_ref, rows_ref, score_ref, best_ref, norm_ref, mixed_ref, back_ref, sent_ref, tail_len_ref, sems = refs[8:]
    copies = start_copies(
        [
            pltpu.make_async_copy(source, target, sems.at[i])
            for i, (source, target) in enumerate(
                (
                    (table_hbm, table_ref),
                    (len_hbm, len_ref),
                    (prompt_hbm, prompt_ref),
                    (q_hbm, q_ref),
                    (kv_hbm, kv_ref),
                    (tail_hbm.at[pl.ds(0, held_ref.shape[0])], held_ref),
                    (tail_len_hbm, tail_len_ref),
                )
            )
        ]
    )
    prompts, pages_max = table_ref.shape
    slots, page_len, heads, _ = kv_ref.shape
    samples, new = q_ref.shape[:2]
    dim = q_ref.shape[3]
    lines = outs[0].shape[0] - 8
    small = new * heads
    block = samples // prompts * small
    bf16, f32 = jnp.bfloat16, jnp.float32
    page_pos = lax.axis_index("page")
    first = page_pos * slots
    best_ref[...] = jnp.full(best_ref.shape, NEGATIVE, f32)
    norm_ref[...] = jnp.zeros(norm_ref.shape, f32)
    mixed_ref[...] = jnp.zeros(mixed_ref.shape, f32)
    for copy in copies[:3]:
        copy.wait()
    for p in range(prompts):
        count_ref[p] = p * (samples // prompts)
        for g in range(pages_max):
            slot = table_ref[p, g] - first
            here = jnp.logical_and(slot >= 0, slot < slots)
            where_ref[jnp.where(here, slot, slots)] = p * pages_max + g
    copies[3].wait()
    query_ref[...] = flat_rows(q_ref[...]).astype(f32)
    for s in range(samples):
        prompt = prompt_ref[s]
        place = count_ref[prompt]
        count_ref[prompt] = place + 1
        place_ref[s] = place
        to = pl.ds(pl.multiple_of(place * small, small), small)
        back_ref[to, :] = query_ref[s * small : (s + 1) * small, :]
    rows_ref[...] = back_ref[...].astype(bf16)
    width = page_len * heads
    row = lax.broadcasted_iota(jnp.int32, (block, width), 0)
    col = lax.broadcasted_iota(jnp.int32, (block, width), 1)
    position = jnp.where(row % heads == col % heads, col, page_len * heads * pages_max)
    copies[4].wait()
    cache = flat_rows(kv_ref[...])
    at = []
    for j in range(slots):
        entry = where_ref[j]
        prompt = entry // pages_max
        left = (len_ref[prompt] - (entry % pages_max) * page_len) * heads
        at.append(pl.ds(pl.multiple_of(prompt * block, block), block))
        scores = lax.dot_general(
            rows_ref[at[j], :],
            cache[j * width : (j + 1) * width, :dim],
            (((1,), (1,)), ((), ())),
            preferred_element_type=f32,
        )
        scores = jnp.where(position < jnp.minimum(left, width), scores, NEGATIVE)
        score_ref[j] = scores
        best = best_ref[at[j], :]
        for start in range(0, width, dim):
            best = jnp.maximum(best, scores[:, start : start + dim])
        best_ref[at[j], :] = best
    best = jnp.max(best_ref[...], axis=1, keepdims=True)
    best_ref[...] = jnp.broadcast_to(best, best_ref.shape)
    for j in range(slots):
        best = best_ref[at[j], :]
        best = jnp.concatenate([best] * (width // dim), axis=1)
        weights = jnp.exp2((score_ref[j] - best) * scale)
        norm = norm_ref[at[j], :]
        for start in range(0, width, dim):
            norm = norm + weights[:, start : start + dim]
        norm_ref[at[j], :] = norm
        mixed_ref[at[j], :] += jnp.dot(
            weights.astype(bf16),
            cache[j * width : (j + 1) * width, dim:],
            preferred_element_type=f32,
        )
    norm = jnp.sum(norm_ref[...], axis=1, keepdims=True)
    lane = lax.broadcasted_iota(jnp.int32, norm_ref.shape, 1)
    norm_ref[...] = jnp.where(lane == 0, best_ref[...], norm)
    for k, out_ref in enumerate(outs):
        for i in range(lines // small):
            place = place_ref[(page_pos ^ k) * (lines // small) + i]
            source = pl.ds(pl.multiple_of(place * small, small), small)
            to = slice(i * small, (i + 1) * small)
            if k == 0:
                out_ref[to, :] = mixed_ref[source, :]
            else:
                sent_ref[to, :] = mixed_ref[source, :]
            back_ref[to, :] = norm_ref[source, :]
        both = back_ref[0:lines, :].T[0:2]
        if k == 0:
            out_ref[lines : lines + 2, :] = both
        else:
            pad = jnp.zeros((2, dim), bf16)
            below = [*pieces3(both[0:1]), *pieces3(both[1:2]), pad]
            out_ref[0:lines, :] = sent_ref[...].astype(bf16)
            out_ref[lines : lines + 8, :] = jnp.concatenate(below, axis=0)
    copies[6].wait()
    own = own_len_ref.shape[0]
    for i in range(own):
        own_q_ref[i] = q_ref[page_pos * own + i]
        own_len_ref[i] = jnp.full(own_len_ref.shape[1:], tail_len_ref[page_pos * own + i])
    copies[5].wait()


def prompt_partial(queries, prompt_kv, tail_kv, page_table, prompt_len, sample_prompt, tail_len):
    samples, new, heads, dim = queries.shape
    slots, page_len = prompt_kv.shape[:2]
    total = samples * new * heads
    block = total // page_table.shape[0]
    lines = total // 4
    own = tail_kv.shape[0]
    anywhere = pl.BlockSpec(memory_space=pl.ANY)
    vmem = pl.BlockSpec(memory_space=pltpu.VMEM)
    wide = pltpu.VMEM((total, dim), jnp.float32)
    return pl.pallas_call(
        functools.partial(prompt_kernel, math.log2(math.e) / math.sqrt(dim)),
        in_specs=[anywhere] * 7,
        out_specs=[vmem] * 7,
        out_shape=[pltpu.VMEM((lines + 8, dim), jnp.float32)]
        + [pltpu.VMEM((lines + 8, dim), jnp.bfloat16)] * 3
        + [
            pltpu.VMEM((own * 1 // 2, *tail_kv.shape[1:]), tail_kv.dtype),
            pltpu.VMEM((own, new, heads, dim), queries.dtype),
            pltpu.VMEM((own, new * heads, dim), jnp.int32),
        ],
        scratch_shapes=[
            pltpu.SMEM(page_table.shape, jnp.int32),
            pltpu.SMEM(prompt_len.shape, jnp.int32),
            pltpu.SMEM(sample_prompt.shape, jnp.int32),
            pltpu.VMEM(queries.shape, queries.dtype),
            pltpu.VMEM(prompt_kv.shape, prompt_kv.dtype),
            pltpu.SMEM((slots + 1,), jnp.int32),
            pltpu.SMEM(prompt_len.shape, jnp.int32),
            pltpu.SMEM(sample_prompt.shape, jnp.int32),
            wide,
            pltpu.VMEM((total, dim), jnp.bfloat16),
            pltpu.VMEM((slots, block, page_len * heads), jnp.float32),
            wide,
            wide,
            wide,
            wide,
            pltpu.VMEM((lines, dim), jnp.float32),
            pltpu.SMEM(tail_len.shape, jnp.int32),
            pltpu.SemaphoreType.DMA((7,)),
        ],
        compiler_params=pltpu.CompilerParams(vmem_limit_bytes=VMEM_LIMIT),
        name="prompt_attention",
    )(
        *map(
            in_hbm,
            (page_table, prompt_len, sample_prompt, queries, prompt_kv, tail_kv, tail_len),
        )
    )


def tail_kernel(scale, q_ref, len_ref, held_ref, kv_hbm, out_ref, kv_ref, column_ref, sem):
    held, length, heads, _ = held_ref.shape
    own, new, _, dim = q_ref.shape
    lines, half = new * heads, length * heads // 2
    bf16, f32 = jnp.bfloat16, jnp.float32
    copy = pltpu.make_async_copy(kv_hbm.at[pl.ds(held, own - held)], kv_ref, sem)
    copy.start()
    row = lax.broadcasted_iota(jnp.int32, (2 * lines, half), 0)
    col = lax.broadcasted_iota(jnp.int32, (2 * lines, half), 1) + (row // lines) * half
    line = row % lines
    same_head = line % heads == col % heads
    ahead = jnp.where(same_head, col // heads - line // heads, length + new)
    lane = lax.broadcasted_iota(jnp.int32, (lines, dim), 1)
    for part in (range(0, own // 2), range(own // 2, own)):
        if part.stop > held:
            copy.wait()
        scores, values = [], []
        for i in part:
            cache = flat_rows(held_ref[i] if i < held else kv_ref[i - held])
            keys = jnp.concatenate([cache[:half, :dim], cache[half:, :dim]], axis=1)
            values.append(jnp.concatenate([cache[:half, dim:], cache[half:, dim:]], axis=1))
            query = flat_rows(q_ref[i])
            blank = jnp.zeros_like(query)
            query = jnp.concatenate(
                [
                    jnp.concatenate([query, blank], axis=1),
                    jnp.concatenate([blank, query], axis=1),
                ],
                axis=0,
            )
            score = lax.dot_general(
                query, keys, (((1,), (1,)), ((), ())), preferred_element_type=f32
            )
            limit = jnp.concatenate([len_ref[i]] * 2, axis=0)
            limit = jnp.concatenate([limit] * (half // dim), axis=1)
            scores.append(jnp.where(ahead <= limit, score, NEGATIVE))
        bests = [jnp.max(score, axis=1, keepdims=True) for score in scores]
        bests = [jnp.maximum(best[:lines], best[lines:]) for best in bests]
        weights = [
            jnp.exp2((score - jnp.concatenate([best, best], axis=0)) * scale)
            for score, best in zip(scores, bests)
        ]
        norms = [jnp.sum(weight, axis=1, keepdims=True) for weight in weights]
        for i, weight, value, best, norm in zip(part, weights, values, bests, norms):
            mixed = jnp.dot(weight.astype(bf16), value, preferred_element_type=f32)
            at = pl.ds(i * lines, lines)
            out_ref[at, :] = mixed[:lines, :dim] + mixed[lines:, dim:]
            column_ref[at, :] = jnp.where(lane == 0, best, norm[:lines] + norm[lines:])
    total = out_ref.shape[0] - 8
    out_ref[total : total + 2, :] = column_ref[...].T[0:2]


def tail_partial(own_queries, own_lengths, held_tail, tail_kv):
    own, new, heads, dim = own_queries.shape
    lines = own * new * heads
    left = (own - held_tail.shape[0], *tail_kv.shape[1:])
    vmem = pl.BlockSpec(memory_space=pltpu.VMEM)
    return pl.pallas_call(
        functools.partial(tail_kernel, math.log2(math.e) / math.sqrt(dim)),
        in_specs=[vmem] * 3 + [pl.BlockSpec(memory_space=pl.ANY)],
        out_specs=vmem,
        out_shape=pltpu.VMEM((lines + 8, dim), jnp.float32),
        scratch_shapes=[pltpu.VMEM(left, tail_kv.dtype)]
        + [pltpu.VMEM((lines, dim), jnp.float32), pltpu.SemaphoreType.DMA],
        compiler_params=pltpu.CompilerParams(vmem_limit_bytes=VMEM_LIMIT),
        cost_estimate=FREE,
        name="tail_attention",
    )(own_queries, own_lengths, held_tail, in_hbm(tail_kv))


def merge_kernel(scale, *refs):
    parts, out_ref, held_ref = refs[:-2], refs[-2], refs[-1]
    lines, dim = held_ref.shape
    heads = out_ref.shape[1] // dim
    bests, norms = [], []
    for part in parts:
        below = part[lines : lines + 8, :].astype(jnp.float32)
        if part.dtype == jnp.float32:
            bests.append(below[0:1])
            norms.append(below[1:2])
        else:
            bests.append((below[0:1] + below[1:2]) + below[2:3])
            norms.append((below[3:4] + below[4:5]) + below[5:6])
    best = functools.reduce(jnp.maximum, bests)
    scales = [jnp.exp2((one - best) * scale) for one in bests]
    norm = sum(factor * own_norm for factor, own_norm in zip(scales, norms))
    total = jnp.zeros((lines, dim), jnp.float32)
    for factor, part in zip(scales, parts):
        share = jnp.broadcast_to(factor / norm, (lines, lines)).T
        total = total + share * part[0:lines, :].astype(jnp.float32)
    held_ref[...] = total
    for h in range(heads):
        out_ref[:, h * dim : (h + 1) * dim] = held_ref[
            pl.ds(h, lines // heads, stride=heads), :
        ].astype(out_ref.dtype)


def merge_partials(parts, heads):
    lines, dim = parts[0].shape[0] - 8, parts[0].shape[1]
    vmem = pl.BlockSpec(memory_space=pltpu.VMEM)
    return pl.pallas_call(
        functools.partial(merge_kernel, math.log2(math.e) / math.sqrt(dim)),
        in_specs=[vmem] * len(parts),
        out_specs=vmem,
        out_shape=jax.ShapeDtypeStruct((lines // heads, heads * dim), jnp.bfloat16),
        scratch_shapes=[pltpu.VMEM((lines, dim), jnp.float32)],
        compiler_params=pltpu.CompilerParams(vmem_limit_bytes=VMEM_LIMIT),
        name="merge_partials",
    )(*parts)


def shard_copies(w_hbm, w_ref, sems, shards, axis):
    page_pos = lax.axis_index("page")
    units = w_ref.shape[1 + axis]
    copies = []
    for i, k in enumerate(shards):
        at = pl.ds(pl.multiple_of((page_pos ^ k) * units, 128), units)
        source = w_hbm.at[:, at] if axis else w_hbm.at[at, :]
        copies.append(pltpu.make_async_copy(source, w_ref.at[i], sems.at[i]))
    return start_copies(copies)


def hold_kernel(plan, after_ref, *refs):
    weights, held, sems = refs[: len(plan)], refs[len(plan) : -1], refs[-1]
    copies = []
    for w_hbm, out_ref, (first, shards) in zip(weights, held, plan):
        own_sems = sems.at[pl.ds(first, len(shards))]
        copies += shard_copies(w_hbm, out_ref, own_sems, shards, 1)
    for copy in copies:
        copy.wait()


def hold_columns(after, wanted):
    plan, total = [], 0
    for _, shards, _ in wanted:
        plan.append((total, shards))
        total += len(shards)
    vmem = pl.BlockSpec(memory_space=pltpu.VMEM)
    return pl.pallas_call(
        functools.partial(hold_kernel, tuple(plan)),
        in_specs=[vmem] + [pl.BlockSpec(memory_space=pl.ANY)] * len(wanted),
        out_specs=[vmem] * len(wanted),
        out_shape=[
            pltpu.VMEM((len(shards), weight.shape[0], units), weight.dtype)
            for weight, shards, units in wanted
        ],
        scratch_shapes=[pltpu.SemaphoreType.DMA((total,))],
        compiler_params=pltpu.CompilerParams(vmem_limit_bytes=VMEM_LIMIT),
        cost_estimate=FREE,
        name="hold_columns",
    )(after, *[in_hbm(weight) for weight, _, _ in wanted])


def project_kernel(per_group, *refs):
    blocks, (w_ref, stream_ref, keep_ref, give_ref, lhs_ref, sum_ref) = refs[:4], refs[4:]
    page_pos, blk_pos = lax.axis_index("page"), lax.axis_index("blk")
    height = blocks[0].shape[0]
    group = w_ref.shape[2]
    width = stream_ref.shape[2]
    for k, block in enumerate(blocks):
        start = pl.multiple_of((page_pos ^ k) * height, height)
        lhs_ref[pl.ds(start, height), :] = block[...]
    product = jnp.dot(lhs_ref[...], w_ref[0], preferred_element_type=jnp.float32)
    sum_ref[...] = product.reshape(sum_ref.shape)
    for part in range(per_group):

        @pl.when(blk_pos == page_pos * per_group + part)
        def _(part=part):
            stream = flat_rows(stream_ref[...]).astype(jnp.float32)
            at = (slice(None), slice(None), slice(part * width, (part + 1) * width))
            sum_ref[at] = sum_ref[at] + stream.reshape(sum_ref.shape[:2] + (width,))

    core = blk_pos % 2
    for chip in range(4):
        keep_ref[chip] = sum_ref[2 * chip + core]
        give_ref[chip] = sum_ref[2 * chip + 1 - core].astype(give_ref.dtype)


def project(blocks, w_out, stream_in, group):
    height, depth = blocks[0].shape
    rows = 4 * height
    vmem = pl.BlockSpec(memory_space=pltpu.VMEM)
    part = (4, rows // 8, group)
    return pl.pallas_call(
        functools.partial(project_kernel, group // stream_in.shape[2]),
        in_specs=[vmem] * 6,
        out_specs=[vmem] * 2,
        out_shape=[
            jax.ShapeDtypeStruct(part, jnp.float32),
            jax.ShapeDtypeStruct(part, jnp.bfloat16),
        ],
        scratch_shapes=[
            pltpu.VMEM((rows, depth), jnp.bfloat16),
            pltpu.VMEM((8, rows // 8, group), jnp.float32),
        ],
        compiler_params=pltpu.CompilerParams(vmem_limit_bytes=VMEM_LIMIT),
        name="project_attention",
    )(*blocks, w_out, stream_in)


def pair_kernel(keep_ref, got_ref, own_ref, *out_refs):
    chip = lax.axis_index("blk") // 2
    own_ref[...] = keep_ref[chip] + got_ref[chip].astype(jnp.float32)
    for k, out_ref in enumerate(out_refs, 1):
        total = keep_ref[chip ^ k] + got_ref[chip ^ k].astype(jnp.float32)
        out_ref[...] = total.astype(out_ref.dtype)


def pair_pieces(keep, got):
    vmem = pl.BlockSpec(memory_space=pltpu.VMEM)
    shape = keep.shape[1:]
    return pl.pallas_call(
        pair_kernel,
        in_specs=[vmem] * 2,
        out_specs=[vmem] * 4,
        out_shape=[jax.ShapeDtypeStruct(shape, jnp.float32)]
        + [jax.ShapeDtypeStruct(shape, jnp.bfloat16)] * 3,
        compiler_params=pltpu.CompilerParams(vmem_limit_bytes=VMEM_LIMIT),
        name="pair_pieces",
    )(keep, got)


def as_row(ref):
    return ref[...].astype(jnp.float32).reshape(1, ref.shape[0])


def own_part(row, width):
    page_pos = lax.axis_index("page")
    parts = [row[:, p * width : (p + 1) * width] for p in range(row.shape[1] // width)]
    return sum(jnp.where(page_pos == p, part, 0.0) for p, part in enumerate(parts))


def residual_kernel(own_ref, c_ref, b_ref, a_ref, bias_ref, score_ref, out_ref):
    group, piece = own_ref.shape[1], score_ref.shape[0]
    bias = own_part(as_row(bias_ref), group)
    total = own_ref[...] + bias
    for ref in (a_ref, b_ref, c_ref):
        total = total + ref[...].astype(jnp.float32)
    out_ref[:, :group] = total.astype(out_ref.dtype)
    out_ref[:, group : group + piece] = jnp.broadcast_to(
        as_row(score_ref), (own_ref.shape[0], piece)
    ).astype(out_ref.dtype)


def residual_rows(own, arrived, b_out, w_score):
    vmem = pl.BlockSpec(memory_space=pltpu.VMEM)
    return pl.pallas_call(
        residual_kernel,
        in_specs=[vmem] * 6,
        out_specs=vmem,
        out_shape=pltpu.VMEM((own.shape[0], own.shape[1] + 256), jnp.bfloat16),
        compiler_params=pltpu.CompilerParams(vmem_limit_bytes=VMEM_LIMIT),
        name="residual_rows",
    )(own, *arrived, b_out, w_score)


def split2(value):
    high = value.astype(jnp.bfloat16)
    return high, (value - high.astype(jnp.float32)).astype(jnp.bfloat16)


def whole2(high, low):
    return high.astype(jnp.float32) + low.astype(jnp.float32)


def up_first_kernel(*refs):
    blocks, refs = refs[:8], refs[8:]
    gain_ref, bias_ref, down_ref, far_ref, near_ref = refs[:5]
    out_refs, weight_ref, refs = refs[5:10], refs[10], refs[11:]
    lhs_ref, residual_ref, stats_ref, column_ref, weights_ref = refs
    blk_pos = lax.axis_index("blk")
    core, chip = blk_pos % 2, blk_pos // 2
    height, group = blocks[0].shape[0], lhs_ref.shape[1]
    rows, piece = 8 * height, group // 8
    gain = as_row(gain_ref)
    places = []
    for i, block in enumerate(blocks):
        from_core = core if i < 4 else 1 - core
        owner = 2 * (chip ^ (i % 4)) + from_core
        places.append(pl.ds(pl.multiple_of(owner * height, height), height))
        weights_ref[pl.ds(owner, 1), :] = block[0:1, group:].astype(jnp.float32)
    weights = [weights_ref[b : b + 1, :piece] for b in range(8)]
    weight_ref[...] = jnp.concatenate(weights, axis=1)
    own_weights = [jnp.where(blk_pos == b, weight, 0.0) for b, weight in enumerate(weights)]
    score_row = jnp.concatenate(own_weights, axis=1)
    own_weight = sum(own_weights)
    fixed = jnp.sum(as_row(down_ref) * own_weight, axis=1, keepdims=True)
    lane = lax.broadcasted_iota(jnp.int32, (height, rows), 1)
    for block, at in zip(blocks, places):
        residual = block[:, :group].astype(jnp.float32)
        mean = jnp.sum(residual, axis=1, keepdims=True) * (1.0 / group)
        centred = residual - mean
        square = jnp.sum(centred * centred, axis=1, keepdims=True)
        base = jnp.sum(residual * score_row, axis=1, keepdims=True) + fixed
        residual_ref[at, :] = block[:, :group]
        lhs_ref[at, :] = (centred * gain).astype(lhs_ref.dtype)
        column_ref[at, :] = jnp.where(lane == 0, mean, jnp.where(lane == 1, square, base))
    row = lax.broadcasted_iota(jnp.int32, (lhs_ref.shape[0] - rows, group), 0)
    bias = as_row(bias_ref)
    lhs_ref[rows:, :] = jnp.where(
        row == 0, gain, jnp.where(row == 1, bias, 0.0)
    ).astype(lhs_ref.dtype)
    columns = column_ref[...].T
    pieces = []
    for i in range(3):
        pieces += split2(columns[i : i + 1])
    stats_ref[...] = jnp.concatenate(pieces, axis=0)
    for i, (top_ref, bottom_ref) in enumerate((out_refs[0:2], out_refs[2:4])):
        part = up_product(lhs_ref, far_ref.at[i], stats_ref, rows)
        top_ref[...] = part[:TOP]
        bottom_ref[...] = part[TOP:]
    out_refs[4][...] = up_product(lhs_ref, near_ref.at[0], stats_ref, rows)


def up_product(lhs_ref, w_ref, stats_ref, rows):
    product = jnp.dot(lhs_ref[...], w_ref[...], preferred_element_type=jnp.float32)
    below = product[rows : rows + 8]
    padded = jnp.concatenate(
        [
            jnp.zeros((2, rows), jnp.float32),
            stats_ref[...].astype(jnp.float32),
        ],
        axis=0,
    )
    row = lax.broadcasted_iota(jnp.int32, (8, rows), 0)
    first = jnp.where(row < 2, below[:, :rows], padded)
    below = jnp.concatenate([first, below[:, rows:]], axis=1)
    return jnp.concatenate([product[:rows], below], axis=0).astype(jnp.bfloat16)


def up_first(blocks, ln_gain, ln_bias, b_down, held_up, near_up):
    height = blocks[0].shape[0]
    rows = 8 * height
    _, group, units = held_up.shape
    bf16, f32 = jnp.bfloat16, jnp.float32
    vmem = pl.BlockSpec(memory_space=pltpu.VMEM)
    return pl.pallas_call(
        up_first_kernel,
        in_specs=[vmem] * 13,
        out_specs=[vmem] * 9,
        out_shape=[pltpu.VMEM((TOP, units), bf16), pltpu.VMEM((rows - TOP + 8, units), bf16)] * 2
        + [
            pltpu.VMEM((rows + 8, units), bf16),
            pltpu.VMEM((1, group), f32),
            pltpu.VMEM((rows + 16, group), bf16),
            jax.ShapeDtypeStruct((rows, group), bf16),
            pltpu.VMEM((6, rows), bf16),
        ],
        scratch_shapes=[pltpu.VMEM((rows, rows), f32)]
        + [
            pltpu.VMEM((8, blocks[0].shape[1] - group), f32),
        ],
        compiler_params=pltpu.CompilerParams(vmem_limit_bytes=VMEM_LIMIT),
        name="norm_and_up",
    )(
        *blocks,
        ln_gain,
        ln_bias,
        b_down,
        held_up,
        near_up,
    )


def up_own_kernel(lhs_ref, stats_ref, w_hbm, out_ref, w_ref, sems):
    copies = shard_copies(w_hbm, w_ref, sems, (0,), 1)
    copies[0].wait()
    out_ref[...] = up_product(lhs_ref, w_ref.at[0], stats_ref, stats_ref.shape[1])


def up_own(lhs, stats, w_up):
    group = lhs.shape[1]
    units = w_up.shape[1] // 4
    bf16 = jnp.bfloat16
    vmem = pl.BlockSpec(memory_space=pltpu.VMEM)
    return pl.pallas_call(
        up_own_kernel,
        in_specs=[vmem] * 2 + [pl.BlockSpec(memory_space=pl.ANY)],
        out_specs=vmem,
        out_shape=pltpu.VMEM((stats.shape[1] + 8, units), bf16),
        scratch_shapes=[pltpu.VMEM((1, group, units), bf16), pltpu.SemaphoreType.DMA((1,))],
        compiler_params=pltpu.CompilerParams(vmem_limit_bytes=VMEM_LIMIT),
        cost_estimate=FREE,
        name="up_own",
    )(lhs, stats, in_hbm(w_up))


def relay_kernel(a_ref, b_ref, out_ref):
    out_ref[...] = (a_ref[...].astype(jnp.float32) + b_ref[...].astype(jnp.float32)).astype(
        out_ref.dtype
    )


def relay_sum(part, got):
    vmem = pl.BlockSpec(memory_space=pltpu.VMEM)
    return pl.pallas_call(
        relay_kernel,
        in_specs=[vmem] * 2,
        out_specs=vmem,
        out_shape=pltpu.VMEM(part.shape, part.dtype),
        compiler_params=pltpu.CompilerParams(vmem_limit_bytes=VMEM_LIMIT),
        cost_estimate=FREE,
        name="relay_sum",
    )(part, got)


def image_kernel(first, score_ref, w_hbm, out_ref, w_ref, sems):
    count, units, group = w_ref.shape
    copies = start_copies(
        [
            pltpu.make_async_copy(
                w_hbm.at[pl.ds((first + i) * units, units)], w_ref.at[i], sems.at[i]
            )
            for i in range(count)
        ]
    )
    lanes = 128
    for i in range(count):
        copies[i].wait()
        for start in range(0, units, lanes):
            total = jnp.zeros((lanes, lanes), jnp.float32)
            for col in range(0, group, lanes):
                weights = w_ref[i, start : start + lanes, col : col + lanes].astype(jnp.float32)
                total = total + weights * score_ref[:, col : col + lanes]
            high, low = split2(jnp.sum(total.T, axis=0, keepdims=True))
            out_ref[i : i + 1, start : start + lanes] = high.astype(jnp.float32)
            out_ref[count + i : count + i + 1, start : start + lanes] = low.astype(jnp.float32)


def image_of(score_group, w_down, first, count):
    depth, group = w_down.shape
    tile = depth // 4
    vmem = pl.BlockSpec(memory_space=pltpu.VMEM)
    return pl.pallas_call(
        functools.partial(image_kernel, first),
        in_specs=[vmem, pl.BlockSpec(memory_space=pl.ANY)],
        out_specs=vmem,
        out_shape=pltpu.VMEM((2 * count, tile), jnp.float32),
        scratch_shapes=[
            pltpu.VMEM((count, tile, group), jnp.bfloat16),
            pltpu.SemaphoreType.DMA((count,)),
        ],
        compiler_params=pltpu.CompilerParams(vmem_limit_bytes=VMEM_LIMIT),
        cost_estimate=FREE,
        name="score_image",
    )(score_group, in_hbm(w_down))


def hidden_kernel(group, *refs):
    parts, (bias_ref, image_a_ref, image_b_ref, out_ref, base_ref) = refs[:5], refs[5:]
    rows, cut = parts[0].shape[0] - 8, parts[2].shape[0]
    f32 = jnp.float32
    tails = [part[part.shape[0] - 8 :, :].astype(f32) for part in (*parts[:2], *parts[3:])]
    stats = [
        [tail[2 + i : 3 + i, :rows] + tail[3 + i : 4 + i, :rows] for tail in tails]
        for i in (0, 2, 4)
    ]
    means, squares, bases = stats
    row_mean = pair_sum(means) * 0.25
    shifts = [mean - row_mean for mean in means]
    spread = sum(square + group * shift * shift for square, shift in zip(squares, shifts))
    inverse = lax.rsqrt(spread * (0.25 / group) + EPS)
    pad = jnp.zeros((rows - 6, rows), f32)
    columns = jnp.concatenate([inverse, *shifts, pair_sum(bases), pad], axis=0).T
    offset = sum(tail[1:2] for tail in tails) + own_part(as_row(bias_ref), bias_ref.shape[0] // 4)
    upper = parts[2][...].astype(f32)
    lower = parts[3][0 : rows - cut, :].astype(f32) + parts[4][0 : rows - cut, :].astype(f32)
    total = jnp.concatenate([upper, lower], axis=0)
    for part in parts[:2]:
        total = total + part[0:rows, :].astype(f32)
    for k, tail in enumerate(tails):
        total = total + columns[:, 1 + k : 2 + k] * tail[0:1]
    hidden = jnp.maximum(total * columns[:, 0:1] + offset, 0.0)
    image = [ref[at, :] for at in (slice(0, 2), slice(2, 4)) for ref in (image_a_ref, image_b_ref)]
    out_ref[...] = jnp.concatenate([hidden, *image], axis=0).astype(out_ref.dtype)
    base_ref[...] = columns[:, 5:6]


def own_hidden_units(parts, b_up, images, group):
    vmem = pl.BlockSpec(memory_space=pltpu.VMEM)
    height, units = parts[0].shape
    return pl.pallas_call(
        functools.partial(hidden_kernel, group),
        in_specs=[vmem] * 8,
        out_specs=[vmem] * 2,
        out_shape=[
            pltpu.VMEM((height, units), jnp.bfloat16),
            pltpu.VMEM((height - 8, 1), jnp.float32),
        ],
        compiler_params=pltpu.CompilerParams(vmem_limit_bytes=VMEM_LIMIT),
        name="hidden_units",
    )(*parts, b_up, *images)


def down_first_kernel(hidden_ref, w_hbm, sum_ref, held_ref, w_ref, sems, held_sems):
    rows = sum_ref.shape[0]
    copies = shard_copies(w_hbm, w_ref, sems, (0,), 0)
    held = shard_copies(w_hbm, held_ref, held_sems, (1, 2, 3), 0)
    copies[0].wait()
    sum_ref[...] = jnp.dot(
        hidden_ref[0:rows, :], w_ref[0], preferred_element_type=jnp.float32
    )
    for copy in held:
        copy.wait()


def down_first(hidden, w_down):
    rows, units = hidden.shape[0] - 8, hidden.shape[1]
    group = w_down.shape[1]
    vmem = pl.BlockSpec(memory_space=pltpu.VMEM)
    return pl.pallas_call(
        down_first_kernel,
        in_specs=[vmem, pl.BlockSpec(memory_space=pl.ANY)],
        out_specs=[vmem] * 2,
        out_shape=[
            pltpu.VMEM((rows, group), jnp.float32),
            pltpu.VMEM((3, units, group), jnp.bfloat16),
        ],
        scratch_shapes=[
            pltpu.VMEM((1, units, group), jnp.bfloat16),
            pltpu.SemaphoreType.DMA((1,)),
            pltpu.SemaphoreType.DMA((3,)),
        ],
        compiler_params=pltpu.CompilerParams(vmem_limit_bytes=VMEM_LIMIT),
        cost_estimate=FREE,
        name="down_own",
    )(hidden, in_hbm(w_down))


def down_middle_kernel(sum_ref, held_ref, near_ref, far_ref, out_ref):
    rows = sum_ref.shape[0]
    out_ref[...] = (
        sum_ref[...]
        + jnp.dot(near_ref[0:rows, :], held_ref[0], preferred_element_type=jnp.float32)
        + jnp.dot(far_ref[0:rows, :], held_ref[1], preferred_element_type=jnp.float32)
    )


def down_middle(summed, held, near, far):
    vmem = pl.BlockSpec(memory_space=pltpu.VMEM)
    return pl.pallas_call(
        down_middle_kernel,
        in_specs=[vmem] * 4,
        out_specs=vmem,
        out_shape=pltpu.VMEM(summed.shape, summed.dtype),
        compiler_params=pltpu.CompilerParams(vmem_limit_bytes=VMEM_LIMIT),
        cost_estimate=FREE,
        name="down_middle",
    )(summed, held, near, far)


def down_last_kernel(base_ref, sum_ref, held_ref, *refs):
    parts, (keep_ref, give_ref, score_ref, image_ref) = refs[:4], refs[4:]
    rows = sum_ref.shape[0]
    f32 = jnp.float32
    page_pos = lax.axis_index("page")
    core = lax.axis_index("blk") % 2
    piece = keep_ref.shape[2]
    product = sum_ref[...] + jnp.dot(
        parts[3][0:rows, :], held_ref[2], preferred_element_type=f32
    )
    tails = [part[rows:, :].astype(f32) for part in parts]
    image_ref[...] = pair_sum([tail[0:4] + tail[4:8] for tail in tails])
    by_owner = []
    for k, part in enumerate(parts):
        image = image_ref[pl.ds(page_pos ^ k, 1), :]
        by_owner.append(jnp.sum(part[0:rows, :].astype(f32) * image, axis=1, keepdims=True))
    score = base_ref[...] + pair_sum(by_owner)
    score_ref[...] = score
    pieces = split3(score)
    for chip in range(4):
        pair = [product[:, (2 * chip + c) * piece : (2 * chip + c + 1) * piece] for c in range(2)]
        keep_ref[chip] = jnp.where(core == 0, pair[0], pair[1])
        give_ref[chip, :, :piece] = jnp.where(core == 0, pair[1], pair[0]).astype(give_ref.dtype)
        give_ref[chip, :, piece:] = pieces


def down_last(base, summed, held, parts):
    rows, group = summed.shape
    units = parts[0].shape[1]
    vmem = pl.BlockSpec(memory_space=pltpu.VMEM)
    return pl.pallas_call(
        down_last_kernel,
        in_specs=[vmem] * 7,
        out_specs=[vmem] * 3,
        out_shape=[
            pltpu.VMEM((4, rows, group // 8), jnp.float32),
            pltpu.VMEM((4, rows, group // 8 + 3), jnp.bfloat16),
            pltpu.VMEM((rows, 1), jnp.float32),
        ],
        scratch_shapes=[pltpu.VMEM((4, units), jnp.float32)],
        compiler_params=pltpu.CompilerParams(vmem_limit_bytes=VMEM_LIMIT),
        name="down_last",
    )(base, summed, held, *parts)


def split3(value):
    return jnp.concatenate(pieces3(value), axis=1)


def whole3(pieces):
    return jnp.sum(pieces.astype(jnp.float32), axis=1, keepdims=True)


def pair_score_kernel(keep_ref, score_ref, got_ref, own_ref, both_ref, *out_refs):
    chip = lax.axis_index("blk") // 2
    piece = keep_ref.shape[2]
    score = whole3(split3(score_ref[...])) + whole3(got_ref[0, :, piece:])
    both_ref[...] = score
    pieces = split3(score)
    own_ref[...] = keep_ref[chip] + got_ref[chip, :, :piece].astype(jnp.float32)
    for k, out_ref in enumerate(out_refs, 1):
        total = keep_ref[chip ^ k] + got_ref[chip ^ k, :, :piece].astype(jnp.float32)
        out_ref[:, :piece] = total.astype(out_ref.dtype)
        out_ref[:, piece:] = pieces


def pair_scores(keep, score, got):
    vmem = pl.BlockSpec(memory_space=pltpu.VMEM)
    _, rows, piece = keep.shape
    return pl.pallas_call(
        pair_score_kernel,
        in_specs=[vmem] * 3,
        out_specs=[vmem] * 5,
        out_shape=[
            jax.ShapeDtypeStruct((rows, piece), jnp.float32),
            jax.ShapeDtypeStruct((rows, 1), jnp.float32),
        ]
        + [jax.ShapeDtypeStruct((rows, piece + 3), jnp.bfloat16)] * 3,
        compiler_params=pltpu.CompilerParams(vmem_limit_bytes=VMEM_LIMIT),
        name="pair_scores",
    )(keep, score, got)


def finish_kernel(own_ref, base_ref, score_ref, c_ref, b_ref, a_ref, out_ref, total_ref, held_ref):
    piece = own_ref.shape[1]
    total = own_ref[...] + base_ref[...]
    for ref in (a_ref, b_ref, c_ref):
        total = total + ref[:, :piece].astype(jnp.float32)
    out_ref[...] = total.astype(out_ref.dtype).reshape(out_ref.shape)
    scores = [whole3(ref[:, piece:]) for ref in (a_ref, b_ref, c_ref)]
    own_score = whole3(split3(score_ref[...]))
    score = (own_score + scores[0]) + (scores[1] + scores[2])
    new, samples = total_ref.shape
    held_ref[...] = jnp.broadcast_to(score, held_ref.shape)
    for n in range(new):
        total_ref[n : n + 1, :] = held_ref[pl.ds(n, samples, stride=new), :].T[0:1]


def finish(own, base, score, arrived, samples):
    vmem = pl.BlockSpec(memory_space=pltpu.VMEM)
    rows, piece = own.shape
    return pl.pallas_call(
        finish_kernel,
        in_specs=[vmem] * 6,
        out_specs=[vmem] * 2,
        out_shape=[
            jax.ShapeDtypeStruct((samples, rows // samples, piece), jnp.bfloat16),
            jax.ShapeDtypeStruct((rows // samples, samples), jnp.float32),
        ],
        scratch_shapes=[pltpu.VMEM((rows, 128), jnp.float32)],
        compiler_params=pltpu.CompilerParams(vmem_limit_bytes=VMEM_LIMIT),
        name="finish",
    )(own, base, score, *arrived)


def body(
    queries,
    prompt_kv,
    tail_kv,
    page_table,
    prompt_len,
    tail_len,
    sample_prompt,
    stream_in,
    w_out,
    b_out,
    ln_gain,
    ln_bias,
    w_up,
    b_up,
    w_down,
    b_down,
    w_score,
):
    bf16, f32 = jnp.bfloat16, jnp.float32
    samples, new_count, heads_dev, head_dim = queries.shape
    group = ln_gain.shape[0]
    blk_pos = lax.axis_index("blk")
    piece = b_down.shape[0]
    *packed, held_tail, own_queries, own_lengths = prompt_partial(
        queries, prompt_kv, tail_kv, page_table, prompt_len, sample_prompt, tail_len
    )
    sent = {k: send_xor(packed[k], "page", k) for k in (2, 3, 1)}
    shares = [packed[0], sent[1], sent[2], sent[3]]
    tail = tail_partial(own_queries, own_lengths, held_tail, tail_kv)
    own_attention = merge_partials(shares + [tail], heads_dev)
    sent = {k: send_xor(own_attention, "page", k) for k in (2, 1, 3)}
    attention = [own_attention, sent[1], sent[2], sent[3]]
    units = w_up.shape[1] // 4
    held_out, near_up = hold_columns(
        own_attention, ((w_out, (0,), group), (w_up, (1,), units))
    )
    keep, give = project(attention, held_out, stream_in, group)
    own, *pieces = pair_pieces(keep, send_xor(give, "blk", 1))
    arrived = [send_xor(pieces[k - 1], "blk", 2 * k) for k in (3, 2, 1)]
    (held_up,) = hold_columns(own, ((w_up, (3, 2), units),))
    own, held_up = lax.optimization_barrier((own, held_up))
    own_rows = residual_rows(own, arrived, b_out, w_score)
    same_core = gather_xor(own_rows, "blk", (2, 4, 6))
    blocks = same_core + [send_xor(block, "blk", 1) for block in same_core]
    top3, bottom3, top2, bottom2, part1, score_group, lhs, residual, stats = up_first(
        blocks, ln_gain, ln_bias, b_down, held_up, near_up
    )
    passing = send_xor(top3, "page", 1)
    far = send_xor(bottom3, "page", 3)
    middle = send_xor(bottom2, "page", 2)
    near = send_xor(part1, "page", 1)
    part0 = up_own(lhs, stats, w_up)
    image_a = image_of(score_group, w_down, 0, 2)
    passing, part0, image_a = lax.optimization_barrier((passing, part0, image_a))
    both, score_group = lax.optimization_barrier((relay_sum(top2, passing), score_group))
    images = image_a, image_of(score_group, w_down, 2, 2)
    parts = [part0, near, send_xor(both, "page", 2), middle, far]
    hidden, base_score = own_hidden_units(parts, b_up, images, group)
    summed, held = down_first(hidden, w_down)
    far, near, summed = lax.optimization_barrier(
        (send_xor(hidden, "page", 2), send_xor(hidden, "page", 1), summed)
    )
    summed = down_middle(summed, held, near, far)
    relayed = send_xor(far, "page", 1)
    keep, give, score = down_last(base_score, summed, held, [hidden, near, far, relayed])
    own_base = lax.dynamic_slice_in_dim(residual, blk_pos * piece, piece, 1).astype(
        f32
    ) + b_down.astype(f32)
    own, score, *pieces = pair_scores(keep, score, send_xor(give, "blk", 1))
    arrived = [send_xor(pieces[k - 1], "blk", 2 * k) for k in (3, 2, 1)]
    output, score = finish(own, own_base, score, arrived, samples)
    return (output, score.T)


def general_body(
    queries,
    prompt_kv,
    tail_kv,
    page_table,
    prompt_len,
    tail_len,
    sample_prompt,
    stream_in,
    w_out,
    b_out,
    ln_gain,
    ln_bias,
    w_up,
    b_up,
    w_down,
    b_down,
    w_score,
):
    samples, new_count, heads_dev, head_dim = queries.shape
    slots_dev, page_len = (prompt_kv.shape[0], prompt_kv.shape[1])
    own_count, tail_max = (tail_kv.shape[0], tail_kv.shape[1])
    prompts, pages_max = page_table.shape
    page_pos = lax.axis_index("page")
    blk_pos = lax.axis_index("blk")
    inv_sqrt = 1.0 / math.sqrt(head_dim)
    entries = page_table.reshape(-1)
    slot_ids = page_pos * slots_dev + jnp.arange(slots_dev, dtype=jnp.int32)
    matched = (entries[:, None] == slot_ids[None, :]).astype(jnp.int32)
    owner_index = jnp.sum(matched * jnp.arange(entries.shape[0], dtype=jnp.int32)[:, None], axis=0)
    slot_prompt = owner_index // pages_max
    slot_page = owner_index % pages_max
    prompt_pick = (slot_prompt[:, None] == jnp.arange(prompts, dtype=jnp.int32)[None, :]).astype(
        jnp.int32
    )
    slot_limit = jnp.sum(prompt_pick * prompt_len[None, :], axis=1)
    key_pos = slot_page[:, None] * page_len + jnp.arange(page_len, dtype=jnp.int32)[None, :]
    key_live = (key_pos < slot_limit[:, None]).reshape(-1)
    key_prompt = jnp.repeat(slot_prompt, page_len)
    prompt_visible = ((sample_prompt[:, None] == key_prompt[None, :]) & key_live[None, :])[
        :, None, None, :
    ]
    cache_rows = prompt_kv.reshape(slots_dev * page_len, heads_dev, 2 * head_dim)
    prompt_scores = (
        jnp.einsum(
            "snhd,khd->snhk",
            queries,
            cache_rows[:, :, :head_dim],
            preferred_element_type=jnp.float32,
        )
        * inv_sqrt
    )
    high_p, sum_p, weights_p = softmax_part(prompt_scores, prompt_visible)
    mixed_p = jnp.einsum(
        "snhk,khd->snhd", weights_p, cache_rows[:, :, head_dim:], preferred_element_type=jnp.float32
    )
    first_row = page_pos * own_count
    own_queries = lax.dynamic_slice_in_dim(queries, first_row, own_count, 0)
    own_lengths = lax.dynamic_slice_in_dim(tail_len, first_row, own_count, 0)
    tail_scores = (
        jnp.einsum(
            "snhd,sthd->snht",
            own_queries,
            tail_kv[..., :head_dim],
            preferred_element_type=jnp.float32,
        )
        * inv_sqrt
    )
    reach_pos = own_lengths[:, None] + jnp.arange(new_count, dtype=jnp.int32)[None, :]
    tail_visible = (
        jnp.arange(tail_max, dtype=jnp.int32)[None, None, None, :] <= reach_pos[:, :, None, None]
    )
    high_t, sum_t, weights_t = softmax_part(tail_scores, tail_visible)
    mixed_t = jnp.einsum(
        "snht,sthd->snhd", weights_t, tail_kv[..., head_dim:], preferred_element_type=jnp.float32
    )
    high_t = lax.dynamic_update_slice_in_dim(
        jnp.full(high_p.shape, NEGATIVE, jnp.float32), high_t, first_row, 0
    )
    sum_t = lax.dynamic_update_slice_in_dim(
        jnp.zeros(sum_p.shape, jnp.float32), sum_t, first_row, 0
    )
    mixed_t = lax.dynamic_update_slice_in_dim(
        jnp.zeros(mixed_p.shape, jnp.float32), mixed_t, first_row, 0
    )
    partial_value = join_partials((high_p, sum_p, mixed_p), (high_t, sum_t, mixed_t))
    merged = combined_all(partial_value, "page", join_partials)
    weight_sum, weighted = (merged[1], merged[2])
    attention = (
        (weighted / weight_sum[..., None])
        .astype(jnp.bfloat16)
        .reshape(samples * new_count, heads_dev * head_dim)
    )
    contrib = jnp.dot(attention, w_out, preferred_element_type=jnp.float32)
    slice_width = stream_in.shape[2]
    column = blk_pos * slice_width
    own_stream = stream_in.reshape(samples * new_count, slice_width).astype(jnp.float32)
    contrib = lax.dynamic_update_slice_in_dim(
        contrib, lax.dynamic_slice_in_dim(contrib, column, slice_width, 1) + own_stream, column, 1
    )
    summed = lax.psum(contrib, "blk")
    residual = (summed + b_out.astype(jnp.float32)).astype(jnp.bfloat16)
    residual_f = residual.astype(jnp.float32)
    row_mean = jnp.mean(residual_f, axis=-1, keepdims=True)
    centred = residual_f - row_mean
    inverse_std = lax.rsqrt(jnp.mean(centred * centred, axis=-1, keepdims=True) + 1e-05)
    feature_count = ln_gain.shape[0]
    first_col = page_pos * feature_count
    normed = (
        lax.dynamic_slice_in_dim(centred, first_col, feature_count, 1)
        * inverse_std
        * ln_gain.astype(jnp.float32)
        + ln_bias.astype(jnp.float32)
    ).astype(jnp.bfloat16)
    up_part = jnp.dot(normed, w_up, preferred_element_type=jnp.float32).astype(jnp.bfloat16)
    hidden_sum = lax.psum(up_part, "page").astype(jnp.float32)
    hidden = jnp.maximum(hidden_sum + b_up.astype(jnp.float32), 0.0).astype(jnp.bfloat16)
    projected = jnp.dot(hidden, w_down, preferred_element_type=jnp.float32)
    out_share = lax.psum_scatter(projected, "blk", scatter_dimension=1, tiled=True)
    piece_width = b_down.shape[0]
    out_column = first_col + blk_pos * piece_width
    output = (
        out_share
        + lax.dynamic_slice_in_dim(residual_f, out_column, piece_width, 1)
        + b_down.astype(jnp.float32)
    ).astype(jnp.bfloat16)
    score_part = jnp.sum(output.astype(jnp.float32) * w_score.astype(jnp.float32), axis=-1)
    row_score = lax.psum(score_part, ("page", "blk"))
    return (output.reshape(samples, new_count, piece_width), row_score.reshape(samples, new_count))


def solution(mesh):
    compute = body if (mesh.shape["page"], mesh.shape["blk"]) == (4, 8) else general_body

    placed = (
        P(None, None, "blk", None),
        P("page", None, "blk", None),
        P("page", None, "blk", None),
        P(),
        P(),
        P(),
        P(),
        P(None, None, "blk"),
        P("blk", None),
        P(),
        P("page"),
        P("page"),
        P("page", "blk"),
        P("blk"),
        P("blk", "page"),
        P(("page", "blk")),
        P(("page", "blk")),
    )
    return jax.shard_map(
        compute,
        mesh=mesh,
        in_specs=placed,
        out_specs=(P(None, None, ("page", "blk")), P()),
        check_vma=False,
    )
```

```python
import functools
import math

import jax
import jax.numpy as jnp
from jax import lax
from jax.experimental import pallas as pl
from jax.experimental.pallas import tpu as pltpu
from jax.sharding import PartitionSpec as P

NEGATIVE = -1e30
EPS = 1e-05
VMEM_LIMIT = 24 * 2**20
TOP = 80
FREE = pl.CostEstimate(flops=0, bytes_accessed=0, transcendentals=0)


def combined_all(value, axis, join):
    pieces = jax.tree.map(lambda part: lax.all_gather(part, axis), value)
    head = jax.tree.map(lambda part: part[0], pieces)
    tail = jax.tree.map(lambda part: part[1:], pieces)
    subtotal, _ = lax.scan(lambda subtotal, share: (join(subtotal, share), None), head, tail)
    return subtotal


def join_partials(earlier, later):
    highest = jnp.maximum(earlier[0], later[0])
    left_scale = jnp.exp(earlier[0] - highest)
    right_scale = jnp.exp(later[0] - highest)
    return (
        highest,
        earlier[1] * left_scale + later[1] * right_scale,
        earlier[2] * left_scale[..., None] + later[2] * right_scale[..., None],
    )


def softmax_part(scores, visible):
    masked = jnp.where(visible, scores, NEGATIVE)
    highest = jnp.max(masked, axis=-1)
    weights = jnp.where(visible, jnp.exp(scores - highest[..., None]), 0.0)
    return (highest, jnp.sum(weights, axis=-1), weights.astype(jnp.bfloat16))


def send_xor(value, axis, distance):
    size = lax.axis_size(axis)
    return lax.ppermute(value, axis, [(i, i ^ distance) for i in range(size)])


def in_hbm(value):
    return pltpu.with_memory_space_constraint(value, pltpu.HBM)


def gather_xor(value, axis, distances):
    return [value] + [send_xor(value, axis, k) for k in distances]


def pair_sum(pieces):
    return (pieces[0] + pieces[1]) + (pieces[2] + pieces[3])


def start_copies(copies):
    for copy in copies:
        copy.start()
    return copies


def flat_rows(ref_value):
    shape = ref_value.shape
    return ref_value.reshape(math.prod(shape[:-1]), shape[-1])


def pieces3(value):
    high = value.astype(jnp.bfloat16)
    left = value - high.astype(jnp.float32)
    middle = left.astype(jnp.bfloat16)
    return high, middle, (left - middle.astype(jnp.float32)).astype(jnp.bfloat16)


def prompt_kernel(scale, table_hbm, len_hbm, prompt_hbm, q_hbm, kv_hbm, tail_hbm, tail_len_hbm, *refs):
    outs, (held_ref, own_q_ref, own_len_ref), refs = refs[:4], refs[4:7], refs[7:]
    table_ref, len_ref, prompt_ref, q_ref, kv_ref, where_ref, count_ref, place_ref = refs[:8]
    query_ref, rows_ref, score_ref, best_ref, norm_ref, mixed_ref, back_ref, sent_ref, tail_len_ref, sems = refs[8:]
    copies = start_copies(
        [
            pltpu.make_async_copy(source, target, sems.at[i])
            for i, (source, target) in enumerate(
                (
                    (table_hbm, table_ref),
                    (len_hbm, len_ref),
                    (prompt_hbm, prompt_ref),
                    (q_hbm, q_ref),
                    (kv_hbm, kv_ref),
                    (tail_hbm.at[pl.ds(0, held_ref.shape[0])], held_ref),
                    (tail_len_hbm, tail_len_ref),
                )
            )
        ]
    )
    prompts, pages_max = table_ref.shape
    slots, page_len, heads, _ = kv_ref.shape
    samples, new = q_ref.shape[:2]
    dim = q_ref.shape[3]
    lines = outs[0].shape[0] - 8
    small = new * heads
    block = samples // prompts * small
    bf16, f32 = jnp.bfloat16, jnp.float32
    page_pos = lax.axis_index("page")
    first = page_pos * slots
    best_ref[...] = jnp.full(best_ref.shape, NEGATIVE, f32)
    norm_ref[...] = jnp.zeros(norm_ref.shape, f32)
    mixed_ref[...] = jnp.zeros(mixed_ref.shape, f32)
    for copy in copies[:3]:
        copy.wait()
    for p in range(prompts):
        count_ref[p] = p * (samples // prompts)
        for g in range(pages_max):
            slot = table_ref[p, g] - first
            here = jnp.logical_and(slot >= 0, slot < slots)
            where_ref[jnp.where(here, slot, slots)] = p * pages_max + g
    copies[3].wait()
    query_ref[...] = flat_rows(q_ref[...]).astype(f32)
    for s in range(samples):
        prompt = prompt_ref[s]
        place = count_ref[prompt]
        count_ref[prompt] = place + 1
        place_ref[s] = place
        to = pl.ds(pl.multiple_of(place * small, small), small)
        back_ref[to, :] = query_ref[s * small : (s + 1) * small, :]
    rows_ref[...] = back_ref[...].astype(bf16)
    width = page_len * heads
    row = lax.broadcasted_iota(jnp.int32, (block, width), 0)
    col = lax.broadcasted_iota(jnp.int32, (block, width), 1)
    position = jnp.where(row % heads == col % heads, col, page_len * heads * pages_max)
    copies[4].wait()
    cache = flat_rows(kv_ref[...])
    at = []
    for j in range(slots):
        entry = where_ref[j]
        prompt = entry // pages_max
        left = (len_ref[prompt] - (entry % pages_max) * page_len) * heads
        at.append(pl.ds(pl.multiple_of(prompt * block, block), block))
        scores = lax.dot_general(
            rows_ref[at[j], :],
            cache[j * width : (j + 1) * width, :dim],
            (((1,), (1,)), ((), ())),
            preferred_element_type=f32,
        )
        scores = jnp.where(position < jnp.minimum(left, width), scores, NEGATIVE)
        score_ref[j] = scores
        best = best_ref[at[j], :]
        for start in range(0, width, dim):
            best = jnp.maximum(best, scores[:, start : start + dim])
        best_ref[at[j], :] = best
    best = jnp.max(best_ref[...], axis=1, keepdims=True)
    best_ref[...] = jnp.broadcast_to(best, best_ref.shape)
    for j in range(slots):
        best = best_ref[at[j], :]
        best = jnp.concatenate([best] * (width // dim), axis=1)
        weights = jnp.exp2((score_ref[j] - best) * scale)
        norm = norm_ref[at[j], :]
        for start in range(0, width, dim):
            norm = norm + weights[:, start : start + dim]
        norm_ref[at[j], :] = norm
        mixed_ref[at[j], :] += jnp.dot(
            weights.astype(bf16),
            cache[j * width : (j + 1) * width, dim:],
            preferred_element_type=f32,
        )
    norm = jnp.sum(norm_ref[...], axis=1, keepdims=True)
    lane = lax.broadcasted_iota(jnp.int32, norm_ref.shape, 1)
    norm_ref[...] = jnp.where(lane == 0, best_ref[...], norm)
    for k, out_ref in enumerate(outs):
        for i in range(lines // small):
            place = place_ref[(page_pos ^ k) * (lines // small) + i]
            source = pl.ds(pl.multiple_of(place * small, small), small)
            to = slice(i * small, (i + 1) * small)
            if k == 0:
                out_ref[to, :] = mixed_ref[source, :]
            else:
                sent_ref[to, :] = mixed_ref[source, :]
            back_ref[to, :] = norm_ref[source, :]
        both = back_ref[0:lines, :].T[0:2]
        if k == 0:
            out_ref[lines : lines + 2, :] = both
        else:
            pad = jnp.zeros((2, dim), bf16)
            below = [*pieces3(both[0:1]), *pieces3(both[1:2]), pad]
            out_ref[0:lines, :] = sent_ref[...].astype(bf16)
            out_ref[lines : lines + 8, :] = jnp.concatenate(below, axis=0)
    copies[6].wait()
    own = own_len_ref.shape[0]
    for i in range(own):
        own_q_ref[i] = q_ref[page_pos * own + i]
        own_len_ref[i] = jnp.full(own_len_ref.shape[1:], tail_len_ref[page_pos * own + i])
    copies[5].wait()


def prompt_partial(queries, prompt_kv, tail_kv, page_table, prompt_len, sample_prompt, tail_len):
    samples, new, heads, dim = queries.shape
    slots, page_len = prompt_kv.shape[:2]
    total = samples * new * heads
    block = total // page_table.shape[0]
    lines = total // 4
    own = tail_kv.shape[0]
    anywhere = pl.BlockSpec(memory_space=pl.ANY)
    vmem = pl.BlockSpec(memory_space=pltpu.VMEM)
    wide = pltpu.VMEM((total, dim), jnp.float32)
    return pl.pallas_call(
        functools.partial(prompt_kernel, math.log2(math.e) / math.sqrt(dim)),
        in_specs=[anywhere] * 7,
        out_specs=[vmem] * 7,
        out_shape=[pltpu.VMEM((lines + 8, dim), jnp.float32)]
        + [pltpu.VMEM((lines + 8, dim), jnp.bfloat16)] * 3
        + [
            pltpu.VMEM((own * 1 // 2, *tail_kv.shape[1:]), tail_kv.dtype),
            pltpu.VMEM((own, new, heads, dim), queries.dtype),
            pltpu.VMEM((own, new * heads, dim), jnp.int32),
        ],
        scratch_shapes=[
            pltpu.SMEM(page_table.shape, jnp.int32),
            pltpu.SMEM(prompt_len.shape, jnp.int32),
            pltpu.SMEM(sample_prompt.shape, jnp.int32),
            pltpu.VMEM(queries.shape, queries.dtype),
            pltpu.VMEM(prompt_kv.shape, prompt_kv.dtype),
            pltpu.SMEM((slots + 1,), jnp.int32),
            pltpu.SMEM(prompt_len.shape, jnp.int32),
            pltpu.SMEM(sample_prompt.shape, jnp.int32),
            wide,
            pltpu.VMEM((total, dim), jnp.bfloat16),
            pltpu.VMEM((slots, block, page_len * heads), jnp.float32),
            wide,
            wide,
            wide,
            wide,
            pltpu.VMEM((lines, dim), jnp.float32),
            pltpu.SMEM(tail_len.shape, jnp.int32),
            pltpu.SemaphoreType.DMA((7,)),
        ],
        compiler_params=pltpu.CompilerParams(vmem_limit_bytes=VMEM_LIMIT),
        name="prompt_attention",
    )(
        *map(
            in_hbm,
            (page_table, prompt_len, sample_prompt, queries, prompt_kv, tail_kv, tail_len),
        )
    )


def tail_kernel(scale, q_ref, len_ref, held_ref, kv_hbm, out_ref, kv_ref, column_ref, sem):
    held, length, heads, _ = held_ref.shape
    own, new, _, dim = q_ref.shape
    lines, half = new * heads, length * heads // 2
    bf16, f32 = jnp.bfloat16, jnp.float32
    copy = pltpu.make_async_copy(kv_hbm.at[pl.ds(held, own - held)], kv_ref, sem)
    copy.start()
    row = lax.broadcasted_iota(jnp.int32, (2 * lines, half), 0)
    col = lax.broadcasted_iota(jnp.int32, (2 * lines, half), 1) + (row // lines) * half
    line = row % lines
    same_head = line % heads == col % heads
    ahead = jnp.where(same_head, col // heads - line // heads, length + new)
    lane = lax.broadcasted_iota(jnp.int32, (lines, dim), 1)
    for part in (range(0, own // 2), range(own // 2, own)):
        if part.stop > held:
            copy.wait()
        scores, values = [], []
        for i in part:
            cache = flat_rows(held_ref[i] if i < held else kv_ref[i - held])
            keys = jnp.concatenate([cache[:half, :dim], cache[half:, :dim]], axis=1)
            values.append(jnp.concatenate([cache[:half, dim:], cache[half:, dim:]], axis=1))
            query = flat_rows(q_ref[i])
            blank = jnp.zeros_like(query)
            query = jnp.concatenate(
                [
                    jnp.concatenate([query, blank], axis=1),
                    jnp.concatenate([blank, query], axis=1),
                ],
                axis=0,
            )
            score = lax.dot_general(
                query, keys, (((1,), (1,)), ((), ())), preferred_element_type=f32
            )
            limit = jnp.concatenate([len_ref[i]] * 2, axis=0)
            limit = jnp.concatenate([limit] * (half // dim), axis=1)
            scores.append(jnp.where(ahead <= limit, score, NEGATIVE))
        bests = [jnp.max(score, axis=1, keepdims=True) for score in scores]
        bests = [jnp.maximum(best[:lines], best[lines:]) for best in bests]
        weights = [
            jnp.exp2((score - jnp.concatenate([best, best], axis=0)) * scale)
            for score, best in zip(scores, bests)
        ]
        norms = [jnp.sum(weight, axis=1, keepdims=True) for weight in weights]
        for i, weight, value, best, norm in zip(part, weights, values, bests, norms):
            mixed = jnp.dot(weight.astype(bf16), value, preferred_element_type=f32)
            at = pl.ds(i * lines, lines)
            out_ref[at, :] = mixed[:lines, :dim] + mixed[lines:, dim:]
            column_ref[at, :] = jnp.where(lane == 0, best, norm[:lines] + norm[lines:])
    total = out_ref.shape[0] - 8
    out_ref[total : total + 2, :] = column_ref[...].T[0:2]


def tail_partial(own_queries, own_lengths, held_tail, tail_kv):
    own, new, heads, dim = own_queries.shape
    lines = own * new * heads
    left = (own - held_tail.shape[0], *tail_kv.shape[1:])
    vmem = pl.BlockSpec(memory_space=pltpu.VMEM)
    return pl.pallas_call(
        functools.partial(tail_kernel, math.log2(math.e) / math.sqrt(dim)),
        in_specs=[vmem] * 3 + [pl.BlockSpec(memory_space=pl.ANY)],
        out_specs=vmem,
        out_shape=pltpu.VMEM((lines + 8, dim), jnp.float32),
        scratch_shapes=[pltpu.VMEM(left, tail_kv.dtype)]
        + [pltpu.VMEM((lines, dim), jnp.float32), pltpu.SemaphoreType.DMA],
        compiler_params=pltpu.CompilerParams(vmem_limit_bytes=VMEM_LIMIT),
        cost_estimate=FREE,
        name="tail_attention",
    )(own_queries, own_lengths, held_tail, in_hbm(tail_kv))


def merge_kernel(scale, *refs):
    parts, out_ref, held_ref = refs[:-2], refs[-2], refs[-1]
    lines, dim = held_ref.shape
    heads = out_ref.shape[1] // dim
    bests, norms = [], []
    for part in parts:
        below = part[lines : lines + 8, :].astype(jnp.float32)
        if part.dtype == jnp.float32:
            bests.append(below[0:1])
            norms.append(below[1:2])
        else:
            bests.append((below[0:1] + below[1:2]) + below[2:3])
            norms.append((below[3:4] + below[4:5]) + below[5:6])
    best = functools.reduce(jnp.maximum, bests)
    scales = [jnp.exp2((one - best) * scale) for one in bests]
    norm = sum(factor * own_norm for factor, own_norm in zip(scales, norms))
    total = jnp.zeros((lines, dim), jnp.float32)
    for factor, part in zip(scales, parts):
        share = jnp.broadcast_to(factor / norm, (lines, lines)).T
        total = total + share * part[0:lines, :].astype(jnp.float32)
    held_ref[...] = total
    for h in range(heads):
        out_ref[:, h * dim : (h + 1) * dim] = held_ref[
            pl.ds(h, lines // heads, stride=heads), :
        ].astype(out_ref.dtype)


def merge_partials(parts, heads):
    lines, dim = parts[0].shape[0] - 8, parts[0].shape[1]
    vmem = pl.BlockSpec(memory_space=pltpu.VMEM)
    return pl.pallas_call(
        functools.partial(merge_kernel, math.log2(math.e) / math.sqrt(dim)),
        in_specs=[vmem] * len(parts),
        out_specs=vmem,
        out_shape=jax.ShapeDtypeStruct((lines // heads, heads * dim), jnp.bfloat16),
        scratch_shapes=[pltpu.VMEM((lines, dim), jnp.float32)],
        compiler_params=pltpu.CompilerParams(vmem_limit_bytes=VMEM_LIMIT),
        name="merge_partials",
    )(*parts)


def shard_copies(w_hbm, w_ref, sems, shards, axis):
    page_pos = lax.axis_index("page")
    units = w_ref.shape[1 + axis]
    copies = []
    for i, k in enumerate(shards):
        at = pl.ds(pl.multiple_of((page_pos ^ k) * units, 128), units)
        source = w_hbm.at[:, at] if axis else w_hbm.at[at, :]
        copies.append(pltpu.make_async_copy(source, w_ref.at[i], sems.at[i]))
    return start_copies(copies)


def hold_kernel(plan, after_ref, *refs):
    weights, held, sems = refs[: len(plan)], refs[len(plan) : -1], refs[-1]
    copies = []
    for w_hbm, out_ref, (first, shards) in zip(weights, held, plan):
        own_sems = sems.at[pl.ds(first, len(shards))]
        copies += shard_copies(w_hbm, out_ref, own_sems, shards, 1)
    for copy in copies:
        copy.wait()


def hold_columns(after, wanted):
    plan, total = [], 0
    for _, shards, _ in wanted:
        plan.append((total, shards))
        total += len(shards)
    vmem = pl.BlockSpec(memory_space=pltpu.VMEM)
    return pl.pallas_call(
        functools.partial(hold_kernel, tuple(plan)),
        in_specs=[vmem] + [pl.BlockSpec(memory_space=pl.ANY)] * len(wanted),
        out_specs=[vmem] * len(wanted),
        out_shape=[
            pltpu.VMEM((len(shards), weight.shape[0], units), weight.dtype)
            for weight, shards, units in wanted
        ],
        scratch_shapes=[pltpu.SemaphoreType.DMA((total,))],
        compiler_params=pltpu.CompilerParams(vmem_limit_bytes=VMEM_LIMIT),
        cost_estimate=FREE,
        name="hold_columns",
    )(after, *[in_hbm(weight) for weight, _, _ in wanted])


def project_kernel(per_group, *refs):
    blocks, (w_ref, stream_ref, keep_ref, give_ref, lhs_ref, sum_ref) = refs[:4], refs[4:]
    page_pos, blk_pos = lax.axis_index("page"), lax.axis_index("blk")
    height = blocks[0].shape[0]
    group = w_ref.shape[2]
    width = stream_ref.shape[2]
    for k, block in enumerate(blocks):
        start = pl.multiple_of((page_pos ^ k) * height, height)
        lhs_ref[pl.ds(start, height), :] = block[...]
    product = jnp.dot(lhs_ref[...], w_ref[0], preferred_element_type=jnp.float32)
    sum_ref[...] = product.reshape(sum_ref.shape)
    for part in range(per_group):

        @pl.when(blk_pos == page_pos * per_group + part)
        def _(part=part):
            stream = flat_rows(stream_ref[...]).astype(jnp.float32)
            at = (slice(None), slice(None), slice(part * width, (part + 1) * width))
            sum_ref[at] = sum_ref[at] + stream.reshape(sum_ref.shape[:2] + (width,))

    core = blk_pos % 2
    for chip in range(4):
        keep_ref[chip] = sum_ref[2 * chip + core]
        give_ref[chip] = sum_ref[2 * chip + 1 - core].astype(give_ref.dtype)


def project(blocks, w_out, stream_in, group):
    height, depth = blocks[0].shape
    rows = 4 * height
    vmem = pl.BlockSpec(memory_space=pltpu.VMEM)
    part = (4, rows // 8, group)
    return pl.pallas_call(
        functools.partial(project_kernel, group // stream_in.shape[2]),
        in_specs=[vmem] * 6,
        out_specs=[vmem] * 2,
        out_shape=[
            jax.ShapeDtypeStruct(part, jnp.float32),
            jax.ShapeDtypeStruct(part, jnp.bfloat16),
        ],
        scratch_shapes=[
            pltpu.VMEM((rows, depth), jnp.bfloat16),
            pltpu.VMEM((8, rows // 8, group), jnp.float32),
        ],
        compiler_params=pltpu.CompilerParams(vmem_limit_bytes=VMEM_LIMIT),
        name="project_attention",
    )(*blocks, w_out, stream_in)


def pair_kernel(keep_ref, got_ref, own_ref, *out_refs):
    chip = lax.axis_index("blk") // 2
    own_ref[...] = keep_ref[chip] + got_ref[chip].astype(jnp.float32)
    for k, out_ref in enumerate(out_refs, 1):
        total = keep_ref[chip ^ k] + got_ref[chip ^ k].astype(jnp.float32)
        out_ref[...] = total.astype(out_ref.dtype)


def pair_pieces(keep, got):
    vmem = pl.BlockSpec(memory_space=pltpu.VMEM)
    shape = keep.shape[1:]
    return pl.pallas_call(
        pair_kernel,
        in_specs=[vmem] * 2,
        out_specs=[vmem] * 4,
        out_shape=[jax.ShapeDtypeStruct(shape, jnp.float32)]
        + [jax.ShapeDtypeStruct(shape, jnp.bfloat16)] * 3,
        compiler_params=pltpu.CompilerParams(vmem_limit_bytes=VMEM_LIMIT),
        name="pair_pieces",
    )(keep, got)


def as_row(ref):
    return ref[...].astype(jnp.float32).reshape(1, ref.shape[0])


def own_part(row, width):
    page_pos = lax.axis_index("page")
    parts = [row[:, p * width : (p + 1) * width] for p in range(row.shape[1] // width)]
    return sum(jnp.where(page_pos == p, part, 0.0) for p, part in enumerate(parts))


def residual_kernel(own_ref, c_ref, b_ref, a_ref, bias_ref, score_ref, out_ref):
    group, piece = own_ref.shape[1], score_ref.shape[0]
    bias = own_part(as_row(bias_ref), group)
    total = own_ref[...] + bias
    for ref in (a_ref, b_ref, c_ref):
        total = total + ref[...].astype(jnp.float32)
    out_ref[:, :group] = total.astype(out_ref.dtype)
    out_ref[:, group : group + piece] = jnp.broadcast_to(
        as_row(score_ref), (own_ref.shape[0], piece)
    ).astype(out_ref.dtype)


def residual_rows(own, arrived, b_out, w_score):
    vmem = pl.BlockSpec(memory_space=pltpu.VMEM)
    return pl.pallas_call(
        residual_kernel,
        in_specs=[vmem] * 6,
        out_specs=vmem,
        out_shape=pltpu.VMEM((own.shape[0], own.shape[1] + 256), jnp.bfloat16),
        compiler_params=pltpu.CompilerParams(vmem_limit_bytes=VMEM_LIMIT),
        name="residual_rows",
    )(own, *arrived, b_out, w_score)


def split2(value):
    high = value.astype(jnp.bfloat16)
    return high, (value - high.astype(jnp.float32)).astype(jnp.bfloat16)


def whole2(high, low):
    return high.astype(jnp.float32) + low.astype(jnp.float32)


def up_first_kernel(*refs):
    blocks, refs = refs[:8], refs[8:]
    gain_ref, bias_ref, down_ref, far_ref, near_ref = refs[:5]
    out_refs, weight_ref, refs = refs[5:10], refs[10], refs[11:]
    lhs_ref, residual_ref, stats_ref, column_ref, weights_ref = refs
    blk_pos = lax.axis_index("blk")
    core, chip = blk_pos % 2, blk_pos // 2
    height, group = blocks[0].shape[0], lhs_ref.shape[1]
    rows, piece = 8 * height, group // 8
    gain = as_row(gain_ref)
    places = []
    for i, block in enumerate(blocks):
        from_core = core if i < 4 else 1 - core
        owner = 2 * (chip ^ (i % 4)) + from_core
        places.append(pl.ds(pl.multiple_of(owner * height, height), height))
        weights_ref[pl.ds(owner, 1), :] = block[0:1, group:].astype(jnp.float32)
    weights = [weights_ref[b : b + 1, :piece] for b in range(8)]
    weight_ref[...] = jnp.concatenate(weights, axis=1)
    own_weights = [jnp.where(blk_pos == b, weight, 0.0) for b, weight in enumerate(weights)]
    score_row = jnp.concatenate(own_weights, axis=1)
    own_weight = sum(own_weights)
    fixed = jnp.sum(as_row(down_ref) * own_weight, axis=1, keepdims=True)
    lane = lax.broadcasted_iota(jnp.int32, (height, rows), 1)
    for block, at in zip(blocks, places):
        residual = block[:, :group].astype(jnp.float32)
        mean = jnp.sum(residual, axis=1, keepdims=True) * (1.0 / group)
        centred = residual - mean
        square = jnp.sum(centred * centred, axis=1, keepdims=True)
        base = jnp.sum(residual * score_row, axis=1, keepdims=True) + fixed
        residual_ref[at, :] = block[:, :group]
        lhs_ref[at, :] = (centred * gain).astype(lhs_ref.dtype)
        column_ref[at, :] = jnp.where(lane == 0, mean, jnp.where(lane == 1, square, base))
    row = lax.broadcasted_iota(jnp.int32, (lhs_ref.shape[0] - rows, group), 0)
    bias = as_row(bias_ref)
    lhs_ref[rows:, :] = jnp.where(
        row == 0, gain, jnp.where(row == 1, bias, 0.0)
    ).astype(lhs_ref.dtype)
    columns = column_ref[...].T
    pieces = []
    for i in range(3):
        pieces += split2(columns[i : i + 1])
    stats_ref[...] = jnp.concatenate(pieces, axis=0)
    for i, (top_ref, bottom_ref) in enumerate((out_refs[0:2], out_refs[2:4])):
        part = up_product(lhs_ref, far_ref.at[i], stats_ref, rows)
        top_ref[...] = part[:TOP]
        bottom_ref[...] = part[TOP:]
    out_refs[4][...] = up_product(lhs_ref, near_ref.at[0], stats_ref, rows)


def up_product(lhs_ref, w_ref, stats_ref, rows):
    product = jnp.dot(lhs_ref[...], w_ref[...], preferred_element_type=jnp.float32)
    below = product[rows : rows + 8]
    padded = jnp.concatenate(
        [
            jnp.zeros((2, rows), jnp.float32),
            stats_ref[...].astype(jnp.float32),
        ],
        axis=0,
    )
    row = lax.broadcasted_iota(jnp.int32, (8, rows), 0)
    first = jnp.where(row < 2, below[:, :rows], padded)
    below = jnp.concatenate([first, below[:, rows:]], axis=1)
    return jnp.concatenate([product[:rows], below], axis=0).astype(jnp.bfloat16)


def up_first(blocks, ln_gain, ln_bias, b_down, held_up, near_up):
    height = blocks[0].shape[0]
    rows = 8 * height
    _, group, units = held_up.shape
    bf16, f32 = jnp.bfloat16, jnp.float32
    vmem = pl.BlockSpec(memory_space=pltpu.VMEM)
    return pl.pallas_call(
        up_first_kernel,
        in_specs=[vmem] * 13,
        out_specs=[vmem] * 9,
        out_shape=[pltpu.VMEM((TOP, units), bf16), pltpu.VMEM((rows - TOP + 8, units), bf16)] * 2
        + [
            pltpu.VMEM((rows + 8, units), bf16),
            pltpu.VMEM((1, group), f32),
            pltpu.VMEM((rows + 16, group), bf16),
            jax.ShapeDtypeStruct((rows, group), bf16),
            pltpu.VMEM((6, rows), bf16),
        ],
        scratch_shapes=[pltpu.VMEM((rows, rows), f32)]
        + [
            pltpu.VMEM((8, blocks[0].shape[1] - group), f32),
        ],
        compiler_params=pltpu.CompilerParams(vmem_limit_bytes=VMEM_LIMIT),
        name="norm_and_up",
    )(
        *blocks,
        ln_gain,
        ln_bias,
        b_down,
        held_up,
        near_up,
    )


def up_own_kernel(lhs_ref, stats_ref, w_hbm, out_ref, w_ref, sems):
    copies = shard_copies(w_hbm, w_ref, sems, (0,), 1)
    copies[0].wait()
    out_ref[...] = up_product(lhs_ref, w_ref.at[0], stats_ref, stats_ref.shape[1])


def up_own(lhs, stats, w_up):
    group = lhs.shape[1]
    units = w_up.shape[1] // 4
    bf16 = jnp.bfloat16
    vmem = pl.BlockSpec(memory_space=pltpu.VMEM)
    return pl.pallas_call(
        up_own_kernel,
        in_specs=[vmem] * 2 + [pl.BlockSpec(memory_space=pl.ANY)],
        out_specs=vmem,
        out_shape=pltpu.VMEM((stats.shape[1] + 8, units), bf16),
        scratch_shapes=[pltpu.VMEM((1, group, units), bf16), pltpu.SemaphoreType.DMA((1,))],
        compiler_params=pltpu.CompilerParams(vmem_limit_bytes=VMEM_LIMIT),
        cost_estimate=FREE,
        name="up_own",
    )(lhs, stats, in_hbm(w_up))


def relay_kernel(a_ref, b_ref, out_ref):
    out_ref[...] = (a_ref[...].astype(jnp.float32) + b_ref[...].astype(jnp.float32)).astype(
        out_ref.dtype
    )


def relay_sum(part, got):
    vmem = pl.BlockSpec(memory_space=pltpu.VMEM)
    return pl.pallas_call(
        relay_kernel,
        in_specs=[vmem] * 2,
        out_specs=vmem,
        out_shape=pltpu.VMEM(part.shape, part.dtype),
        compiler_params=pltpu.CompilerParams(vmem_limit_bytes=VMEM_LIMIT),
        cost_estimate=FREE,
        name="relay_sum",
    )(part, got)


def image_kernel(first, score_ref, w_hbm, out_ref, w_ref, sems):
    count, units, group = w_ref.shape
    copies = start_copies(
        [
            pltpu.make_async_copy(
                w_hbm.at[pl.ds((first + i) * units, units)], w_ref.at[i], sems.at[i]
            )
            for i in range(count)
        ]
    )
    lanes = 128
    for i in range(count):
        copies[i].wait()
        for start in range(0, units, lanes):
            total = jnp.zeros((lanes, lanes), jnp.float32)
            for col in range(0, group, lanes):
                weights = w_ref[i, start : start + lanes, col : col + lanes].astype(jnp.float32)
                total = total + weights * score_ref[:, col : col + lanes]
            high, low = split2(jnp.sum(total.T, axis=0, keepdims=True))
            out_ref[i : i + 1, start : start + lanes] = high.astype(jnp.float32)
            out_ref[count + i : count + i + 1, start : start + lanes] = low.astype(jnp.float32)


def image_of(score_group, w_down, first, count):
    depth, group = w_down.shape
    tile = depth // 4
    vmem = pl.BlockSpec(memory_space=pltpu.VMEM)
    return pl.pallas_call(
        functools.partial(image_kernel, first),
        in_specs=[vmem, pl.BlockSpec(memory_space=pl.ANY)],
        out_specs=vmem,
        out_shape=pltpu.VMEM((2 * count, tile), jnp.float32),
        scratch_shapes=[
            pltpu.VMEM((count, tile, group), jnp.bfloat16),
            pltpu.SemaphoreType.DMA((count,)),
        ],
        compiler_params=pltpu.CompilerParams(vmem_limit_bytes=VMEM_LIMIT),
        cost_estimate=FREE,
        name="score_image",
    )(score_group, in_hbm(w_down))


def hidden_kernel(group, *refs):
    parts, (bias_ref, image_a_ref, image_b_ref, out_ref, base_ref) = refs[:5], refs[5:]
    rows, cut = parts[0].shape[0] - 8, parts[2].shape[0]
    f32 = jnp.float32
    tails = [part[part.shape[0] - 8 :, :].astype(f32) for part in (*parts[:2], *parts[3:])]
    stats = [
        [tail[2 + i : 3 + i, :rows] + tail[3 + i : 4 + i, :rows] for tail in tails]
        for i in (0, 2, 4)
    ]
    means, squares, bases = stats
    row_mean = pair_sum(means) * 0.25
    shifts = [mean - row_mean for mean in means]
    spread = sum(square + group * shift * shift for square, shift in zip(squares, shifts))
    inverse = lax.rsqrt(spread * (0.25 / group) + EPS)
    pad = jnp.zeros((rows - 6, rows), f32)
    columns = jnp.concatenate([inverse, *shifts, pair_sum(bases), pad], axis=0).T
    offset = sum(tail[1:2] for tail in tails) + own_part(as_row(bias_ref), bias_ref.shape[0] // 4)
    upper = parts[2][...].astype(f32)
    lower = parts[3][0 : rows - cut, :].astype(f32) + parts[4][0 : rows - cut, :].astype(f32)
    total = jnp.concatenate([upper, lower], axis=0)
    for part in parts[:2]:
        total = total + part[0:rows, :].astype(f32)
    for k, tail in enumerate(tails):
        total = total + columns[:, 1 + k : 2 + k] * tail[0:1]
    hidden = jnp.maximum(total * columns[:, 0:1] + offset, 0.0)
    image = [ref[at, :] for at in (slice(0, 2), slice(2, 4)) for ref in (image_a_ref, image_b_ref)]
    out_ref[...] = jnp.concatenate([hidden, *image], axis=0).astype(out_ref.dtype)
    base_ref[...] = columns[:, 5:6]


def own_hidden_units(parts, b_up, images, group):
    vmem = pl.BlockSpec(memory_space=pltpu.VMEM)
    height, units = parts[0].shape
    return pl.pallas_call(
        functools.partial(hidden_kernel, group),
        in_specs=[vmem] * 8,
        out_specs=[vmem] * 2,
        out_shape=[
            pltpu.VMEM((height, units), jnp.bfloat16),
            pltpu.VMEM((height - 8, 1), jnp.float32),
        ],
        compiler_params=pltpu.CompilerParams(vmem_limit_bytes=VMEM_LIMIT),
        name="hidden_units",
    )(*parts, b_up, *images)


def down_first_kernel(hidden_ref, w_hbm, sum_ref, held_ref, w_ref, sems, held_sems):
    rows = sum_ref.shape[0]
    copies = shard_copies(w_hbm, w_ref, sems, (0,), 0)
    held = shard_copies(w_hbm, held_ref, held_sems, (1, 2, 3), 0)
    copies[0].wait()
    sum_ref[...] = jnp.dot(
        hidden_ref[0:rows, :], w_ref[0], preferred_element_type=jnp.float32
    )
    for copy in held:
        copy.wait()


def down_first(hidden, w_down):
    rows, units = hidden.shape[0] - 8, hidden.shape[1]
    group = w_down.shape[1]
    vmem = pl.BlockSpec(memory_space=pltpu.VMEM)
    return pl.pallas_call(
        down_first_kernel,
        in_specs=[vmem, pl.BlockSpec(memory_space=pl.ANY)],
        out_specs=[vmem] * 2,
        out_shape=[
            pltpu.VMEM((rows, group), jnp.float32),
            pltpu.VMEM((3, units, group), jnp.bfloat16),
        ],
        scratch_shapes=[
            pltpu.VMEM((1, units, group), jnp.bfloat16),
            pltpu.SemaphoreType.DMA((1,)),
            pltpu.SemaphoreType.DMA((3,)),
        ],
        compiler_params=pltpu.CompilerParams(vmem_limit_bytes=VMEM_LIMIT),
        cost_estimate=FREE,
        name="down_own",
    )(hidden, in_hbm(w_down))


def down_middle_kernel(sum_ref, held_ref, near_ref, far_ref, out_ref):
    rows = sum_ref.shape[0]
    out_ref[...] = (
        sum_ref[...]
        + jnp.dot(near_ref[0:rows, :], held_ref[0], preferred_element_type=jnp.float32)
        + jnp.dot(far_ref[0:rows, :], held_ref[1], preferred_element_type=jnp.float32)
    )


def down_middle(summed, held, near, far):
    vmem = pl.BlockSpec(memory_space=pltpu.VMEM)
    return pl.pallas_call(
        down_middle_kernel,
        in_specs=[vmem] * 4,
        out_specs=vmem,
        out_shape=pltpu.VMEM(summed.shape, summed.dtype),
        compiler_params=pltpu.CompilerParams(vmem_limit_bytes=VMEM_LIMIT),
        cost_estimate=FREE,
        name="down_middle",
    )(summed, held, near, far)


def down_last_kernel(base_ref, sum_ref, held_ref, *refs):
    parts, (keep_ref, give_ref, score_ref, image_ref) = refs[:4], refs[4:]
    rows = sum_ref.shape[0]
    f32 = jnp.float32
    page_pos = lax.axis_index("page")
    core = lax.axis_index("blk") % 2
    piece = keep_ref.shape[2]
    product = sum_ref[...] + jnp.dot(
        parts[3][0:rows, :], held_ref[2], preferred_element_type=f32
    )
    tails = [part[rows:, :].astype(f32) for part in parts]
    image_ref[...] = pair_sum([tail[0:4] + tail[4:8] for tail in tails])
    by_owner = []
    for k, part in enumerate(parts):
        image = image_ref[pl.ds(page_pos ^ k, 1), :]
        by_owner.append(jnp.sum(part[0:rows, :].astype(f32) * image, axis=1, keepdims=True))
    score = base_ref[...] + pair_sum(by_owner)
    score_ref[...] = score
    pieces = split3(score)
    for chip in range(4):
        pair = [product[:, (2 * chip + c) * piece : (2 * chip + c + 1) * piece] for c in range(2)]
        keep_ref[chip] = jnp.where(core == 0, pair[0], pair[1])
        give_ref[chip, :, :piece] = jnp.where(core == 0, pair[1], pair[0]).astype(give_ref.dtype)
        give_ref[chip, :, piece:] = pieces


def down_last(base, summed, held, parts):
    rows, group = summed.shape
    units = parts[0].shape[1]
    vmem = pl.BlockSpec(memory_space=pltpu.VMEM)
    return pl.pallas_call(
        down_last_kernel,
        in_specs=[vmem] * 7,
        out_specs=[vmem] * 3,
        out_shape=[
            pltpu.VMEM((4, rows, group // 8), jnp.float32),
            pltpu.VMEM((4, rows, group // 8 + 3), jnp.bfloat16),
            pltpu.VMEM((rows, 1), jnp.float32),
        ],
        scratch_shapes=[pltpu.VMEM((4, units), jnp.float32)],
        compiler_params=pltpu.CompilerParams(vmem_limit_bytes=VMEM_LIMIT),
        name="down_last",
    )(base, summed, held, *parts)


def split3(value):
    return jnp.concatenate(pieces3(value), axis=1)


def whole3(pieces):
    return jnp.sum(pieces.astype(jnp.float32), axis=1, keepdims=True)


def pair_score_kernel(keep_ref, score_ref, got_ref, own_ref, both_ref, *out_refs):
    chip = lax.axis_index("blk") // 2
    piece = keep_ref.shape[2]
    score = whole3(split3(score_ref[...])) + whole3(got_ref[0, :, piece:])
    both_ref[...] = score
    pieces = split3(score)
    own_ref[...] = keep_ref[chip] + got_ref[chip, :, :piece].astype(jnp.float32)
    for k, out_ref in enumerate(out_refs, 1):
        total = keep_ref[chip ^ k] + got_ref[chip ^ k, :, :piece].astype(jnp.float32)
        out_ref[:, :piece] = total.astype(out_ref.dtype)
        out_ref[:, piece:] = pieces


def pair_scores(keep, score, got):
    vmem = pl.BlockSpec(memory_space=pltpu.VMEM)
    _, rows, piece = keep.shape
    return pl.pallas_call(
        pair_score_kernel,
        in_specs=[vmem] * 3,
        out_specs=[vmem] * 5,
        out_shape=[
            jax.ShapeDtypeStruct((rows, piece), jnp.float32),
            jax.ShapeDtypeStruct((rows, 1), jnp.float32),
        ]
        + [jax.ShapeDtypeStruct((rows, piece + 3), jnp.bfloat16)] * 3,
        compiler_params=pltpu.CompilerParams(vmem_limit_bytes=VMEM_LIMIT),
        name="pair_scores",
    )(keep, score, got)


def finish_kernel(own_ref, base_ref, score_ref, c_ref, b_ref, a_ref, out_ref, total_ref, held_ref):
    piece = own_ref.shape[1]
    total = own_ref[...] + base_ref[...]
    for ref in (a_ref, b_ref, c_ref):
        total = total + ref[:, :piece].astype(jnp.float32)
    out_ref[...] = total.astype(out_ref.dtype).reshape(out_ref.shape)
    scores = [whole3(ref[:, piece:]) for ref in (a_ref, b_ref, c_ref)]
    own_score = whole3(split3(score_ref[...]))
    score = (own_score + scores[0]) + (scores[1] + scores[2])
    new, samples = total_ref.shape
    held_ref[...] = jnp.broadcast_to(score, held_ref.shape)
    for n in range(new):
        total_ref[n : n + 1, :] = held_ref[pl.ds(n, samples, stride=new), :].T[0:1]


def finish(own, base, score, arrived, samples):
    vmem = pl.BlockSpec(memory_space=pltpu.VMEM)
    rows, piece = own.shape
    return pl.pallas_call(
        finish_kernel,
        in_specs=[vmem] * 6,
        out_specs=[vmem] * 2,
        out_shape=[
            jax.ShapeDtypeStruct((samples, rows // samples, piece), jnp.bfloat16),
            jax.ShapeDtypeStruct((rows // samples, samples), jnp.float32),
        ],
        scratch_shapes=[pltpu.VMEM((rows, 128), jnp.float32)],
        compiler_params=pltpu.CompilerParams(vmem_limit_bytes=VMEM_LIMIT),
        name="finish",
    )(own, base, score, *arrived)


def body(
    queries,
    prompt_kv,
    tail_kv,
    page_table,
    prompt_len,
    tail_len,
    sample_prompt,
    stream_in,
    w_out,
    b_out,
    ln_gain,
    ln_bias,
    w_up,
    b_up,
    w_down,
    b_down,
    w_score,
):
    bf16, f32 = jnp.bfloat16, jnp.float32
    samples, new_count, heads_dev, head_dim = queries.shape
    group = ln_gain.shape[0]
    blk_pos = lax.axis_index("blk")
    piece = b_down.shape[0]
    *packed, held_tail, own_queries, own_lengths = prompt_partial(
        queries, prompt_kv, tail_kv, page_table, prompt_len, sample_prompt, tail_len
    )
    sent = {k: send_xor(packed[k], "page", k) for k in (2, 3, 1)}
    shares = [packed[0], sent[1], sent[2], sent[3]]
    tail = tail_partial(own_queries, own_lengths, held_tail, tail_kv)
    own_attention = merge_partials(shares + [tail], heads_dev)
    sent = {k: send_xor(own_attention, "page", k) for k in (2, 1, 3)}
    attention = [own_attention, sent[1], sent[2], sent[3]]
    units = w_up.shape[1] // 4
    held_out, near_up = hold_columns(
        own_attention, ((w_out, (0,), group), (w_up, (1,), units))
    )
    keep, give = project(attention, held_out, stream_in, group)
    own, *pieces = pair_pieces(keep, send_xor(give, "blk", 1))
    arrived = [send_xor(pieces[k - 1], "blk", 2 * k) for k in (3, 2, 1)]
    (held_up,) = hold_columns(own, ((w_up, (3, 2), units),))
    own, held_up = lax.optimization_barrier((own, held_up))
    own_rows = residual_rows(own, arrived, b_out, w_score)
    same_core = gather_xor(own_rows, "blk", (2, 4, 6))
    blocks = same_core + [send_xor(block, "blk", 1) for block in same_core]
    top3, bottom3, top2, bottom2, part1, score_group, lhs, residual, stats = up_first(
        blocks, ln_gain, ln_bias, b_down, held_up, near_up
    )
    passing = send_xor(top3, "page", 1)
    far = send_xor(bottom3, "page", 3)
    middle = send_xor(bottom2, "page", 2)
    near = send_xor(part1, "page", 1)
    image_a = image_of(score_group, w_down, 0, 2)
    passing, image_a = lax.optimization_barrier((passing, image_a))
    both, score_group, lhs = lax.optimization_barrier((relay_sum(top2, passing), score_group, lhs))
    part0 = up_own(lhs, stats, w_up)
    images = image_a, image_of(score_group, w_down, 2, 2)
    parts = [part0, near, send_xor(both, "page", 2), middle, far]
    hidden, base_score = own_hidden_units(parts, b_up, images, group)
    summed, held = down_first(hidden, w_down)
    far, near, summed = lax.optimization_barrier(
        (send_xor(hidden, "page", 2), send_xor(hidden, "page", 1), summed)
    )
    summed = down_middle(summed, held, near, far)
    relayed = send_xor(far, "page", 1)
    keep, give, score = down_last(base_score, summed, held, [hidden, near, far, relayed])
    own_base = lax.dynamic_slice_in_dim(residual, blk_pos * piece, piece, 1).astype(
        f32
    ) + b_down.astype(f32)
    own, score, *pieces = pair_scores(keep, score, send_xor(give, "blk", 1))
    arrived = [send_xor(pieces[k - 1], "blk", 2 * k) for k in (3, 2, 1)]
    output, score = finish(own, own_base, score, arrived, samples)
    return (output, score.T)


def general_body(
    queries,
    prompt_kv,
    tail_kv,
    page_table,
    prompt_len,
    tail_len,
    sample_prompt,
    stream_in,
    w_out,
    b_out,
    ln_gain,
    ln_bias,
    w_up,
    b_up,
    w_down,
    b_down,
    w_score,
):
    samples, new_count, heads_dev, head_dim = queries.shape
    slots_dev, page_len = (prompt_kv.shape[0], prompt_kv.shape[1])
    own_count, tail_max = (tail_kv.shape[0], tail_kv.shape[1])
    prompts, pages_max = page_table.shape
    page_pos = lax.axis_index("page")
    blk_pos = lax.axis_index("blk")
    inv_sqrt = 1.0 / math.sqrt(head_dim)
    entries = page_table.reshape(-1)
    slot_ids = page_pos * slots_dev + jnp.arange(slots_dev, dtype=jnp.int32)
    matched = (entries[:, None] == slot_ids[None, :]).astype(jnp.int32)
    owner_index = jnp.sum(matched * jnp.arange(entries.shape[0], dtype=jnp.int32)[:, None], axis=0)
    slot_prompt = owner_index // pages_max
    slot_page = owner_index % pages_max
    prompt_pick = (slot_prompt[:, None] == jnp.arange(prompts, dtype=jnp.int32)[None, :]).astype(
        jnp.int32
    )
    slot_limit = jnp.sum(prompt_pick * prompt_len[None, :], axis=1)
    key_pos = slot_page[:, None] * page_len + jnp.arange(page_len, dtype=jnp.int32)[None, :]
    key_live = (key_pos < slot_limit[:, None]).reshape(-1)
    key_prompt = jnp.repeat(slot_prompt, page_len)
    prompt_visible = ((sample_prompt[:, None] == key_prompt[None, :]) & key_live[None, :])[
        :, None, None, :
    ]
    cache_rows = prompt_kv.reshape(slots_dev * page_len, heads_dev, 2 * head_dim)
    prompt_scores = (
        jnp.einsum(
            "snhd,khd->snhk",
            queries,
            cache_rows[:, :, :head_dim],
            preferred_element_type=jnp.float32,
        )
        * inv_sqrt
    )
    high_p, sum_p, weights_p = softmax_part(prompt_scores, prompt_visible)
    mixed_p = jnp.einsum(
        "snhk,khd->snhd", weights_p, cache_rows[:, :, head_dim:], preferred_element_type=jnp.float32
    )
    first_row = page_pos * own_count
    own_queries = lax.dynamic_slice_in_dim(queries, first_row, own_count, 0)
    own_lengths = lax.dynamic_slice_in_dim(tail_len, first_row, own_count, 0)
    tail_scores = (
        jnp.einsum(
            "snhd,sthd->snht",
            own_queries,
            tail_kv[..., :head_dim],
            preferred_element_type=jnp.float32,
        )
        * inv_sqrt
    )
    reach_pos = own_lengths[:, None] + jnp.arange(new_count, dtype=jnp.int32)[None, :]
    tail_visible = (
        jnp.arange(tail_max, dtype=jnp.int32)[None, None, None, :] <= reach_pos[:, :, None, None]
    )
    high_t, sum_t, weights_t = softmax_part(tail_scores, tail_visible)
    mixed_t = jnp.einsum(
        "snht,sthd->snhd", weights_t, tail_kv[..., head_dim:], preferred_element_type=jnp.float32
    )
    high_t = lax.dynamic_update_slice_in_dim(
        jnp.full(high_p.shape, NEGATIVE, jnp.float32), high_t, first_row, 0
    )
    sum_t = lax.dynamic_update_slice_in_dim(
        jnp.zeros(sum_p.shape, jnp.float32), sum_t, first_row, 0
    )
    mixed_t = lax.dynamic_update_slice_in_dim(
        jnp.zeros(mixed_p.shape, jnp.float32), mixed_t, first_row, 0
    )
    partial_value = join_partials((high_p, sum_p, mixed_p), (high_t, sum_t, mixed_t))
    merged = combined_all(partial_value, "page", join_partials)
    weight_sum, weighted = (merged[1], merged[2])
    attention = (
        (weighted / weight_sum[..., None])
        .astype(jnp.bfloat16)
        .reshape(samples * new_count, heads_dev * head_dim)
    )
    contrib = jnp.dot(attention, w_out, preferred_element_type=jnp.float32)
    slice_width = stream_in.shape[2]
    column = blk_pos * slice_width
    own_stream = stream_in.reshape(samples * new_count, slice_width).astype(jnp.float32)
    contrib = lax.dynamic_update_slice_in_dim(
        contrib, lax.dynamic_slice_in_dim(contrib, column, slice_width, 1) + own_stream, column, 1
    )
    summed = lax.psum(contrib, "blk")
    residual = (summed + b_out.astype(jnp.float32)).astype(jnp.bfloat16)
    residual_f = residual.astype(jnp.float32)
    row_mean = jnp.mean(residual_f, axis=-1, keepdims=True)
    centred = residual_f - row_mean
    inverse_std = lax.rsqrt(jnp.mean(centred * centred, axis=-1, keepdims=True) + 1e-05)
    feature_count = ln_gain.shape[0]
    first_col = page_pos * feature_count
    normed = (
        lax.dynamic_slice_in_dim(centred, first_col, feature_count, 1)
        * inverse_std
        * ln_gain.astype(jnp.float32)
        + ln_bias.astype(jnp.float32)
    ).astype(jnp.bfloat16)
    up_part = jnp.dot(normed, w_up, preferred_element_type=jnp.float32).astype(jnp.bfloat16)
    hidden_sum = lax.psum(up_part, "page").astype(jnp.float32)
    hidden = jnp.maximum(hidden_sum + b_up.astype(jnp.float32), 0.0).astype(jnp.bfloat16)
    projected = jnp.dot(hidden, w_down, preferred_element_type=jnp.float32)
    out_share = lax.psum_scatter(projected, "blk", scatter_dimension=1, tiled=True)
    piece_width = b_down.shape[0]
    out_column = first_col + blk_pos * piece_width
    output = (
        out_share
        + lax.dynamic_slice_in_dim(residual_f, out_column, piece_width, 1)
        + b_down.astype(jnp.float32)
    ).astype(jnp.bfloat16)
    score_part = jnp.sum(output.astype(jnp.float32) * w_score.astype(jnp.float32), axis=-1)
    row_score = lax.psum(score_part, ("page", "blk"))
    return (output.reshape(samples, new_count, piece_width), row_score.reshape(samples, new_count))


def solution(mesh):
    compute = body if (mesh.shape["page"], mesh.shape["blk"]) == (4, 8) else general_body

    placed = (
        P(None, None, "blk", None),
        P("page", None, "blk", None),
        P("page", None, "blk", None),
        P(),
        P(),
        P(),
        P(),
        P(None, None, "blk"),
        P("blk", None),
        P(),
        P("page"),
        P("page"),
        P("page", "blk"),
        P("blk"),
        P("blk", "page"),
        P(("page", "blk")),
        P(("page", "blk")),
    )
    return jax.shard_map(
        compute,
        mesh=mesh,
        in_specs=placed,
        out_specs=(P(None, None, ("page", "blk")), P()),
        check_vma=False,
    )
```
